128 devices in a mesh: clip: 8 (over y, z_lo), seq: 16 (over z_hi, x, core).
Axes of the slice: x: 4, y: 4, z: 4 (z_hi: 2, z_lo: 2; z = z_hi * 2 + z_lo), core: 2. Of those that a mesh axis runs over, the one named last changes fastest.
Arguments:
- features: bfloat16 [8, 16, 32, 32, 256], P('clip', None, 'seq'), may hold values from -53 to 53
- first_conv: bfloat16 [3, 3, 3, 256, 256], replicated, may hold values from -0.078125 to 0.078125
- second_conv: bfloat16 [3, 3, 3, 256, 256], replicated, may hold values from -0.078125 to 0.078125
- out_conv: bfloat16 [3, 3, 3, 256, 16], replicated, may hold values from -0.078125 to 0.078125
- norm_gains: float32 [3, 256], replicated, may hold values from 0.25 to 1.75
- norm_shifts: float32 [3, 256], replicated, may hold values from -3 to 3
- embed_weight: bfloat16 [64, 3072], replicated, may hold values from -0.75 to 0.75
- embed_bias: float32 [3072], replicated, may hold values from -5 to 5
- mod_shift: float32 [8, 3072], P('clip'), may hold values from -3 to 3
- mod_scale: float32 [8, 3072], P('clip'), may hold values from -3 to 3
- qkv_weight: bfloat16 [4608, 3072], P(('clip', 'seq')), may hold values from -0.8 to 0.8
Outputs:
- latent: float32 [8, 16, 32, 32, 16], P('clip', None, 'seq')
- frame_heads: bfloat16 [8, 16, 256, 1536], P('clip', 'seq')
The draws below stay inside these ranges and needn't reach their ends.
All inputs are finite; a program needn't handle non-finite values.
Results may differ from the reference program's by a relative error of at most 0.012.
Values may be sent and summed in bfloat16 or wider, within the bound.
No kernel may reach another device: no remote copies, remote signals or barrier semaphores. Data moves between devices by JAX's collectives and lax.ppermute only.
A program may use at most 192 MiB of HBM per device.

```python
import math
import jax
import jax.numpy as jnp
from jax import lax

C = 256
GROUPS = 32
LAT = 16
D = 3072
HEADS = 12
HDIM = 128
WIDTH = 32
CLIPS = 8
FRAMES = 16
HEIGHT = 32


def draw_features(key, part):
    key = jax.random.fold_in(key, 11)
    key_base, key_cell, key_chan = jax.random.split(key, 3)
    normal_part = jax.random.truncated_normal(key_base, -4.0, 4.0, (CLIPS, FRAMES, HEIGHT, WIDTH, C), jnp.float32)
    cell_scale = jax.random.uniform(key_cell, (CLIPS, FRAMES, HEIGHT, WIDTH, 1), jnp.float32, 0.5, 1.5)
    chan_scale = jnp.exp(jax.random.uniform(key_chan, (C,), jnp.float32, math.log(0.32), math.log(3.2)))
    row_pos = jnp.arange(HEIGHT, dtype=jnp.float32) / max(HEIGHT - 1, 1)
    row_scale = 0.5 * jnp.exp(row_pos * math.log(3.0))
    return (normal_part * cell_scale * chan_scale * row_scale[:, None, None]).astype(jnp.bfloat16)


def draw_qkv_weight(key, part):
    key = jax.random.fold_in(key, 23)
    key_base = jax.random.fold_in(key, 0)
    spread = 1.0 / math.sqrt(3072.0)
    normal_part = jax.random.truncated_normal(key_base, -4.0, 4.0, (3, HEADS, HDIM, D), jnp.float32) * spread
    return normal_part.reshape(3 * HEADS * HDIM, D).astype(jnp.bfloat16)


def block_levels(own_key, dims, cuts, smallest, largest):
    gain, own = 1.0, jax.random.fold_in(own_key, 6)
    for axis_at, shards_of in cuts:
        draws = jnp.exp(jax.random.uniform(jax.random.fold_in(own, axis_at), (shards_of,), jnp.float32, smallest / len(cuts), largest / len(cuts)))
        gain = gain * jnp.repeat(draws, dims[axis_at] // shards_of).reshape([-1 if axis == axis_at else 1 for axis in range(len(dims))])
    return gain


def bell_draw(key, extent, scale, limit, pieces=(), kind=jnp.bfloat16):
    gain = block_levels(key, extent, pieces, -0.22, 0.18) if pieces else 1.0
    drawn = jax.random.normal(key, extent, jnp.float32) * scale * gain
    return jnp.minimum(jnp.maximum(drawn, -limit), limit).astype(kind)


def setup_inputs(seed: int = 0) -> dict:
    key_of = jax.random.split(jax.random.key(seed), 12)
    return {
        "features": draw_features(jax.random.fold_in(key_of[11], 71), 0),
        "first_conv": bell_draw(key_of[1], (3, 3, 3, C, C), (27 * C) ** -0.5, 0.078125),
        "second_conv": bell_draw(key_of[2], (3, 3, 3, C, C), (27 * C) ** -0.5, 0.078125),
        "out_conv": bell_draw(key_of[3], (3, 3, 3, C, LAT), (27 * C) ** -0.5, 0.078125),
        "norm_gains": jnp.clip(1.0 + 0.15 * jax.random.normal(key_of[4], (3, C), jnp.float32), 0.25, 1.75),
        "norm_shifts": bell_draw(key_of[5], (3, C), 0.5, 3.0, (), jnp.float32),
        "embed_weight": bell_draw(key_of[6], (4 * LAT, D), (4 * LAT) ** -0.5, 0.75),
        "embed_bias": bell_draw(key_of[7], (D,), 1.0, 5.0, (), jnp.float32),
        "mod_shift": bell_draw(key_of[8], (CLIPS, D), 0.5, 3.0, ((0, 8),), jnp.float32),
        "mod_scale": bell_draw(key_of[9], (CLIPS, D), 0.5, 3.0, ((0, 8),), jnp.float32),
        "qkv_weight": draw_qkv_weight(jax.random.fold_in(key_of[11], 71), 0),
    }


epsilon = 1e-06

def norm_silu(values, norm_gain, norm_shift):
    n_chans = values.shape[-1]
    grouped = values.reshape(values.shape[:-1] + (GROUPS, n_chans // GROUPS))
    center = lax.optimization_barrier(jnp.mean(grouped, axis=(0, 1, 2, 4), keepdims=True))
    offset = grouped - center
    spread = lax.optimization_barrier(jnp.mean(offset * offset, axis=(0, 1, 2, 4), keepdims=True))
    normed = (offset * lax.rsqrt(spread + epsilon)).reshape(values.shape) * norm_gain + norm_shift
    return jax.nn.silu(normed).astype(jnp.bfloat16)

def convolve(active, kernel):
    result = lax.conv_general_dilated(active.astype(jnp.float32)[None], kernel.astype(jnp.float32), (1, 1, 1), ((2, 0), (1, 1), (1, 1)), dimension_numbers=('NDHWC', 'DHWIO', 'NDHWC'), precision=lax.Precision.HIGHEST)
    return result[0]

def attend(queries, keys_all, values_all):
    scale = 1.0 / math.sqrt(HDIM)
    scores = jnp.einsum('fphd,gphd->phfg', queries.astype(jnp.float32), keys_all.astype(jnp.float32)) * scale
    row_peak = lax.optimization_barrier(jnp.max(scores, axis=-1, keepdims=True))
    raised = jnp.exp(scores - row_peak)
    weights = (raised / lax.optimization_barrier(jnp.sum(raised, axis=-1, keepdims=True))).astype(jnp.bfloat16)
    return jnp.einsum('phfg,gphd->fphd', weights.astype(jnp.float32), values_all.astype(jnp.float32)).astype(jnp.bfloat16)

def one_clip(features, mod_shift, mod_scale, params):
    first_conv, second_conv, out_conv, norm_gains, norm_shifts, embed_weight, embed_bias, qkv_weight = params
    source = features.astype(jnp.float32)
    first_act = norm_silu(source, norm_gains[0], norm_shifts[0])
    second_act = norm_silu(convolve(first_act, first_conv), norm_gains[1], norm_shifts[1])
    block_out = (source + convolve(second_act, second_conv)).astype(jnp.bfloat16)
    third_act = norm_silu(block_out.astype(jnp.float32), norm_gains[2], norm_shifts[2])
    latent = convolve(third_act, out_conv)
    frames, height, n_width, n_lat = latent.shape
    places = height // 2 * (n_width // 2)
    patches = latent.reshape(frames, height // 2, 2, n_width // 2, 2, n_lat).transpose(0, 1, 3, 2, 4, 5)
    patches = patches.reshape(frames * places, 4 * n_lat).astype(jnp.bfloat16)
    embedded = jnp.dot(patches, embed_weight, preferred_element_type=jnp.float32) + embed_bias
    center = lax.optimization_barrier(jnp.mean(embedded, axis=-1, keepdims=True))
    offset = embedded - center
    spread = lax.optimization_barrier(jnp.mean(offset * offset, axis=-1, keepdims=True))
    modulated = (offset * lax.rsqrt(spread + epsilon) * (1.0 + mod_scale) + mod_shift).astype(jnp.bfloat16)
    projected = jnp.dot(modulated, qkv_weight.T, preferred_element_type=jnp.float32).astype(jnp.bfloat16)
    projected = projected.reshape(frames, places, 3, HEADS, HDIM)
    attended = attend(projected[:, :, 0], projected[:, :, 1], projected[:, :, 2])
    return (latent, attended.reshape(frames, places, HEADS * HDIM))

def reference(features, first_conv, second_conv, out_conv, norm_gains, norm_shifts, embed_weight, embed_bias, mod_shift, mod_scale, qkv_weight):
    params = (first_conv, second_conv, out_conv, norm_gains, norm_shifts, embed_weight, embed_bias, qkv_weight)

    def per_clip(clip_items):
        return one_clip(clip_items[0], clip_items[1], clip_items[2], params)
    latent, frame_heads = lax.map(per_clip, (features, mod_shift, mod_scale))
    return (latent, frame_heads)
```

```python
import functools
import math

import jax
import jax.numpy as jnp
from jax import lax
from jax.experimental import pallas as pl
from jax.experimental.pallas import tpu as pltpu
from jax.sharding import PartitionSpec as P

C = 256
GROUPS = 32
LAT = 16
D = 3072
HEADS = 12
HDIM = 128
FRAMES = 16
HALF = 16
ROW = FRAMES * 2 * HALF
CELLS = 2 * ROW
SEQ = 16
CLIPS = 8
QROWS = 36
QPAD = 48
EPS = 1e-06
F32 = jnp.float32
BF16 = jnp.bfloat16
VMEM = pl.BlockSpec(memory_space=pltpu.VMEM)
SMEM = pl.BlockSpec(memory_space=pltpu.SMEM)
ANY = pl.BlockSpec(memory_space=pl.ANY)


def nt_dot(a, b):
    return lax.dot_general(a, b, (((1,), (1,)), ((), ())), preferred_element_type=F32)


def dot(a, b):
    return jnp.dot(a, b, preferred_element_type=F32)


def exact_dot(rows, zero_one):
    high = rows.astype(BF16).astype(F32)
    rest = rows - high
    mid = rest.astype(BF16).astype(F32)
    low = rest - mid
    parts = jnp.concatenate([high, mid, low, jnp.zeros_like(low)], axis=0).astype(BF16)
    out = dot(parts, zero_one)
    return out[0:8] + out[8:16] + out[16:24]


def iota(shape, dim):
    return lax.broadcasted_iota(jnp.int32, shape, dim)


def one_hot(cond):
    return jnp.where(cond, 1.0, 0.0).astype(BF16)


def rows8(first, second=None):
    n = first.shape[1]
    row = iota((8, n), 0)
    out = jnp.where(row == 0, jnp.broadcast_to(first, (8, n)), 0.0)
    if second is not None:
        out = jnp.where(row == 1, jnp.broadcast_to(second, (8, n)), out)
    return out


def write_stats(cells, stats_ref):
    count = cells.shape[0]
    mean_c = jnp.sum(cells, axis=0, keepdims=True) * (1.0 / count)
    same = one_hot((iota((C, C), 0) >> 3) == (iota((C, C), 1) >> 3))
    mean_g = exact_dot(rows8(mean_c), same)[0:1] * (1.0 / 8)
    off = cells - mean_c
    square_c = jnp.sum(off * off, axis=0, keepdims=True)
    gap = mean_c - mean_g
    square_c = square_c + count * (gap * gap)
    lane = iota((C, 128), 1)
    pick = one_hot((iota((C, 128), 0) >> 3) == (lane & 31))
    both = exact_dot(rows8(mean_c * (1.0 / 8), square_c), pick)
    row = jnp.where(iota((1, 128), 1) < GROUPS, both[0:1], both[1:2])
    stats_ref[...] = jnp.broadcast_to(row[None], (SEQ, 1, 128))


def read_stats(stats_ref, count):
    each = stats_ref[...].reshape(SEQ, 128)
    lane = iota((1, 128), 1)
    mean = jnp.sum(each, axis=0, keepdims=True) * (1.0 / SEQ)
    off = each - mean
    between = jnp.sum(off * off, axis=0, keepdims=True) * (8.0 * count)
    within = mean * SEQ
    total = jnp.where(lane < GROUPS, between, jnp.where(lane < 2 * GROUPS, within, 0.0))
    mean = jnp.where(lane < GROUPS, mean, 0.0)
    spread = one_hot((iota((128, C), 0) & 31) == (iota((128, C), 1) >> 3))
    both = exact_dot(rows8(mean, total), spread)
    return both[0:1], lax.rsqrt(both[1:2] * (1.0 / (8.0 * count * SEQ)) + EPS)


def split_kernel(feat_ref, f0_ref, f1_ref, stats_ref, wide):
    cells = feat_ref[...].astype(F32).reshape(CELLS, C)
    for side in range(2):
        wide[side] = cells[:, side * 128 : (side + 1) * 128]
    for frame in range(FRAMES):
        for row, out in ((0, f0_ref), (1, f1_ref)):
            for parity in range(2):
                base = (frame * 2 + row) * 32 + parity
                at = (frame * 2 + parity) * HALF
                for side in range(2):
                    part = wide[side, pl.ds(base, HALF, stride=2)]
                    out[at : at + HALF, side * 128 : (side + 1) * 128] = part.astype(BF16)
    write_stats(cells, stats_ref)


def fill_window(place_ref, stats_ref, rows, gain, shift, window):
    mean, rstd = read_stats(stats_ref, CELLS)
    gain = rstd * gain * 0.5
    shift = shift * 0.5
    place = place_ref[0]
    top_on = jnp.where(place > 0, 1.0, 0.0).astype(F32)
    low_on = jnp.where(place < SEQ - 1, 1.0, 0.0).astype(F32)
    window[:, 0:2] = jnp.zeros((4, 2, 4, HALF, C), BF16)
    step = 4
    n = step * HALF
    pair = iota((n, C), 0) & (HALF - 1)
    for row, source in enumerate(rows):
        for frame in range(0, FRAMES, step):
            x = source[frame * 32 : (frame + step) * 32].astype(F32)
            half = (x - mean) * gain + shift
            act = half + half * jnp.tanh(half)
            if row == 0:
                act = act * top_on
            if row == 3:
                act = act * low_on
            act = act.reshape(step, 2, HALF, C)
            even = act[:, 0].reshape(n, C)
            odd = act[:, 1].reshape(n, C)
            odd_before = jnp.where(pair == 0, 0.0, pltpu.roll(odd, 1, 0))
            even_after = jnp.where(pair == HALF - 1, 0.0, pltpu.roll(even, n - 1, 0))
            for plane, part in enumerate((odd_before, even, odd, even_after)):
                window[row, 2 + frame : 2 + frame + step, plane] = part.astype(BF16).reshape(
                    step, HALF, C
                )


def convolve(window, weight):
    total = None
    for tap in range(27):
        p, q, r = tap // 9, tap // 3 % 3, tap % 3
        cells = window[q : q + 2, p : p + FRAMES, r : r + 2].reshape(CELLS, C)
        term = dot(cells, weight[tap])
        total = term if total is None else total + term
    return total


def first_kernel(
    place_ref, stats_ref, top_ref, f0_ref, f1_ref, low_ref, gain_ref, shift_ref, weight_hbm,
    hidden_ref, h0_ref, h1_ref, stats_out, window, weight, sem,
):
    copy = pltpu.make_async_copy(weight_hbm, weight, sem)
    copy.start()
    rows = (top_ref, f0_ref, f1_ref, low_ref)
    fill_window(place_ref, stats_ref, rows, gain_ref[0:1], shift_ref[0:1], window)
    copy.wait()
    hidden = convolve(window, weight)
    hidden_ref[...] = hidden
    h0_ref[...] = hidden[:ROW].astype(BF16)
    h1_ref[...] = hidden[ROW:].astype(BF16)
    write_stats(hidden, stats_out)


def second_kernel(
    place_ref, stats_ref, top_ref, hidden_ref, low_ref, f0_ref, f1_ref, gain_ref, shift_ref, weight_hbm,
    b0_ref, b1_ref, stats_out, window, weight, sem,
):
    copy = pltpu.make_async_copy(weight_hbm, weight, sem)
    copy.start()
    rows = (top_ref, hidden_ref.at[0:ROW], hidden_ref.at[ROW:CELLS], low_ref)
    fill_window(place_ref, stats_ref, rows, gain_ref[1:2], shift_ref[1:2], window)
    copy.wait()
    added = convolve(window, weight)
    b0 = (added[:ROW] + f0_ref[...].astype(F32)).astype(BF16)
    b1 = (added[ROW:] + f1_ref[...].astype(F32)).astype(BF16)
    b0_ref[...] = b0
    b1_ref[...] = b1
    write_stats(jnp.concatenate([b0, b1], axis=0).astype(F32), stats_out)


def third_kernel(
    place_ref, stats_ref, top_ref, b0_ref, b1_ref, low_ref, gain_ref, shift_ref, weight_ref, embed_ref, bias_ref,
    latent_ref, tokens_ref, window,
):
    rows = (top_ref, b0_ref, b1_ref, low_ref)
    fill_window(place_ref, stats_ref, rows, gain_ref[2:3], shift_ref[2:3], window)
    latent = convolve(window, weight_ref).reshape(2, FRAMES, 2, HALF, LAT)
    n = FRAMES * HALF
    patches = jnp.concatenate(
        [latent[dh, :, dw].reshape(n, LAT) for dh in range(2) for dw in range(2)], axis=1
    )
    latent_ref[...] = patches
    rounded = patches.astype(BF16)
    embedded = dot(jnp.concatenate([rounded, rounded], axis=1), embed_ref[...]) + bias_ref[0:1]
    spread = jnp.sum(embedded * embedded, axis=1, keepdims=True) * (1.0 / D)
    rstd = lax.rsqrt(spread + EPS)
    high = rstd.astype(BF16).astype(F32)
    lane = iota((n, 128), 1)
    wide = jnp.concatenate([rounded.astype(F32) * rstd, jnp.zeros((n, 64), F32)], axis=1)
    wide = jnp.where((lane == 64) | (lane == 65), high, wide)
    wide = jnp.where((lane == 66) | (lane == 67), 1.0, wide)
    wide = jnp.where(lane == 68, rstd - high, wide)
    tokens_ref[...] = wide.astype(BF16)


def embed_kernel(embed_ref, bias_ref, embed_out, bias_out):
    embed = embed_ref[...].astype(F32)
    embed = embed - jnp.mean(embed, axis=1, keepdims=True)
    high = embed.astype(BF16)
    embed_out[0:64] = high
    embed_out[64:128] = (embed - high.astype(F32)).astype(BF16)
    bias = bias_ref[...]
    bias_out[...] = jnp.broadcast_to(bias - jnp.mean(bias, axis=1, keepdims=True), (8, D))


def fold_kernel(near_ref, far_refs, embed_ref, bias_ref, scale_ref, shift_ref, out_ref):
    scale = 1.0 + scale_ref[...]
    embed = (embed_ref[0:64].astype(F32) + embed_ref[64:128].astype(F32)) * scale
    row = iota((16, D), 0)
    ends = jnp.where(row == 0, bias_ref[0:1] * scale, jnp.where(row == 1, shift_ref[...], 0.0))
    every = jnp.concatenate([embed, ends], axis=0)
    high = every.astype(BF16).astype(F32)
    gap = jnp.zeros((48, D), F32)
    both = jnp.concatenate([high, gap, every - high, gap], axis=0).astype(BF16)
    lane = iota((QROWS, 128), 1)
    blocks = [near_ref.at[i] for i in range(2)] + [far.at[i] for far in far_refs for i in range(2)]
    for i, block in enumerate(blocks):
        out = nt_dot(block[...], both)
        out = out[:, 0:128] + out[:, 128:256]
        bias, shift = out[:, 64:65], out[:, 65:66]
        bias_high = bias.astype(BF16).astype(F32)
        shift_high = shift.astype(BF16).astype(F32)
        out = jnp.where((lane == 64) | (lane == 68), bias_high, out)
        out = jnp.where(lane == 65, bias - bias_high, out)
        out = jnp.where(lane == 66, shift_high, out)
        out = jnp.where(lane == 67, shift - shift_high, out)
        out_ref[i] = jnp.concatenate([out, jnp.zeros((QPAD - QROWS, 128), F32)], axis=0).astype(BF16)


def sort_kernel(place_ref, near_ref, far_ref, out_ref, wide):
    seq, clip = place_ref[0], place_ref[1]
    for j in range(SEQ):
        source = (near_ref, far_ref)[j & 1]
        for k in range(CLIPS):
            block = source[j >> 1, k].astype(F32)
            at = ((clip ^ k) * SEQ + (seq ^ j)) * QROWS
            wide[pl.ds(at, QROWS)] = block[:QROWS]
    out_ref[...] = wide[...].astype(BF16)


def attend_kernel(place_ref, near_ref, far_ref, fold_ref, out_ref, queries, mixed):
    seq = place_ref[0]
    blocks = [(near_ref, far_ref)[j & 1].at[j >> 1] for j in range(SEQ)]
    mine = pl.ds(pl.multiple_of(seq * HALF, HALF), HALF)
    tokens = jnp.concatenate([block[mine] for block in blocks], axis=0)
    wide = HEADS * HDIM
    scaled = (nt_dot(tokens, fold_ref[0:wide]) * (1.0 / math.sqrt(HDIM))).astype(BF16)
    for head in range(HEADS):
        cols = slice(head * HDIM, (head + 1) * HDIM)
        keyed = dot(scaled[:, cols], fold_ref[wide + head * HDIM : wide + (head + 1) * HDIM])
        queries[:, head] = keyed.astype(BF16).reshape(SEQ, HALF, 128)
    n = HEADS * HALF
    keys = FRAMES * HALF
    off = (iota((n, keys), 0) & (HALF - 1)) != (iota((n, keys), 1) & (HALF - 1))
    bar = jnp.where(off, -jnp.inf, 0.0)
    for j, block in enumerate(blocks):
        scores = nt_dot(queries[j].reshape(n, 128), block[...]) + bar
        raised = jnp.exp(scores - jnp.max(scores, axis=1, keepdims=True))
        mix = dot(raised.astype(BF16), block[...])
        mix = mix * (1.0 / mix[:, 66:67])
        mixed[:, j * HALF : (j + 1) * HALF] = mix.astype(BF16).reshape(HEADS, HALF, 128)
    for head in range(HEADS):
        cols = slice(head * HDIM, (head + 1) * HDIM)
        at = 2 * wide + head * HDIM
        out = nt_dot(mixed[head], fold_ref[at : at + HDIM]).astype(BF16)
        for j in range(SEQ):
            rows = pl.ds(pl.multiple_of((seq ^ j) * HALF, HALF), HALF)
            out_ref[rows, cols] = out[j * HALF : (j + 1) * HALF]


def shape(*dims, dtype=BF16):
    return jax.ShapeDtypeStruct(dims, dtype)


def call(body, outs, ins, scratch=(), flops=0, moved=0, limit=32):
    return pl.pallas_call(
        body,
        out_shape=outs,
        in_specs=ins,
        out_specs=jax.tree.map(lambda _: VMEM, outs),
        scratch_shapes=list(scratch),
        compiler_params=pltpu.CompilerParams(vmem_limit_bytes=limit << 20),
        cost_estimate=pl.CostEstimate(flops=flops, bytes_accessed=moved, transcendentals=0),
        name=body.__name__ if hasattr(body, "__name__") else None,
    )


def swap(values, axis, bits, count):
    return lax.ppermute(values, axis, [(i, i ^ bits) for i in range(count)])


def neighbours(low_row, high_row):
    top = lax.ppermute(high_row, "seq", [(i, i + 1) for i in range(SEQ - 1)])
    low = lax.ppermute(low_row, "seq", [(i + 1, i) for i in range(SEQ - 1)])
    return top, low


def exchange(stats):
    return lax.all_to_all(stats, "seq", 0, 0, tiled=True)


def gather_seq(block):
    pair = jnp.stack([block, swap(block, "seq", 8, SEQ)])
    others = [swap(pair, "seq", bits, SEQ) for bits in (2, 4, 6)]
    near = jnp.stack([pair] + others, axis=1).reshape((8,) + block.shape)
    return near, swap(near, "seq", 1, SEQ)


WINDOW = pltpu.VMEM((4, FRAMES + 2, 4, HALF, C), BF16)
WEIGHT = pltpu.VMEM((27, C, C), BF16)
CONV_FLOPS = 2 * CELLS * 27 * C * C


def shards(
    features,
    first_conv,
    second_conv,
    out_conv,
    norm_gains,
    norm_shifts,
    embed_weight,
    embed_bias,
    mod_shift,
    mod_scale,
    qkv_weight,
):
    place = jnp.stack([lax.axis_index("seq"), lax.axis_index("clip")]).astype(jnp.int32)
    row = shape(ROW, C)
    stats = shape(SEQ, 1, 128, dtype=F32)

    near_rows = jnp.stack([qkv_weight, swap(qkv_weight, "clip", 1, CLIPS)])
    far_rows = [swap(near_rows, "clip", bits, CLIPS) for bits in (2, 4, 6)]

    f0, f1, stats0 = call(
        split_kernel, [row, row, stats], [VMEM], [pltpu.VMEM((2, CELLS, 128), F32)], 0, 1 << 20
    )(features.reshape(FRAMES, 2, 32, C))
    top, low = neighbours(f0, f1)
    stats0 = exchange(stats0)
    hidden, h0, h1, stats1 = call(
        first_kernel,
        [shape(CELLS, C, dtype=F32), row, row, stats],
        [SMEM] + [VMEM] * 7 + [ANY],
        [WINDOW, WEIGHT, pltpu.SemaphoreType.DMA],
        CONV_FLOPS,
        5 << 20,
    )(place, stats0, top, f0, f1, low, norm_gains, norm_shifts, first_conv.reshape(27, C, C))
    top, low = neighbours(h0, h1)
    stats1 = exchange(stats1)
    b0, b1, stats2 = call(
        second_kernel,
        [row, row, stats],
        [SMEM] + [VMEM] * 8 + [ANY],
        [WINDOW, WEIGHT, pltpu.SemaphoreType.DMA],
        CONV_FLOPS,
        6 << 20,
    )(place, stats1, top, hidden, low, f0, f1, norm_gains, norm_shifts, second_conv.reshape(27, C, C))
    top, low = neighbours(b0, b1)

    embed, bias = call(embed_kernel, [shape(128, D), shape(8, D, dtype=F32)], [VMEM] * 2)(
        embed_weight, embed_bias.reshape(1, D)
    )
    folded = call(
        lambda near, a, b, c, *rest: fold_kernel(near, (a, b, c), *rest),
        shape(CLIPS, QPAD, 128),
        [VMEM] * 8,
    )(near_rows, *far_rows, embed, bias, mod_scale, mod_shift)
    fold_near, fold_far = gather_seq(folded)

    stats2 = exchange(stats2)
    patches, tokens = call(
        third_kernel,
        [shape(FRAMES * HALF, 4 * LAT, dtype=F32), shape(FRAMES * HALF, 128)],
        [SMEM] + [VMEM] * 10,
        [WINDOW],
        CONV_FLOPS // 2,
        4 << 20,
    )(
        place, stats2, top, b0, b1, low, norm_gains, norm_shifts, out_conv.reshape(27, C, LAT), embed, bias
    )
    token_near, token_far = gather_seq(tokens)
    sorted_rows = call(
        sort_kernel,
        shape(3 * HEADS * HDIM, 128),
        [SMEM] + [VMEM] * 2,
        [pltpu.VMEM((3 * HEADS * HDIM, 128), F32)],
    )(place, fold_near, fold_far)
    frame_heads = call(
        attend_kernel,
        shape(SEQ * HALF, HEADS * HDIM),
        [SMEM] + [VMEM] * 3,
        [pltpu.VMEM((SEQ, HEADS, HALF, 128), BF16), pltpu.VMEM((HEADS, SEQ * HALF, 128), BF16)],
    )(place, token_near, token_far, sorted_rows)
    latent = patches.reshape(FRAMES, HALF, 2, 2, LAT).transpose(0, 2, 1, 3, 4)
    return (
        latent.reshape(1, FRAMES, 2, 2 * HALF, LAT),
        frame_heads.reshape(1, 1, SEQ * HALF, HEADS * HDIM),
    )


def solution(mesh):
    placed = (
        P("clip", None, "seq", None, None),
        P(),
        P(),
        P(),
        P(),
        P(),
        P(),
        P(),
        P("clip", None),
        P("clip", None),
        P(("clip", "seq"), None),
    )
    return jax.shard_map(
        shards,
        mesh=mesh,
        in_specs=placed,
        out_specs=(P("clip", None, "seq", None, None), P("clip", "seq", None, None)),
        check_vma=False,
    )
```

```python
import functools
import math

import jax
import jax.numpy as jnp
from jax import lax
from jax.experimental import pallas as pl
from jax.experimental.pallas import tpu as pltpu
from jax.sharding import PartitionSpec as P

C = 256
GROUPS = 32
LAT = 16
D = 3072
HEADS = 12
HDIM = 128
FRAMES = 16
HALF = 16
ROW = FRAMES * 2 * HALF
CELLS = 2 * ROW
SEQ = 16
CLIPS = 8
QROWS = 36
QPAD = 48
EPS = 1e-06
F32 = jnp.float32
BF16 = jnp.bfloat16
VMEM = pl.BlockSpec(memory_space=pltpu.VMEM)
SMEM = pl.BlockSpec(memory_space=pltpu.SMEM)
ANY = pl.BlockSpec(memory_space=pl.ANY)


def nt_dot(a, b):
    return lax.dot_general(a, b, (((1,), (1,)), ((), ())), preferred_element_type=F32)


def dot(a, b):
    return jnp.dot(a, b, preferred_element_type=F32)


def exact_dot(rows, zero_one):
    high = rows.astype(BF16).astype(F32)
    rest = rows - high
    mid = rest.astype(BF16).astype(F32)
    low = rest - mid
    parts = jnp.concatenate([high, mid, low, jnp.zeros_like(low)], axis=0).astype(BF16)
    out = dot(parts, zero_one)
    return out[0:8] + out[8:16] + out[16:24]


def iota(shape, dim):
    return lax.broadcasted_iota(jnp.int32, shape, dim)


def one_hot(cond):
    return jnp.where(cond, 1.0, 0.0).astype(BF16)


def rows8(first, second=None):
    n = first.shape[1]
    row = iota((8, n), 0)
    out = jnp.where(row == 0, jnp.broadcast_to(first, (8, n)), 0.0)
    if second is not None:
        out = jnp.where(row == 1, jnp.broadcast_to(second, (8, n)), out)
    return out


def write_stats(cells, stats_ref):
    count = cells.shape[0]
    mean_c = jnp.sum(cells, axis=0, keepdims=True) * (1.0 / count)
    same = one_hot((iota((C, C), 0) >> 3) == (iota((C, C), 1) >> 3))
    mean_g = exact_dot(rows8(mean_c), same)[0:1] * (1.0 / 8)
    off = cells - mean_c
    square_c = jnp.sum(off * off, axis=0, keepdims=True)
    gap = mean_c - mean_g
    square_c = square_c + count * (gap * gap)
    lane = iota((C, 128), 1)
    pick = one_hot((iota((C, 128), 0) >> 3) == (lane & 31))
    both = exact_dot(rows8(mean_c * (1.0 / 8), square_c), pick)
    row = jnp.where(iota((1, 128), 1) < GROUPS, both[0:1], both[1:2])
    stats_ref[...] = jnp.broadcast_to(row[None], (SEQ, 1, 128))


def read_stats(stats_ref, count):
    each = stats_ref[...].reshape(SEQ, 128)
    lane = iota((1, 128), 1)
    mean = jnp.sum(each, axis=0, keepdims=True) * (1.0 / SEQ)
    off = each - mean
    between = jnp.sum(off * off, axis=0, keepdims=True) * (8.0 * count)
    within = mean * SEQ
    total = jnp.where(lane < GROUPS, between, jnp.where(lane < 2 * GROUPS, within, 0.0))
    mean = jnp.where(lane < GROUPS, mean, 0.0)
    spread = one_hot((iota((128, C), 0) & 31) == (iota((128, C), 1) >> 3))
    both = exact_dot(rows8(mean, total), spread)
    return both[0:1], lax.rsqrt(both[1:2] * (1.0 / (8.0 * count * SEQ)) + EPS)


def split_kernel(feat_ref, f0_ref, f1_ref, stats_ref, wide):
    cells = feat_ref[...].astype(F32).reshape(CELLS, C)
    for side in range(2):
        wide[side] = cells[:, side * 128 : (side + 1) * 128]
    for frame in range(FRAMES):
        for row, out in ((0, f0_ref), (1, f1_ref)):
            for parity in range(2):
                base = (frame * 2 + row) * 32 + parity
                at = (frame * 2 + parity) * HALF
                for side in range(2):
                    part = wide[side, pl.ds(base, HALF, stride=2)]
                    out[at : at + HALF, side * 128 : (side + 1) * 128] = part.astype(BF16)
    write_stats(cells, stats_ref)


def fill_window(place_ref, stats_ref, rows, gain, shift, window):
    mean, rstd = read_stats(stats_ref, CELLS)
    gain = rstd * gain * 0.5
    shift = shift * 0.5
    place = place_ref[0]
    top_on = jnp.where(place > 0, 1.0, 0.0).astype(F32)
    low_on = jnp.where(place < SEQ - 1, 1.0, 0.0).astype(F32)
    window[:, 0:2] = jnp.zeros((4, 2, 4, HALF, C), BF16)
    step = 4
    n = step * HALF
    pair = iota((n, C), 0) & (HALF - 1)
    for row, source in enumerate(rows):
        for frame in range(0, FRAMES, step):
            x = source[frame * 32 : (frame + step) * 32].astype(F32)
            half = (x - mean) * gain + shift
            act = half + half * jnp.tanh(half)
            if row == 0:
                act = act * top_on
            if row == 3:
                act = act * low_on
            act = act.reshape(step, 2, HALF, C)
            even = act[:, 0].reshape(n, C)
            odd = act[:, 1].reshape(n, C)
            odd_before = jnp.where(pair == 0, 0.0, pltpu.roll(odd, 1, 0))
            even_after = jnp.where(pair == HALF - 1, 0.0, pltpu.roll(even, n - 1, 0))
            for plane, part in enumerate((odd_before, even, odd, even_after)):
                window[row, 2 + frame : 2 + frame + step, plane] = part.astype(BF16).reshape(
                    step, HALF, C
                )


def convolve(window, weight, copies):
    total = None
    for p in range(3):
        copies[p].wait()
        for q in range(3):
            for r in range(3):
                cells = window[q : q + 2, p : p + FRAMES, r : r + 2].reshape(CELLS, C)
                term = dot(cells, weight[9 * p + 3 * q + r])
                total = term if total is None else total + term
    return total


def start_weights(source, weight, sems):
    copies = [
        pltpu.make_async_copy(source.at[9 * p : 9 * p + 9], weight.at[9 * p : 9 * p + 9], sems.at[p])
        for p in range(3)
    ]
    for copy in copies:
        copy.start()
    return copies


def first_kernel(
    place_ref, stats_ref, top_ref, f0_ref, f1_ref, low_ref, gain_ref, shift_ref, weight_hbm,
    hidden_ref, h0_ref, h1_ref, stats_out, window, weight, sems,
):
    copies = start_weights(weight_hbm, weight, sems)
    rows = (top_ref, f0_ref, f1_ref, low_ref)
    fill_window(place_ref, stats_ref, rows, gain_ref[0:1], shift_ref[0:1], window)
    hidden = convolve(window, weight, copies)
    hidden_ref[...] = hidden
    h0_ref[...] = hidden[:ROW].astype(BF16)
    h1_ref[...] = hidden[ROW:].astype(BF16)
    write_stats(hidden, stats_out)


def second_kernel(
    place_ref, stats_ref, top_ref, hidden_ref, low_ref, f0_ref, f1_ref, gain_ref, shift_ref, weight_hbm,
    b0_ref, b1_ref, stats_out, window, weight, sems,
):
    copies = start_weights(weight_hbm, weight, sems)
    rows = (top_ref, hidden_ref.at[0:ROW], hidden_ref.at[ROW:CELLS], low_ref)
    fill_window(place_ref, stats_ref, rows, gain_ref[1:2], shift_ref[1:2], window)
    added = convolve(window, weight, copies)
    b0 = (added[:ROW] + f0_ref[...].astype(F32)).astype(BF16)
    b1 = (added[ROW:] + f1_ref[...].astype(F32)).astype(BF16)
    b0_ref[...] = b0
    b1_ref[...] = b1
    write_stats(jnp.concatenate([b0, b1], axis=0).astype(F32), stats_out)


def column_to_row(column):
    square = jnp.broadcast_to(column, (128, 128))
    return jnp.sum(jnp.where(iota((128, 128), 0) == iota((128, 128), 1), square, 0.0), axis=0, keepdims=True)


def third_kernel(
    place_ref, stats_ref, top_ref, b0_ref, b1_ref, low_ref, gain_ref, shift_ref, weight_ref, embed_ref, bias_ref,
    own_ref, other_ref, patches_ref, parcel_ref, window, weight,
):
    n = FRAMES * HALF
    for p in range(3):
        for row in range(4):
            for plane in range(4):
                block = (p * 4 + row) * 4 + plane
                for dh in range(2):
                    for dw in range(2):
                        at = (2 * dh + dw) * LAT
                        q, r = row - dh, plane - dw
                        if 0 <= q < 3 and 0 <= r < 3:
                            weight[block, at : at + LAT] = weight_ref[9 * p + 3 * q + r]
                        else:
                            weight[block, at : at + LAT] = jnp.zeros((LAT, C), BF16)
    rows = (top_ref, b0_ref, b1_ref, low_ref)
    fill_window(place_ref, stats_ref, rows, gain_ref[2:3], shift_ref[2:3], window)
    patches = None
    for p in range(3):
        for row in range(4):
            for plane in range(4):
                cells = window[row, p : p + FRAMES, plane].reshape(n, C)
                term = nt_dot(cells, weight[(p * 4 + row) * 4 + plane])
                patches = term if patches is None else patches + term
    patches_ref[...] = patches
    rounded = patches.astype(BF16)
    embedded = dot(jnp.concatenate([rounded, rounded], axis=1), embed_ref[...]) + bias_ref[0:1]
    spread = jnp.sum(embedded * embedded, axis=1, keepdims=True) * (1.0 / D)
    rstd = lax.rsqrt(spread + EPS)
    scaled = (rounded.astype(F32) * rstd).reshape(FRAMES, 2, 8, 64)
    rstd = jnp.broadcast_to(rstd, (n, 128)).reshape(FRAMES, 2, 8, 128)
    both = jnp.concatenate([scaled[:, side].reshape(128, 64) for side in range(2)], axis=1)
    parcel_ref[0:128] = both.astype(BF16)
    line = iota((16, 128), 0)
    lines = jnp.where(line == 4, 1.0, 0.0)
    for side in range(2):
        each = column_to_row(rstd[:, side].reshape(128, 128)[:, 0:1])
        high = each.astype(BF16).astype(F32)
        lines = jnp.where(line == 2 * side, high, lines)
        lines = jnp.where(line == 2 * side + 1, each - high, lines)
    parcel_ref[128:144] = lines.astype(BF16)
    parcel_ref[144:288] = own_ref[...]
    parcel_ref[288:432] = other_ref[...]


def embed_kernel(embed_ref, bias_ref, embed_out, bias_out):
    embed = embed_ref[...].astype(F32)
    embed = embed - jnp.mean(embed, axis=1, keepdims=True)
    high = embed.astype(BF16)
    embed_out[0:64] = high
    embed_out[64:128] = (embed - high.astype(F32)).astype(BF16)
    bias = bias_ref[...]
    bias_out[...] = jnp.broadcast_to(bias - jnp.mean(bias, axis=1, keepdims=True), (8, D))


def fold_kernel(
    w0_ref, w1_ref, w2_ref, w3_ref, embed_ref, bias_ref, scale_ref, shift_ref, mods_ref,
    own_ref, other_ref, stacked, wide,
):
    for i, block in enumerate((w0_ref, w1_ref, w2_ref, w3_ref)):
        stacked[i * QPAD : i * QPAD + QROWS] = block[...]
        stacked[i * QPAD + QROWS : (i + 1) * QPAD] = jnp.zeros((QPAD - QROWS, D), BF16)
    embed = embed_ref[0:64].astype(F32) + embed_ref[64:128].astype(F32)
    row = iota((64, D), 0)
    sides = []
    for scale, shift in (
        (scale_ref[...], shift_ref[...]),
        (mods_ref[0:1], mods_ref[1:2]),
    ):
        scale = 1.0 + scale
        bias = bias_ref[0:1] * scale
        bias_high = bias.astype(BF16).astype(F32)
        shift_high = shift.astype(BF16).astype(F32)
        ends = jnp.where(row == 0, bias_high, jnp.where(row == 1, bias - bias_high, 0.0))
        ends = jnp.where(row == 2, shift_high, jnp.where(row == 3, shift - shift_high, ends))
        sides += [embed * scale, ends]
    every = jnp.concatenate(sides, axis=0).astype(BF16)
    out = nt_dot(stacked[...], every)
    lane = iota((4 * QPAD, 128), 1)
    for side, target in enumerate((own_ref, other_ref)):
        part = out[:, side * 128 : (side + 1) * 128]
        bias = part[:, 64:65] + part[:, 65:66]
        shift = part[:, 66:67] + part[:, 67:68]
        bias_high = bias.astype(BF16).astype(F32)
        shift_high = shift.astype(BF16).astype(F32)
        part = jnp.where((lane == 64) | (lane == 68), bias_high, part)
        part = jnp.where(lane == 65, bias - bias_high, part)
        part = jnp.where(lane == 66, shift_high, part)
        part = jnp.where(lane == 67, shift - shift_high, part)
        for i in range(4):
            wide[i * QROWS : (i + 1) * QROWS] = part[i * QPAD : i * QPAD + QROWS]
        target[...] = wide[...].astype(BF16)


WIDE = HEADS * HDIM


def sort_kernel(place_ref, near_ref, far_ref, plain_ref, turned_ref, keys_ref, loose, wide):
    seq, clip = place_ref[0], place_ref[1]
    for j in range(SEQ):
        source = (near_ref, far_ref)[j & 1]
        loose[j] = source[j >> 1, 144:432].astype(F32)
        for k in range(CLIPS):
            at = ((clip ^ (2 * (k & 3) + (k >> 2))) * SEQ + (seq ^ j)) * QROWS
            wide[pl.ds(at, QROWS)] = loose[j, k * QROWS : (k + 1) * QROWS]
    lane = iota((WIDE, 128), 1)
    for part in range(3):
        rows = wide[part * WIDE : (part + 1) * WIDE]
        if part != 1:
            at = part // 2 * WIDE
            plain_ref[at : at + WIDE] = rows.astype(BF16)
            turned_ref[at : at + WIDE] = pltpu.roll(rows, 64, 1).astype(BF16)
        else:
            bias = rows[:, 64:65] + rows[:, 65:66]
            shift = rows[:, 66:67] + rows[:, 67:68]
            left = jnp.where(lane < 64, rows, 0.0)
            keys_ref[:, 0:128] = left.astype(BF16)
            keys_ref[:, 256:384] = pltpu.roll(left, 64, 1).astype(BF16)
            for side in range(2):
                extra = jnp.where((lane == 2 * side) | (lane == 2 * side + 1), bias, 0.0)
                extra = jnp.where(lane == 4, shift, extra)
                keys_ref[:, 256 * side + 128 : 256 * side + 256] = extra.astype(BF16)


def attend_kernel(place_ref, near_ref, far_ref, plain_ref, turned_ref, keys_ref, out_ref, queries, mixed):
    seq = place_ref[0]
    blocks = [(near_ref, far_ref)[j & 1].at[j >> 1] for j in range(SEQ)]
    tables = (plain_ref, turned_ref)
    lane = iota((128, 128), 1)
    pick = one_hot(iota((8, 128), 1) == iota((8, 128), 0) + seq * 8)
    twin = pl.ds(pl.multiple_of((seq >> 1) * 16, 16), 16)
    tokens, scales = [], []
    for block in blocks:
        pair = block[twin].astype(F32)
        tokens.append(jnp.where((seq & 1) == 1, pair[8:16], pair[0:8]))
        scales.append(nt_dot(pick, block[128:144]))
    tokens = jnp.concatenate(tokens, axis=0)
    scales = jnp.concatenate(scales, axis=0)
    asked = []
    for side in range(2):
        high, low = scales[:, 2 * side : 2 * side + 1], scales[:, 2 * side + 1 : 2 * side + 2]
        spot = lane - 64 * (1 - side)
        own = jnp.where((lane >> 6) == side, tokens, 0.0)
        own = jnp.where((spot == 0) | (spot == 1), high, own)
        own = jnp.where((spot == 2) | (spot == 3), 1.0, own)
        own = jnp.where(spot == 4, low, own).astype(BF16)
        asked.append((nt_dot(own, tables[side][0:WIDE]) * (1.0 / math.sqrt(HDIM))).astype(BF16))
    for head in range(HEADS):
        cols = slice(head * HDIM, (head + 1) * HDIM)
        keyed = [
            dot(asked[side][:, cols], keys_ref[cols, 256 * side : 256 * side + 256]).reshape(SEQ, 8, 256)
            for side in range(2)
        ]
        queries[:, head] = jnp.concatenate(keyed, axis=1).astype(BF16)
    n = HEADS * HALF
    off = (iota((n, 128), 0) & 7) != (iota((n, 128), 1) & 7)
    bar = jnp.where(off, -jnp.inf, 0.0)
    lane = iota((n, 128), 1)
    side = (iota((n, 128), 0) >> 3) & 1
    mine = (lane >> 6) == side
    spot = lane - 64 * (1 - side)
    right = side[:, 0:1] == 1
    for j, block in enumerate(blocks):
        query = queries[j].reshape(n, 256)
        scores = nt_dot(query[:, 0:128], block[0:128]) + dot(query[:, 128:144], block[128:144]) + bar
        raised = jnp.exp(scores - jnp.max(scores, axis=1, keepdims=True)).astype(BF16)
        mix = dot(raised, block[0:128])
        ends = nt_dot(raised, block[128:144])
        inverse = 1.0 / ends[:, 4:5]
        scale = jnp.where(right, ends[:, 2:3] + ends[:, 3:4], ends[:, 0:1] + ends[:, 1:2]) * inverse
        high = scale.astype(BF16).astype(F32)
        mix = jnp.where(mine, mix * inverse, 0.0)
        mix = jnp.where((spot == 0) | (spot == 1), high, mix)
        mix = jnp.where((spot == 2) | (spot == 3), 1.0, mix)
        mix = jnp.where(spot == 4, scale - high, mix).reshape(HEADS, 2, 8, 128)
        for at in range(2):
            mixed[at, :, j * 8 : (j + 1) * 8] = mix[:, at]
    for head in range(HEADS):
        cols = slice(head * HDIM, (head + 1) * HDIM)
        rows = slice(WIDE + head * HDIM, WIDE + (head + 1) * HDIM)
        out = [
            nt_dot(mixed[at, head].astype(BF16), tables[at][rows]).reshape(SEQ, 8, HDIM) for at in range(2)
        ]
        out = jnp.concatenate(out, axis=1).astype(BF16)
        for j in range(SEQ):
            out_ref[pl.ds(pl.multiple_of((seq ^ j) * HALF, HALF), HALF), cols] = out[j]


def shape(*dims, dtype=BF16):
    return jax.ShapeDtypeStruct(dims, dtype)


def call(body, outs, ins, scratch=(), flops=0, moved=0, limit=32):
    return pl.pallas_call(
        body,
        out_shape=outs,
        in_specs=ins,
        out_specs=jax.tree.map(lambda _: VMEM, outs),
        scratch_shapes=list(scratch),
        compiler_params=pltpu.CompilerParams(vmem_limit_bytes=limit << 20),
        cost_estimate=pl.CostEstimate(flops=flops, bytes_accessed=moved, transcendentals=0),
        name=body.__name__ if hasattr(body, "__name__") else None,
    )


def swap(values, axis, bits, count):
    return lax.ppermute(values, axis, [(i, i ^ bits) for i in range(count)])


def neighbours(low_row, high_row):
    top = lax.ppermute(high_row, "seq", [(i, i + 1) for i in range(SEQ - 1)])
    low = lax.ppermute(low_row, "seq", [(i + 1, i) for i in range(SEQ - 1)])
    return top, low


def exchange(stats):
    return lax.all_to_all(stats, "seq", 0, 0, tiled=True)


def gather_seq(block, beside):
    over = swap(block, "seq", 8, SEQ)
    over, beside = lax.optimization_barrier((over, beside))
    pair = jnp.stack([block, over])
    others = [swap(pair, "seq", bits, SEQ) for bits in (2, 4, 6)]
    near = jnp.stack([pair] + others, axis=1).reshape((8,) + block.shape)
    return near, swap(near, "seq", 1, SEQ), beside


WINDOW = pltpu.VMEM((4, FRAMES + 2, 4, HALF, C), BF16)
WEIGHT = pltpu.VMEM((27, C, C), BF16)
SEMS = pltpu.SemaphoreType.DMA((3,))
CONV_FLOPS = 2 * CELLS * 27 * C * C


def shards(
    features,
    first_conv,
    second_conv,
    out_conv,
    norm_gains,
    norm_shifts,
    embed_weight,
    embed_bias,
    mod_shift,
    mod_scale,
    qkv_weight,
):
    place = jnp.stack([lax.axis_index("seq"), lax.axis_index("clip")]).astype(jnp.int32)
    row = shape(ROW, C)
    stats = shape(SEQ, 1, 128, dtype=F32)
    taps = 27

    rows = [qkv_weight] + [swap(qkv_weight, "clip", bits, CLIPS) for bits in (2, 4, 6)]
    mods = swap(jnp.concatenate([mod_scale, mod_shift], axis=0), "clip", 1, CLIPS)

    f0, f1, stats0 = call(
        split_kernel, [row, row, stats], [VMEM], [pltpu.VMEM((2, CELLS, 128), F32)], 0, 1 << 20
    )(features.reshape(FRAMES, 2, 32, C))
    top, low = neighbours(f0, f1)
    stats0 = exchange(stats0)
    hidden, h0, h1, stats1 = call(
        first_kernel,
        [shape(CELLS, C, dtype=F32), row, row, stats],
        [SMEM] + [VMEM] * 7 + [ANY],
        [WINDOW, WEIGHT, SEMS],
        CONV_FLOPS,
        5 << 20,
        56,
    )(place, stats0, top, f0, f1, low, norm_gains, norm_shifts, first_conv.reshape(taps, C, C))
    top, low = neighbours(h0, h1)

    embed, bias = call(embed_kernel, [shape(128, D), shape(8, D, dtype=F32)], [VMEM] * 2)(
        embed_weight, embed_bias.reshape(1, D)
    )
    folded = shape(4 * QROWS, 128)
    own, other = call(
        fold_kernel,
        [folded, folded],
        [VMEM] * 9,
        [pltpu.VMEM((4 * QPAD, D), BF16), pltpu.VMEM((4 * QROWS, 128), F32)],
    )(*rows, embed, bias, mod_scale, mod_shift, mods)
    stats1 = exchange(stats1)
    stats1, own, other = lax.optimization_barrier((stats1, own, other))
    other = swap(other, "clip", 1, CLIPS)

    b0, b1, stats2 = call(
        second_kernel,
        [row, row, stats],
        [SMEM] + [VMEM] * 8 + [ANY],
        [WINDOW, WEIGHT, SEMS],
        CONV_FLOPS,
        6 << 20,
    )(place, stats1, top, hidden, low, f0, f1, norm_gains, norm_shifts, second_conv.reshape(taps, C, C))
    top, low = neighbours(b0, b1)
    stats2 = exchange(stats2)
    patches, parcel = call(
        third_kernel,
        [shape(FRAMES * HALF, 4 * LAT, dtype=F32), shape(432, 128)],
        [SMEM] + [VMEM] * 12,
        [WINDOW, pltpu.VMEM((48, 4 * LAT, C), BF16)],
        CONV_FLOPS // 2,
        4 << 20,
    )(
        place, stats2, top, b0, b1, low, norm_gains, norm_shifts,
        out_conv.transpose(0, 1, 2, 4, 3).reshape(taps, LAT, C), embed, bias, own, other,
    )
    latent = patches.reshape(FRAMES, HALF, 2, 2, LAT).transpose(0, 2, 1, 3, 4)
    latent = latent.reshape(1, FRAMES, 2, 2 * HALF, LAT)
    near, far, latent = gather_seq(parcel, latent)
    plain, turned, keys = call(
        sort_kernel,
        [shape(2 * WIDE, 128), shape(2 * WIDE, 128), shape(WIDE, 512)],
        [SMEM] + [VMEM] * 2,
        [pltpu.VMEM((SEQ, 8 * QROWS, 128), F32), pltpu.VMEM((3 * WIDE, 128), F32)],
    )(place, near, far)
    frame_heads = call(
        attend_kernel,
        shape(SEQ * HALF, WIDE),
        [SMEM] + [VMEM] * 5,
        [pltpu.VMEM((SEQ, HEADS, HALF, 256), BF16), pltpu.VMEM((2, HEADS, 128, 128), F32)],
    )(place, near, far, plain, turned, keys)
    return (latent, frame_heads.reshape(1, 1, SEQ * HALF, WIDE))


def solution(mesh):
    placed = (
        P("clip", None, "seq", None, None),
        P(),
        P(),
        P(),
        P(),
        P(),
        P(),
        P(),
        P("clip", None),
        P("clip", None),
        P(("clip", "seq"), None),
    )
    return jax.shard_map(
        shards,
        mesh=mesh,
        in_specs=placed,
        out_specs=(P("clip", None, "seq", None, None), P("clip", "seq", None, None)),
        check_vma=False,
    )
```

```python
import functools
import math

import jax
import jax.numpy as jnp
from jax import lax
from jax.experimental import pallas as pl
from jax.experimental.pallas import tpu as pltpu
from jax.sharding import PartitionSpec as P

C = 256
GROUPS = 32
LAT = 16
D = 3072
HEADS = 12
HDIM = 128
FRAMES = 16
HALF = 16
ROW = FRAMES * 2 * HALF
CELLS = 2 * ROW
SEQ = 16
CLIPS = 8
QROWS = 36
QPAD = 48
EPS = 1e-06
F32 = jnp.float32
BF16 = jnp.bfloat16
VMEM = pl.BlockSpec(memory_space=pltpu.VMEM)
SMEM = pl.BlockSpec(memory_space=pltpu.SMEM)
HBM = pl.BlockSpec(memory_space=pltpu.HBM)
DMA = pltpu.SemaphoreType.DMA


def nt_dot(a, b):
    return lax.dot_general(a, b, (((1,), (1,)), ((), ())), preferred_element_type=F32)


def dot(a, b):
    return jnp.dot(a, b, preferred_element_type=F32)


def exact_dot(rows, zero_one):
    high = rows.astype(BF16).astype(F32)
    rest = rows - high
    mid = rest.astype(BF16).astype(F32)
    low = rest - mid
    parts = jnp.concatenate([high, mid, low, jnp.zeros_like(low)], axis=0).astype(BF16)
    out = dot(parts, zero_one)
    return out[0:8] + out[8:16] + out[16:24]


def iota(shape, dim):
    return lax.broadcasted_iota(jnp.int32, shape, dim)


def one_hot(cond):
    return jnp.where(cond, 1.0, 0.0).astype(BF16)


def rows8(first, second=None):
    n = first.shape[1]
    row = iota((8, n), 0)
    out = jnp.where(row == 0, jnp.broadcast_to(first, (8, n)), 0.0)
    if second is not None:
        out = jnp.where(row == 1, jnp.broadcast_to(second, (8, n)), out)
    return out


def write_stats(cells, stats_ref):
    count = cells.shape[0]
    mean_c = jnp.sum(cells, axis=0, keepdims=True) * (1.0 / count)
    same = one_hot((iota((C, C), 0) >> 3) == (iota((C, C), 1) >> 3))
    mean_g = exact_dot(rows8(mean_c), same)[0:1] * (1.0 / 8)
    off = cells - mean_c
    square_c = jnp.sum(off * off, axis=0, keepdims=True)
    gap = mean_c - mean_g
    square_c = square_c + count * (gap * gap)
    lane = iota((C, 128), 1)
    pick = one_hot((iota((C, 128), 0) >> 3) == (lane & 31))
    both = exact_dot(rows8(mean_c * (1.0 / 8), square_c), pick)
    row = jnp.where(iota((1, 128), 1) < GROUPS, both[0:1], both[1:2])
    stats_ref[...] = jnp.broadcast_to(row[None], (SEQ, 1, 128))


def read_stats(stats_ref, count):
    each = stats_ref[...].reshape(SEQ, 128)
    lane = iota((1, 128), 1)
    mean = jnp.sum(each, axis=0, keepdims=True) * (1.0 / SEQ)
    off = each - mean
    between = jnp.sum(off * off, axis=0, keepdims=True) * (8.0 * count)
    within = mean * SEQ
    total = jnp.where(lane < GROUPS, between, jnp.where(lane < 2 * GROUPS, within, 0.0))
    mean = jnp.where(lane < GROUPS, mean, 0.0)
    spread = one_hot((iota((128, C), 0) & 31) == (iota((128, C), 1) >> 3))
    both = exact_dot(rows8(mean, total), spread)
    return both[0:1], lax.rsqrt(both[1:2] * (1.0 / (8.0 * count * SEQ)) + EPS)


def own_rows(place_ref, rows_ref, near_ref, far_ref):
    odd = place_ref[0] & 1
    near_ref[...] = rows_ref[pl.ds(pl.multiple_of((1 - odd) * ROW, ROW), ROW)].astype(BF16)
    far_ref[...] = rows_ref[pl.ds(pl.multiple_of(odd * ROW, ROW), ROW)].astype(BF16)


def split_kernel(
    place_ref, feat_hbm, gain_hbm, shift_hbm, scale_hbm, mod_hbm,
    rows_ref, near_ref, far_ref, stats_ref, norms_ref, mods_ref,
    feat_ref, gain_ref, shift_ref, scale_ref, mod_ref, wide, sems,
):
    sources = (feat_hbm, gain_hbm, shift_hbm, scale_hbm, mod_hbm)
    targets = (feat_ref, gain_ref, shift_ref, scale_ref, mod_ref)
    copies = [pltpu.make_async_copy(a, b, sems.at[i]) for i, (a, b) in enumerate(zip(sources, targets))]
    for copy in copies:
        copy.start()
    for copy in copies:
        copy.wait()
    norms_ref[0:3] = gain_ref[...]
    norms_ref[4:7] = shift_ref[...]
    mods_ref[0:1] = scale_ref[...]
    mods_ref[1:2] = mod_ref[...]
    cells = feat_ref[...].astype(F32).reshape(CELLS, C)
    for side in range(2):
        wide[side] = cells[:, side * 128 : (side + 1) * 128]
    for frame in range(FRAMES):
        for row in range(2):
            for parity in range(2):
                base = (frame * 2 + row) * 32 + parity
                at = row * ROW + (frame * 2 + parity) * HALF
                for side in range(2):
                    part = wide[side, pl.ds(base, HALF, stride=2)]
                    rows_ref[at : at + HALF, side * 128 : (side + 1) * 128] = part.astype(BF16)
    own_rows(place_ref, rows_ref, near_ref, far_ref)
    write_stats(cells, stats_ref)


def fill_window(place_ref, stats_ref, rows_ref, near_ref, far_ref, norms_ref, layer, window, centers=None, load=None):
    mean, rstd = read_stats(stats_ref, CELLS)
    gain = rstd * norms_ref[layer : layer + 1] * 0.5
    shift = norms_ref[4 + layer : 5 + layer] * 0.5
    place = place_ref[0]
    odd = place & 1
    near_at = 3 * (1 - odd)
    far_on = jnp.where((place > 0) & (place < SEQ - 1), 1.0, 0.0).astype(F32)
    window[:, 0:2] = jnp.zeros((4, 2, 4, HALF, C), BF16)
    step = 4
    n = step * HALF
    pair = iota((n, C), 0) & (HALF - 1)
    level = -mean
    levels = [level] * 4 if centers is None else [center + level for center in centers]
    sources = (
        (near_at, near_ref),
        (3 - near_at, far_ref),
        (1, rows_ref.at[0:ROW]),
        (2, rows_ref.at[ROW:CELLS]),
    )
    for which, (row, source) in enumerate(sources):
        if which == 2 and load is not None:
            load.wait()
        for frame in range(0, FRAMES, step):
            x = source[frame * 32 : (frame + step) * 32].astype(F32)
            half = (x + levels[which]) * gain + shift
            act = half + half * jnp.tanh(half)
            if which == 1:
                act = act * far_on
            act = act.reshape(step, 2, HALF, C)
            even = act[:, 0].reshape(n, C)
            odd_ones = act[:, 1].reshape(n, C)
            odd_before = jnp.where(pair == 0, 0.0, pltpu.roll(odd_ones, 1, 0))
            even_after = jnp.where(pair == HALF - 1, 0.0, pltpu.roll(even, n - 1, 0))
            for plane, part in enumerate((odd_before, even, odd_ones, even_after)):
                window[row, 2 + frame : 2 + frame + step, plane] = part.astype(BF16).reshape(
                    step, HALF, C
                )


def convolve(window, weight):
    total = None
    for tap in range(27):
        p, q, r = tap // 9, tap // 3 % 3, tap % 3
        cells = window[q : q + 2, p : p + FRAMES, r : r + 2].reshape(CELLS, C)
        term = dot(cells, weight[tap])
        total = term if total is None else total + term
    return total


def first_kernel(
    place_ref, stats_ref, rows_ref, near_ref, far_ref, norms_ref, weight_hbm,
    hidden_hbm, center_ref, near_out, far_out, stats_out, window, weight, hidden_ref, sems,
):
    copy = pltpu.make_async_copy(weight_hbm, weight, sems.at[0])
    copy.start()
    fill_window(place_ref, stats_ref, rows_ref, near_ref, far_ref, norms_ref, 0, window)
    copy.wait()
    hidden = convolve(window, weight)
    center = jnp.sum(hidden, axis=0, keepdims=True) * (1.0 / CELLS)
    hidden_ref[...] = (hidden - center).astype(BF16)
    copy = pltpu.make_async_copy(hidden_ref, hidden_hbm, sems.at[1])
    copy.start()
    center_ref[...] = jnp.broadcast_to(center, (8, C))
    high = center.astype(BF16).astype(F32)
    mid = (center - high).astype(BF16).astype(F32)
    line = iota((16, C), 0)
    terms = jnp.where(line == 0, high, jnp.where(line == 1, mid, jnp.where(line == 2, center - high - mid, 0.0)))
    own_rows(place_ref, hidden_ref, near_out.at[0:ROW], far_out.at[0:ROW])
    near_out[ROW : ROW + 16] = terms.astype(BF16)
    far_out[ROW : ROW + 16] = terms.astype(BF16)
    write_stats(hidden, stats_out)
    copy.wait()


def second_kernel(
    place_ref, stats_ref, hidden_hbm, center_ref, near_ref, far_ref, norms_ref, feat_ref, weight_hbm,
    block_ref, near_out, far_out, stats_out, window, weight, hidden_ref, sems,
):
    load = pltpu.make_async_copy(hidden_hbm, hidden_ref, sems.at[1])
    load.start()
    copy = pltpu.make_async_copy(weight_hbm, weight, sems.at[0])
    copy.start()
    own = center_ref[0:1]
    centers = [jnp.sum(ref[ROW : ROW + 16].astype(F32), axis=0, keepdims=True) for ref in (near_ref, far_ref)]
    centers += [own, own]
    fill_window(place_ref, stats_ref, hidden_ref, near_ref, far_ref, norms_ref, 1, window, centers, load)
    copy.wait()
    block = (convolve(window, weight) + feat_ref[...].astype(F32)).astype(BF16)
    block_ref[...] = block
    own_rows(place_ref, block_ref, near_out, far_out)
    write_stats(block.astype(F32), stats_out)


def column_to_row(column):
    square = jnp.broadcast_to(column, (128, 128))
    return jnp.sum(jnp.where(iota((128, 128), 0) == iota((128, 128), 1), square, 0.0), axis=0, keepdims=True)


def third_kernel(
    place_ref, stats_ref, rows_ref, near_ref, far_ref, norms_ref, weight_ref, embed_ref, bias_ref,
    own_ref, other_ref, patches_ref, parcel_ref, window, weight,
):
    n = FRAMES * HALF
    for p in range(3):
        for row in range(4):
            for plane in range(4):
                block = (p * 4 + row) * 4 + plane
                for dh in range(2):
                    for dw in range(2):
                        at = (2 * dh + dw) * LAT
                        q, r = row - dh, plane - dw
                        if 0 <= q < 3 and 0 <= r < 3:
                            weight[block, at : at + LAT] = weight_ref[9 * p + 3 * q + r]
                        else:
                            weight[block, at : at + LAT] = jnp.zeros((LAT, C), BF16)
    fill_window(place_ref, stats_ref, rows_ref, near_ref, far_ref, norms_ref, 2, window)
    patches = None
    for p in range(3):
        for row in range(4):
            for plane in range(4):
                cells = window[row, p : p + FRAMES, plane].reshape(n, C)
                term = nt_dot(cells, weight[(p * 4 + row) * 4 + plane])
                patches = term if patches is None else patches + term
    patches_ref[...] = patches
    rounded = patches.astype(BF16)
    embedded = dot(jnp.concatenate([rounded, rounded], axis=1), embed_ref[...]) + bias_ref[0:1]
    spread = jnp.sum(embedded * embedded, axis=1, keepdims=True) * (1.0 / D)
    rstd = lax.rsqrt(spread + EPS)
    scaled = (rounded.astype(F32) * rstd).reshape(FRAMES, 2, 8, 64)
    rstd = jnp.broadcast_to(rstd, (n, 128)).reshape(FRAMES, 2, 8, 128)
    both = jnp.concatenate([scaled[:, side].reshape(128, 64) for side in range(2)], axis=1)
    parcel_ref[0:128] = both.astype(BF16)
    line = iota((16, 128), 0)
    lines = jnp.where(line == 4, 1.0, 0.0)
    for side in range(2):
        each = column_to_row(rstd[:, side].reshape(128, 128)[:, 0:1])
        high = each.astype(BF16).astype(F32)
        lines = jnp.where(line == 2 * side, high, lines)
        lines = jnp.where(line == 2 * side + 1, each - high, lines)
    parcel_ref[128:144] = lines.astype(BF16)
    parcel_ref[144:288] = own_ref[...]
    parcel_ref[288:432] = other_ref[...]


def embed_kernel(embed_ref, bias_ref, embed_out, bias_out):
    embed = embed_ref[...].astype(F32)
    embed = embed - jnp.mean(embed, axis=1, keepdims=True)
    high = embed.astype(BF16)
    embed_out[0:64] = high
    embed_out[64:128] = (embed - high.astype(F32)).astype(BF16)
    bias = bias_ref[...]
    bias_out[...] = jnp.broadcast_to(bias - jnp.mean(bias, axis=1, keepdims=True), (8, D))


def fold_kernel(
    here_ref, there_ref, embed_ref, bias_ref, own_mods_ref, mods_ref, own_ref, other_ref, stacked, wide,
):
    for i in range(4):
        stacked[i * QPAD : i * QPAD + QROWS] = (here_ref, there_ref)[i >> 1][i & 1]
        stacked[i * QPAD + QROWS : (i + 1) * QPAD] = jnp.zeros((QPAD - QROWS, D), BF16)
    embed = embed_ref[0:64].astype(F32) + embed_ref[64:128].astype(F32)
    row = iota((64, D), 0)
    sides = []
    for mod_ref in (own_mods_ref, mods_ref):
        scale, shift = 1.0 + mod_ref[0:1], mod_ref[1:2]
        bias = bias_ref[0:1] * scale
        bias_high = bias.astype(BF16).astype(F32)
        shift_high = shift.astype(BF16).astype(F32)
        ends = jnp.where(row == 0, bias_high, jnp.where(row == 1, bias - bias_high, 0.0))
        ends = jnp.where(row == 2, shift_high, jnp.where(row == 3, shift - shift_high, ends))
        sides += [embed * scale, ends]
    every = jnp.concatenate(sides, axis=0).astype(BF16)
    out = nt_dot(stacked[...], every)
    lane = iota((4 * QPAD, 128), 1)
    for side, target in enumerate((own_ref, other_ref)):
        part = out[:, side * 128 : (side + 1) * 128]
        bias = part[:, 64:65] + part[:, 65:66]
        shift = part[:, 66:67] + part[:, 67:68]
        bias_high = bias.astype(BF16).astype(F32)
        shift_high = shift.astype(BF16).astype(F32)
        part = jnp.where((lane == 64) | (lane == 68), bias_high, part)
        part = jnp.where(lane == 65, bias - bias_high, part)
        part = jnp.where(lane == 66, shift_high, part)
        part = jnp.where(lane == 67, shift - shift_high, part)
        for i in range(4):
            wide[i * QROWS : (i + 1) * QROWS] = part[i * QPAD : i * QPAD + QROWS]
        target[...] = wide[...].astype(BF16)


WIDE = HEADS * HDIM


def sort_kernel(place_ref, clip_ref, near_ref, far_ref, asks_ref, keys_ref, values_ref, loose, wide):
    seq, clip = place_ref[0], clip_ref[0]
    for j in range(SEQ):
        source = (near_ref, far_ref)[j & 1]
        loose[j] = source[j >> 1, 144:432].astype(F32)
        for k in range(CLIPS):
            at = ((clip ^ (2 * (k & 3) + (k >> 2))) * SEQ + (seq ^ j)) * QROWS
            wide[pl.ds(at, QROWS)] = loose[j, k * QROWS : (k + 1) * QROWS]
    lane = iota((WIDE, 128), 1)
    rows = wide[0:WIDE]
    asks_ref[:, 0:128] = rows.astype(BF16)
    asks_ref[:, 128:256] = pltpu.roll(rows, 64, 1).astype(BF16)
    for part, target in ((1, keys_ref), (2, values_ref)):
        rows = wide[part * WIDE : (part + 1) * WIDE]
        bias = rows[:, 64:65] + rows[:, 65:66]
        shift = rows[:, 66:67] + rows[:, 67:68]
        left = jnp.where(lane < 64, rows, 0.0)
        target[:, 0:128] = left.astype(BF16)
        target[:, 256:384] = pltpu.roll(left, 64, 1).astype(BF16)
        for side in range(2):
            extra = jnp.where((lane == 2 * side) | (lane == 2 * side + 1), bias, 0.0)
            extra = jnp.where(lane == 4, shift, extra)
            target[:, 256 * side + 128 : 256 * side + 256] = extra.astype(BF16)


def attend_kernel(place_ref, near_ref, far_ref, asks_ref, keys_ref, values_ref, out_ref, queries, mixed, scores, weights):
    seq = place_ref[0]
    blocks = [(near_ref, far_ref)[j & 1].at[j >> 1] for j in range(SEQ)]
    lane = iota((128, 128), 1)
    pick = one_hot(iota((8, 128), 1) == iota((8, 128), 0) + seq * 8)
    twin = pl.ds(pl.multiple_of((seq >> 1) * 16, 16), 16)
    tokens, scales = [], []
    for block in blocks:
        pair = block[twin].astype(F32)
        tokens.append(jnp.where((seq & 1) == 1, pair[8:16], pair[0:8]))
        scales.append(nt_dot(pick, block[128:144]))
    tokens = jnp.concatenate(tokens, axis=0)
    scales = jnp.concatenate(scales, axis=0)
    asked = []
    for side in range(2):
        high, low = scales[:, 2 * side : 2 * side + 1], scales[:, 2 * side + 1 : 2 * side + 2]
        spot = lane - 64 * (1 - side)
        own = jnp.where((lane >> 6) == side, tokens, 0.0)
        own = jnp.where((spot == 0) | (spot == 1), high, own)
        own = jnp.where((spot == 2) | (spot == 3), 1.0, own)
        own = jnp.where(spot == 4, low, own).astype(BF16)
        asked.append((nt_dot(own, asks_ref[:, 128 * side : 128 * side + 128]) * (1.0 / math.sqrt(HDIM))).astype(BF16))
    for head in range(HEADS):
        cols = slice(head * HDIM, (head + 1) * HDIM)
        keyed = [
            dot(asked[side][:, cols], keys_ref[cols, 256 * side : 256 * side + 256]).reshape(SEQ, 8, 256)
            for side in range(2)
        ]
        queries[:, head] = jnp.concatenate(keyed, axis=1).astype(BF16)
    n = HEADS * HALF
    same = jnp.where(iota((8, n), 0) == (iota((8, n), 1) & 7), 1.0, 0.0)
    for j, block in enumerate(blocks):
        query = queries[j].reshape(n, 256)
        ends = lax.dot_general(block[128:144], query[:, 128:144], (((0,), (1,)), ((), ())), preferred_element_type=F32)
        scores[j] = nt_dot(block[0:128], query[:, 0:128]) + ends
    for j in range(SEQ):
        each = scores[j].reshape(FRAMES, 8, n)
        raised = jnp.exp(each - jnp.max(each, axis=0, keepdims=True))
        shares = raised * (same / jnp.sum(raised, axis=0))
        weights[j] = jnp.transpose(shares.astype(BF16).reshape(128, n))
    for j, block in enumerate(blocks):
        mix = dot(weights[j], block[0:128]).reshape(HEADS, 2, 8, 128)
        ends = nt_dot(weights[j], block[128:144]).reshape(HEADS, 2, 8, 16)
        for side in range(2):
            mixed[side, :, j * 8 : (j + 1) * 8, 0:128] = mix[:, side]
            mixed[side, :, j * 8 : (j + 1) * 8, 128:144] = ends[:, side]
    for head in range(HEADS):
        cols = slice(head * HDIM, (head + 1) * HDIM)
        out = []
        for side in range(2):
            part = nt_dot(mixed[side, head, :, 0:128].astype(BF16), values_ref[cols, 256 * side : 256 * side + 128])
            at = 256 * side + 128
            part = part + nt_dot(mixed[side, head, :, 128:144].astype(BF16), values_ref[cols, at : at + 16])
            out.append(part.reshape(SEQ, 8, HDIM))
        out = jnp.concatenate(out, axis=1).astype(BF16)
        for j in range(SEQ):
            out_ref[pl.ds(pl.multiple_of((seq ^ j) * HALF, HALF), HALF), cols] = out[j]


def shape(*dims, dtype=BF16):
    return jax.ShapeDtypeStruct(dims, dtype)


def call(body, outs, ins, scratch=(), flops=0, moved=0, limit=32, first_out=VMEM):
    outs = list(outs) if isinstance(outs, list) else outs
    if first_out is HBM:
        outs[0] = pltpu.HBM(outs[0].shape, outs[0].dtype)
    kernel = pl.pallas_call(
        body,
        out_shape=outs,
        in_specs=ins,
        out_specs=[first_out] + [VMEM] * (len(outs) - 1) if isinstance(outs, list) else VMEM,
        scratch_shapes=list(scratch),
        compiler_params=pltpu.CompilerParams(vmem_limit_bytes=limit << 20),
        cost_estimate=pl.CostEstimate(flops=flops, bytes_accessed=moved, transcendentals=0),
        name=body.__name__,
    )

    def run(*args):
        return kernel(
            *(pltpu.with_memory_space_constraint(x, pltpu.HBM) if spec is HBM else x for x, spec in zip(args, ins))
        )

    return run


def swap(values, axis, bits, count):
    return lax.ppermute(values, axis, [(i, i ^ bits) for i in range(count)])


CHIP_PAIRS = [(i, i ^ 1) for i in range(SEQ)]
NEXT_PAIRS = [(i, (i + 1 if i & 1 else i - 1) % SEQ) for i in range(SEQ)]


def neighbours(near, far):
    far = lax.ppermute(far, "seq", NEXT_PAIRS)
    return lax.ppermute(near, "seq", CHIP_PAIRS), far


def exchange(stats):
    return lax.all_to_all(stats, "seq", 0, 0, tiled=True)


def gather_seq(block, beside):
    over = swap(block, "seq", 8, SEQ)
    over, beside = lax.optimization_barrier((over, beside))
    pair = jnp.stack([block, over])
    others = [swap(pair, "seq", bits, SEQ) for bits in (2, 4, 6)]
    near = jnp.stack([pair] + others, axis=1).reshape((8,) + block.shape)
    return near, swap(near, "seq", 1, SEQ), beside


WINDOW = pltpu.VMEM((4, FRAMES + 2, 4, HALF, C), BF16)
WEIGHT = pltpu.VMEM((27, C, C), BF16)
CONV_FLOPS = 2 * CELLS * 27 * C * C


def shards(
    features,
    first_conv,
    second_conv,
    out_conv,
    norm_gains,
    norm_shifts,
    embed_weight,
    embed_bias,
    mod_shift,
    mod_scale,
    qkv_weight,
):
    place = lax.axis_index("seq").astype(jnp.int32).reshape(1)
    clip = lax.axis_index("clip").astype(jnp.int32).reshape(1)
    row = shape(ROW, C)
    stats = shape(SEQ, 1, 128, dtype=F32)
    taps = 27

    beside = swap(qkv_weight, "clip", 2, CLIPS)
    cells = shape(CELLS, C)
    long_row = shape(ROW + 16, C)
    rows_f, near, far, stats0, norms, own_mods = call(
        split_kernel,
        [cells, row, row, stats, shape(8, C, dtype=F32), shape(2, D, dtype=F32)],
        [SMEM] + [HBM] * 5,
        [
            pltpu.VMEM((FRAMES, 2, 32, C), BF16),
            pltpu.VMEM((3, C), F32),
            pltpu.VMEM((3, C), F32),
            pltpu.VMEM((1, D), F32),
            pltpu.VMEM((1, D), F32),
            pltpu.VMEM((2, CELLS, 128), F32),
            DMA((5,)),
        ],
        0,
        1 << 20,
    )(place, features.reshape(FRAMES, 2, 32, C), norm_gains, norm_shifts, mod_scale, mod_shift)
    near, far = neighbours(near, far)
    mods = swap(own_mods, "clip", 1, CLIPS)
    stats0 = exchange(stats0)
    stats0, mods, beside = lax.optimization_barrier((stats0, mods, beside))
    here = jnp.stack([qkv_weight, beside])
    there = swap(here, "clip", 4, CLIPS)
    hidden, center, near_h, far_h, stats1 = call(
        first_kernel,
        [cells, shape(8, C, dtype=F32), long_row, long_row, stats],
        [SMEM] + [VMEM] * 5 + [HBM],
        [WINDOW, WEIGHT, pltpu.VMEM((CELLS, C), BF16), DMA((2,))],
        CONV_FLOPS,
        5 << 20,
        first_out=HBM,
    )(place, stats0, rows_f, near, far, norms, first_conv.reshape(taps, C, C))
    near, far = neighbours(near_h, far_h)

    embed, bias = call(embed_kernel, [shape(128, D), shape(8, D, dtype=F32)], [VMEM] * 2)(
        embed_weight, embed_bias.reshape(1, D)
    )
    folded = shape(4 * QROWS, 128)
    own, other = call(
        fold_kernel,
        [folded, folded],
        [VMEM] * 6,
        [pltpu.VMEM((4 * QPAD, D), BF16), pltpu.VMEM((4 * QROWS, 128), F32)],
    )(here, there, embed, bias, own_mods, mods)
    stats1 = exchange(stats1)
    stats1, own, other = lax.optimization_barrier((stats1, own, other))
    other = swap(other, "clip", 1, CLIPS)

    block, near_b, far_b, stats2 = call(
        second_kernel,
        [cells, row, row, stats],
        [SMEM, VMEM, HBM] + [VMEM] * 5 + [HBM],
        [WINDOW, WEIGHT, pltpu.VMEM((CELLS, C), BF16), DMA((2,))],
        CONV_FLOPS,
        6 << 20,
    )(place, stats1, hidden, center, near, far, norms, rows_f, second_conv.reshape(taps, C, C))
    near, far = neighbours(near_b, far_b)
    stats2 = exchange(stats2)
    patches, parcel = call(
        third_kernel,
        [shape(FRAMES * HALF, 4 * LAT, dtype=F32), shape(432, 128)],
        [SMEM] + [VMEM] * 10,
        [WINDOW, pltpu.VMEM((48, 4 * LAT, C), BF16)],
        CONV_FLOPS // 2,
        4 << 20,
    )(
        place, stats2, block, near, far, norms,
        out_conv.transpose(0, 1, 2, 4, 3).reshape(taps, LAT, C), embed, bias, own, other,
    )
    latent = patches.reshape(FRAMES, HALF, 2, 2, LAT).transpose(0, 2, 1, 3, 4)
    latent = latent.reshape(1, FRAMES, 2, 2 * HALF, LAT)
    near, far, latent = gather_seq(parcel, latent)
    asks, keys, values = call(
        sort_kernel,
        [shape(WIDE, 256), shape(WIDE, 512), shape(WIDE, 512)],
        [SMEM] * 2 + [VMEM] * 2,
        [pltpu.VMEM((SEQ, 8 * QROWS, 128), F32), pltpu.VMEM((3 * WIDE, 128), F32)],
    )(place, clip, near, far)
    frame_heads = call(
        attend_kernel,
        shape(SEQ * HALF, WIDE),
        [SMEM] + [VMEM] * 5,
        [
            pltpu.VMEM((SEQ, HEADS, HALF, 256), BF16),
            pltpu.VMEM((2, HEADS, 128, 256), F32),
            pltpu.VMEM((SEQ, 128, HEADS * HALF), F32),
            pltpu.VMEM((SEQ, HEADS * HALF, 128), BF16),
        ],
    )(place, near, far, asks, keys, values)
    return (latent, frame_heads.reshape(1, 1, SEQ * HALF, WIDE))


def solution(mesh):
    placed = (
        P("clip", None, "seq", None, None),
        P(),
        P(),
        P(),
        P(),
        P(),
        P(),
        P(),
        P("clip", None),
        P("clip", None),
        P(("clip", "seq"), None),
    )
    return jax.shard_map(
        shards,
        mesh=mesh,
        in_specs=placed,
        out_specs=(P("clip", None, "seq", None, None), P("clip", "seq", None, None)),
        check_vma=False,
    )
```

```python
import functools
import math

import jax
import jax.numpy as jnp
from jax import lax
from jax.experimental import pallas as pl
from jax.experimental.pallas import tpu as pltpu
from jax.sharding import PartitionSpec as P

C = 256
GROUPS = 32
LAT = 16
D = 3072
HEADS = 12
HDIM = 128
FRAMES = 16
HALF = 16
ROW = FRAMES * 2 * HALF
CELLS = 2 * ROW
SEQ = 16
CLIPS = 8
QROWS = 36
QPAD = 48
EPS = 1e-06
F32 = jnp.float32
BF16 = jnp.bfloat16
VMEM = pl.BlockSpec(memory_space=pltpu.VMEM)
SMEM = pl.BlockSpec(memory_space=pltpu.SMEM)
HBM = pl.BlockSpec(memory_space=pltpu.HBM)
DMA = pltpu.SemaphoreType.DMA


def nt_dot(a, b):
    return lax.dot_general(a, b, (((1,), (1,)), ((), ())), preferred_element_type=F32)


def dot(a, b):
    return jnp.dot(a, b, preferred_element_type=F32)


def exact_dot(rows, zero_one):
    high = rows.astype(BF16).astype(F32)
    rest = rows - high
    mid = rest.astype(BF16).astype(F32)
    low = rest - mid
    parts = jnp.concatenate([high, mid, low, jnp.zeros_like(low)], axis=0).astype(BF16)
    out = dot(parts, zero_one)
    return out[0:8] + out[8:16] + out[16:24]


def iota(shape, dim):
    return lax.broadcasted_iota(jnp.int32, shape, dim)


def one_hot(cond):
    return jnp.where(cond, 1.0, 0.0).astype(BF16)


def rows8(first, second=None):
    n = first.shape[1]
    row = iota((8, n), 0)
    out = jnp.where(row == 0, jnp.broadcast_to(first, (8, n)), 0.0)
    if second is not None:
        out = jnp.where(row == 1, jnp.broadcast_to(second, (8, n)), out)
    return out


def write_stats(mean_c, square_c, count, stats_ref):
    same = one_hot((iota((C, C), 0) >> 3) == (iota((C, C), 1) >> 3))
    mean_g = exact_dot(rows8(mean_c), same)[0:1] * (1.0 / 8)
    gap = mean_c - mean_g
    square_c = square_c + count * (gap * gap)
    lane = iota((C, 128), 1)
    pick = one_hot((iota((C, 128), 0) >> 3) == (lane & 31))
    both = exact_dot(rows8(mean_c * (1.0 / 8), square_c), pick)
    row = jnp.where(iota((1, 128), 1) < GROUPS, both[0:1], both[1:2])
    stats_ref[...] = jnp.broadcast_to(row[None], (SEQ, 1, 128))


def read_stats(stats_ref, count):
    each = stats_ref[...].reshape(SEQ, 128)
    lane = iota((1, 128), 1)
    mean = jnp.sum(each, axis=0, keepdims=True) * (1.0 / SEQ)
    off = each - mean
    between = jnp.sum(off * off, axis=0, keepdims=True) * (8.0 * count)
    within = mean * SEQ
    total = jnp.where(lane < GROUPS, between, jnp.where(lane < 2 * GROUPS, within, 0.0))
    mean = jnp.where(lane < GROUPS, mean, 0.0)
    spread = one_hot((iota((128, C), 0) & 31) == (iota((128, C), 1) >> 3))
    both = exact_dot(rows8(mean, total), spread)
    return both[0:1], lax.rsqrt(both[1:2] * (1.0 / (8.0 * count * SEQ)) + EPS)


def own_rows(place_ref, rows_ref, near_ref, far_ref):
    odd = place_ref[0] & 1
    near_ref[...] = rows_ref[pl.ds(pl.multiple_of((1 - odd) * ROW, ROW), ROW)].astype(BF16)
    far_ref[...] = rows_ref[pl.ds(pl.multiple_of(odd * ROW, ROW), ROW)].astype(BF16)


def split_kernel(
    place_ref, feat_hbm, gain_hbm, shift_hbm, scale_hbm, mod_hbm,
    rows_ref, near_ref, far_ref, stats_ref, norms_ref, mods_ref,
    feat_ref, gain_ref, shift_ref, scale_ref, mod_ref, wide, sems,
):
    sources = (feat_hbm, gain_hbm, shift_hbm, scale_hbm, mod_hbm)
    targets = (feat_ref, gain_ref, shift_ref, scale_ref, mod_ref)
    copies = [pltpu.make_async_copy(a, b, sems.at[i]) for i, (a, b) in enumerate(zip(sources, targets))]
    for copy in copies:
        copy.start()
    for copy in copies:
        copy.wait()
    norms_ref[0:3] = gain_ref[...]
    norms_ref[4:7] = shift_ref[...]
    mods_ref[0:1] = scale_ref[...]
    mods_ref[1:2] = mod_ref[...]
    cells = feat_ref[...].astype(F32).reshape(CELLS, C)
    for side in range(2):
        wide[side] = cells[:, side * 128 : (side + 1) * 128]
    for frame in range(FRAMES):
        for row in range(2):
            for parity in range(2):
                base = (frame * 2 + row) * 32 + parity
                at = row * ROW + (frame * 2 + parity) * HALF
                for side in range(2):
                    part = wide[side, pl.ds(base, HALF, stride=2)]
                    rows_ref[at : at + HALF, side * 128 : (side + 1) * 128] = part.astype(BF16)
    own_rows(place_ref, rows_ref, near_ref, far_ref)
    mean = jnp.sum(cells, axis=0, keepdims=True) * (1.0 / CELLS)
    off = cells - mean
    write_stats(mean, jnp.sum(off * off, axis=0, keepdims=True), CELLS, stats_ref)


def fill_window(place_ref, stats_ref, rows_ref, near_ref, far_ref, norms_ref, layer, window, centers=None, load=None):
    mean, rstd = read_stats(stats_ref, CELLS)
    gain = rstd * norms_ref[layer : layer + 1] * 0.5
    shift = norms_ref[4 + layer : 5 + layer] * 0.5
    place = place_ref[0]
    odd = place & 1
    near_at = 3 * (1 - odd)
    far_on = jnp.where((place > 0) & (place < SEQ - 1), 1.0, 0.0).astype(F32)
    window[:, 0:2] = jnp.zeros((4, 2, 4, HALF, C), BF16)
    step = 4
    n = step * HALF
    pair = iota((n, C), 0) & (HALF - 1)
    level = -mean
    levels = [level] * 4 if centers is None else [center + level for center in centers]
    sources = (
        (near_at, near_ref),
        (3 - near_at, far_ref),
        (1, rows_ref.at[0:ROW]),
        (2, rows_ref.at[ROW:CELLS]),
    )
    for which, (row, source) in enumerate(sources):
        if which == 2 and load is not None:
            load.wait()
        for frame in range(0, FRAMES, step):
            x = source[frame * 32 : (frame + step) * 32].astype(F32)
            half = (x + levels[which]) * gain + shift
            act = half + half * jnp.tanh(half)
            if which == 1:
                act = act * far_on
            act = act.reshape(step, 2, HALF, C)
            even = act[:, 0].reshape(n, C)
            odd_ones = act[:, 1].reshape(n, C)
            odd_before = jnp.where(pair == 0, 0.0, pltpu.roll(odd_ones, 1, 0))
            even_after = jnp.where(pair == HALF - 1, 0.0, pltpu.roll(even, n - 1, 0))
            for plane, part in enumerate((odd_before, even, odd_ones, even_after)):
                window[row, 2 + frame : 2 + frame + step, plane] = part.astype(BF16).reshape(
                    step, HALF, C
                )


TILE = 256


def start_weights(source, weight, sems):
    copies = [
        pltpu.make_async_copy(source.at[9 * p : 9 * p + 9], weight.at[9 * p : 9 * p + 9], sems.at[p])
        for p in range(3)
    ]
    for copy in copies:
        copy.start()
    return copies


def convolve(window, weight, copies, total, finish):
    for p in range(3):
        copies[p].wait()
        for tile in range(CELLS // TILE):
            row, frame = tile * TILE // ROW, tile * TILE % ROW // 32
            part = None
            for q in range(3):
                for r in range(3):
                    at = frame + p
                    cells = window[q + row, at : at + TILE // 32, r : r + 2].reshape(TILE, C)
                    term = dot(cells, weight[9 * p + 3 * q + r])
                    part = term if part is None else part + term
            rows = slice(tile * TILE, (tile + 1) * TILE)
            if p > 0:
                part = part + total[rows]
            if p < 2:
                total[rows] = part
            else:
                finish(rows, part)


class Moments:
    def __init__(self):
        self.center = self.first = self.second = None

    def add(self, tile):
        if self.center is None:
            self.center = jnp.sum(tile, axis=0, keepdims=True) * (1.0 / TILE)
        off = tile - self.center
        first = jnp.sum(off, axis=0, keepdims=True)
        second = jnp.sum(off * off, axis=0, keepdims=True)
        self.first = first if self.first is None else self.first + first
        self.second = second if self.second is None else self.second + second
        return off

    def write(self, stats_ref):
        gap = self.first * (1.0 / CELLS)
        square = jnp.maximum(self.second - self.first * gap, 0.0)
        write_stats(self.center + gap, square, CELLS, stats_ref)


def first_kernel(
    place_ref, stats_ref, rows_ref, near_ref, far_ref, norms_ref, weight_hbm,
    hidden_hbm, center_ref, near_out, far_out, stats_out, window, weight, total, hidden_ref, sems,
):
    copies = start_weights(weight_hbm, weight, sems)
    fill_window(place_ref, stats_ref, rows_ref, near_ref, far_ref, norms_ref, 0, window)
    moments = Moments()

    def finish(rows, tile):
        hidden_ref[rows] = moments.add(tile).astype(BF16)

    convolve(window, weight, copies, total, finish)
    copy = pltpu.make_async_copy(hidden_ref, hidden_hbm, sems.at[3])
    copy.start()
    center = moments.center
    center_ref[...] = jnp.broadcast_to(center, (8, C))
    high = center.astype(BF16).astype(F32)
    mid = (center - high).astype(BF16).astype(F32)
    line = iota((16, C), 0)
    terms = jnp.where(line == 0, high, jnp.where(line == 1, mid, jnp.where(line == 2, center - high - mid, 0.0)))
    own_rows(place_ref, hidden_ref, near_out.at[0:ROW], far_out.at[0:ROW])
    near_out[ROW : ROW + 16] = terms.astype(BF16)
    far_out[ROW : ROW + 16] = terms.astype(BF16)
    moments.write(stats_out)
    copy.wait()


def second_kernel(
    place_ref, stats_ref, hidden_hbm, center_ref, near_ref, far_ref, norms_ref, feat_ref, weight_hbm,
    block_ref, near_out, far_out, stats_out, window, weight, total, hidden_ref, sems,
):
    load = pltpu.make_async_copy(hidden_hbm, hidden_ref, sems.at[3])
    load.start()
    copies = start_weights(weight_hbm, weight, sems)
    own = center_ref[0:1]
    centers = [jnp.sum(ref[ROW : ROW + 16].astype(F32), axis=0, keepdims=True) for ref in (near_ref, far_ref)]
    centers += [own, own]
    fill_window(place_ref, stats_ref, hidden_ref, near_ref, far_ref, norms_ref, 1, window, centers, load)
    moments = Moments()

    def finish(rows, tile):
        block = (tile + feat_ref[rows].astype(F32)).astype(BF16)
        block_ref[rows] = block
        moments.add(block.astype(F32))

    convolve(window, weight, copies, total, finish)
    own_rows(place_ref, block_ref, near_out, far_out)
    moments.write(stats_out)


def column_to_row(column):
    square = jnp.broadcast_to(column, (128, 128))
    return jnp.sum(jnp.where(iota((128, 128), 0) == iota((128, 128), 1), square, 0.0), axis=0, keepdims=True)


def third_kernel(
    place_ref, stats_ref, rows_ref, near_ref, far_ref, norms_ref, weight_ref, embed_ref, bias_ref,
    own_ref, other_ref, patches_ref, parcel_ref, window, weight,
):
    n = FRAMES * HALF
    for p in range(3):
        for row in range(4):
            for plane in range(4):
                block = (p * 4 + row) * 4 + plane
                for dh in range(2):
                    for dw in range(2):
                        at = (2 * dh + dw) * LAT
                        q, r = row - dh, plane - dw
                        if 0 <= q < 3 and 0 <= r < 3:
                            weight[block, at : at + LAT] = weight_ref[9 * p + 3 * q + r]
                        else:
                            weight[block, at : at + LAT] = jnp.zeros((LAT, C), BF16)
    fill_window(place_ref, stats_ref, rows_ref, near_ref, far_ref, norms_ref, 2, window)
    patches = None
    for p in range(3):
        for row in range(4):
            for plane in range(4):
                cells = window[row, p : p + FRAMES, plane].reshape(n, C)
                term = nt_dot(cells, weight[(p * 4 + row) * 4 + plane])
                patches = term if patches is None else patches + term
    patches_ref[...] = patches
    rounded = patches.astype(BF16)
    embedded = dot(jnp.concatenate([rounded, rounded], axis=1), embed_ref[...]) + bias_ref[0:1]
    spread = jnp.sum(embedded * embedded, axis=1, keepdims=True) * (1.0 / D)
    rstd = lax.rsqrt(spread + EPS)
    scaled = (rounded.astype(F32) * rstd).reshape(FRAMES, 2, 8, 64)
    rstd = jnp.broadcast_to(rstd, (n, 128)).reshape(FRAMES, 2, 8, 128)
    both = jnp.concatenate([scaled[:, side].reshape(128, 64) for side in range(2)], axis=1)
    parcel_ref[0:128] = both.astype(BF16)
    line = iota((16, 128), 0)
    lines = jnp.where(line == 4, 1.0, 0.0)
    for side in range(2):
        each = column_to_row(rstd[:, side].reshape(128, 128)[:, 0:1])
        high = each.astype(BF16).astype(F32)
        lines = jnp.where(line == 2 * side, high, lines)
        lines = jnp.where(line == 2 * side + 1, each - high, lines)
    parcel_ref[128:144] = lines.astype(BF16)
    parcel_ref[144:288] = own_ref[...]
    parcel_ref[288:432] = other_ref[...]


def latent_kernel(patches_ref, latent_ref):
    n = FRAMES * HALF
    patches = patches_ref[...]
    turned = jnp.transpose(jnp.concatenate([patches, jnp.zeros_like(patches)], axis=1))
    out = None
    for dw in range(2):
        rows = jnp.concatenate([turned[(2 * dh + dw) * LAT : (2 * dh + dw + 1) * LAT] for dh in range(2)], axis=0)
        high = rows.astype(BF16).astype(F32)
        mid = (rows - high).astype(BF16).astype(F32)
        parts = jnp.concatenate([high, mid, rows - high - mid], axis=0).astype(BF16)
        column = iota((n, 2 * n), 1)
        spread = one_hot(column == iota((n, 2 * n), 0) * 2 + dw)
        term = dot(parts, spread)
        term = term[0:32] + term[32:64] + term[64:96]
        out = term if out is None else out + term
    for frame in range(FRAMES):
        for dh in range(2):
            latent_ref[frame, dh] = out[dh * LAT : (dh + 1) * LAT, frame * 32 : (frame + 1) * 32]


def embed_kernel(embed_ref, bias_ref, embed_out, bias_out):
    embed = embed_ref[...].astype(F32)
    embed = embed - jnp.mean(embed, axis=1, keepdims=True)
    high = embed.astype(BF16)
    embed_out[0:64] = high
    embed_out[64:128] = (embed - high.astype(F32)).astype(BF16)
    bias = bias_ref[...]
    bias_out[...] = jnp.broadcast_to(bias - jnp.mean(bias, axis=1, keepdims=True), (8, D))


def fold_kernel(
    here_ref, there_ref, embed_ref, bias_ref, own_mods_ref, mods_ref, own_ref, other_ref, stacked, wide,
):
    for i in range(4):
        stacked[i * QPAD : i * QPAD + QROWS] = (here_ref, there_ref)[i >> 1][i & 1]
        stacked[i * QPAD + QROWS : (i + 1) * QPAD] = jnp.zeros((QPAD - QROWS, D), BF16)
    embed = embed_ref[0:64].astype(F32) + embed_ref[64:128].astype(F32)
    row = iota((64, D), 0)
    sides = []
    for mod_ref in (own_mods_ref, mods_ref):
        scale, shift = 1.0 + mod_ref[0:1], mod_ref[1:2]
        bias = bias_ref[0:1] * scale
        bias_high = bias.astype(BF16).astype(F32)
        shift_high = shift.astype(BF16).astype(F32)
        ends = jnp.where(row == 0, bias_high, jnp.where(row == 1, bias - bias_high, 0.0))
        ends = jnp.where(row == 2, shift_high, jnp.where(row == 3, shift - shift_high, ends))
        sides += [embed * scale, ends]
    every = jnp.concatenate(sides, axis=0).astype(BF16)
    out = nt_dot(stacked[...], every)
    lane = iota((4 * QPAD, 128), 1)
    for side, target in enumerate((own_ref, other_ref)):
        part = out[:, side * 128 : (side + 1) * 128]
        bias = part[:, 64:65] + part[:, 65:66]
        shift = part[:, 66:67] + part[:, 67:68]
        bias_high = bias.astype(BF16).astype(F32)
        shift_high = shift.astype(BF16).astype(F32)
        part = jnp.where((lane == 64) | (lane == 68), bias_high, part)
        part = jnp.where(lane == 65, bias - bias_high, part)
        part = jnp.where(lane == 66, shift_high, part)
        part = jnp.where(lane == 67, shift - shift_high, part)
        for i in range(4):
            wide[i * QROWS : (i + 1) * QROWS] = part[i * QPAD : i * QPAD + QROWS]
        target[...] = wide[...].astype(BF16)


WIDE = HEADS * HDIM


def sort_kernel(place_ref, clip_ref, near_ref, far_ref, asks_ref, keys_ref, values_ref, loose, wide):
    seq, clip = place_ref[0], clip_ref[0]
    for j in range(SEQ):
        source = (near_ref, far_ref)[j & 1]
        loose[j] = source[(j >> 1) & 3, j >> 3, 144:432].astype(F32)
        for k in range(CLIPS):
            at = ((clip ^ (2 * (k & 3) + (k >> 2))) * SEQ + (seq ^ j)) * QROWS
            wide[pl.ds(at, QROWS)] = loose[j, k * QROWS : (k + 1) * QROWS]
    lane = iota((WIDE, 128), 1)
    rows = wide[0:WIDE]
    asks_ref[:, 0:128] = rows.astype(BF16)
    asks_ref[:, 128:256] = pltpu.roll(rows, 64, 1).astype(BF16)
    for part, target in ((1, keys_ref), (2, values_ref)):
        rows = wide[part * WIDE : (part + 1) * WIDE]
        bias = rows[:, 64:65] + rows[:, 65:66]
        shift = rows[:, 66:67] + rows[:, 67:68]
        left = jnp.where(lane < 64, rows, 0.0)
        target[:, 0:128] = left.astype(BF16)
        target[:, 256:384] = pltpu.roll(left, 64, 1).astype(BF16)
        for side in range(2):
            extra = jnp.where((lane == 2 * side) | (lane == 2 * side + 1), bias, 0.0)
            extra = jnp.where(lane == 4, shift, extra)
            target[:, 256 * side + 128 : 256 * side + 256] = extra.astype(BF16)


def attend_kernel(place_ref, near_ref, far_ref, asks_ref, keys_ref, values_ref, out_ref, queries, mixed, scores, weights):
    seq = place_ref[0]
    blocks = [(near_ref, far_ref)[j & 1].at[(j >> 1) & 3, j >> 3] for j in range(SEQ)]
    lane = iota((128, 128), 1)
    pick = one_hot(iota((8, 128), 1) == iota((8, 128), 0) + seq * 8)
    twin = pl.ds(pl.multiple_of((seq >> 1) * 16, 16), 16)
    tokens, scales = [], []
    for block in blocks:
        pair = block[twin].astype(F32)
        tokens.append(jnp.where((seq & 1) == 1, pair[8:16], pair[0:8]))
        scales.append(nt_dot(pick, block[128:144]))
    tokens = jnp.concatenate(tokens, axis=0)
    scales = jnp.concatenate(scales, axis=0)
    asked = []
    for side in range(2):
        high, low = scales[:, 2 * side : 2 * side + 1], scales[:, 2 * side + 1 : 2 * side + 2]
        spot = lane - 64 * (1 - side)
        own = jnp.where((lane >> 6) == side, tokens, 0.0)
        own = jnp.where((spot == 0) | (spot == 1), high, own)
        own = jnp.where((spot == 2) | (spot == 3), 1.0, own)
        own = jnp.where(spot == 4, low, own).astype(BF16)
        asked.append((nt_dot(own, asks_ref[:, 128 * side : 128 * side + 128]) * (1.0 / math.sqrt(HDIM))).astype(BF16))
    for head in range(HEADS):
        cols = slice(head * HDIM, (head + 1) * HDIM)
        keyed = [
            dot(asked[side][:, cols], keys_ref[cols, 256 * side : 256 * side + 256]).reshape(SEQ, 8, 256)
            for side in range(2)
        ]
        queries[:, head] = jnp.concatenate(keyed, axis=1).astype(BF16)
    n = HEADS * HALF
    same = jnp.where(iota((8, n), 0) == (iota((8, n), 1) & 7), 1.0, 0.0)
    for j, block in enumerate(blocks):
        query = queries[j].reshape(n, 256)
        ends = lax.dot_general(block[128:144], query[:, 128:144], (((0,), (1,)), ((), ())), preferred_element_type=F32)
        scores[j] = nt_dot(block[0:128], query[:, 0:128]) + ends
    for j in range(SEQ):
        each = scores[j].reshape(FRAMES, 8, n)
        raised = jnp.exp(each - jnp.max(each, axis=0, keepdims=True))
        shares = raised * (same / jnp.sum(raised, axis=0))
        weights[j] = jnp.transpose(shares.astype(BF16).reshape(128, n))
    for j, block in enumerate(blocks):
        mix = dot(weights[j], block[0:128]).reshape(HEADS, 2, 8, 128)
        ends = nt_dot(weights[j], block[128:144]).reshape(HEADS, 2, 8, 16)
        for side in range(2):
            mixed[side, :, j * 8 : (j + 1) * 8, 0:128] = mix[:, side]
            mixed[side, :, j * 8 : (j + 1) * 8, 128:144] = ends[:, side]
    for head in range(HEADS):
        cols = slice(head * HDIM, (head + 1) * HDIM)
        out = []
        for side in range(2):
            part = nt_dot(mixed[side, head, :, 0:128].astype(BF16), values_ref[cols, 256 * side : 256 * side + 128])
            at = 256 * side + 128
            part = part + nt_dot(mixed[side, head, :, 128:144].astype(BF16), values_ref[cols, at : at + 16])
            out.append(part.reshape(SEQ, 8, HDIM))
        out = jnp.concatenate(out, axis=1).astype(BF16)
        for j in range(SEQ):
            out_ref[pl.ds(pl.multiple_of((seq ^ j) * HALF, HALF), HALF), cols] = out[j]


def shape(*dims, dtype=BF16):
    return jax.ShapeDtypeStruct(dims, dtype)


def call(body, outs, ins, scratch=(), flops=0, moved=0, limit=32, first_out=VMEM):
    outs = list(outs) if isinstance(outs, list) else outs
    if first_out is HBM:
        outs[0] = pltpu.HBM(outs[0].shape, outs[0].dtype)
    kernel = pl.pallas_call(
        body,
        out_shape=outs,
        in_specs=ins,
        out_specs=[first_out] + [VMEM] * (len(outs) - 1) if isinstance(outs, list) else VMEM,
        scratch_shapes=list(scratch),
        compiler_params=pltpu.CompilerParams(vmem_limit_bytes=limit << 20),
        cost_estimate=pl.CostEstimate(flops=flops, bytes_accessed=moved, transcendentals=0),
        name=body.__name__,
    )

    def run(*args):
        return kernel(
            *(pltpu.with_memory_space_constraint(x, pltpu.HBM) if spec is HBM else x for x, spec in zip(args, ins))
        )

    return run


def swap(values, axis, bits, count):
    return lax.ppermute(values, axis, [(i, i ^ bits) for i in range(count)])


CHIP_PAIRS = [(i, i ^ 1) for i in range(SEQ)]
NEXT_PAIRS = [(i, (i + 1 if i & 1 else i - 1) % SEQ) for i in range(SEQ)]


def neighbours(near, far):
    far = lax.ppermute(far, "seq", NEXT_PAIRS)
    return lax.ppermute(near, "seq", CHIP_PAIRS), far


def exchange(stats):
    return lax.all_to_all(stats, "seq", 0, 0, tiled=True)


def gather_seq(block, beside):
    over = swap(block, "seq", 8, SEQ)
    over, beside = lax.optimization_barrier((over, beside))
    pair = jnp.stack([block, over])
    near = jnp.stack([pair] + [swap(pair, "seq", bits, SEQ) for bits in (2, 4, 6)])
    return near, swap(near, "seq", 1, SEQ), beside


WINDOW = pltpu.VMEM((4, FRAMES + 2, 4, HALF, C), BF16)
WEIGHT = pltpu.VMEM((27, C, C), BF16)
CONV_FLOPS = 2 * CELLS * 27 * C * C


def shards(
    features,
    first_conv,
    second_conv,
    out_conv,
    norm_gains,
    norm_shifts,
    embed_weight,
    embed_bias,
    mod_shift,
    mod_scale,
    qkv_weight,
):
    place = lax.axis_index("seq").astype(jnp.int32).reshape(1)
    clip = lax.axis_index("clip").astype(jnp.int32).reshape(1)
    row = shape(ROW, C)
    stats = shape(SEQ, 1, 128, dtype=F32)
    taps = 27

    beside = swap(qkv_weight, "clip", 2, CLIPS)
    cells = shape(CELLS, C)
    long_row = shape(ROW + 16, C)
    rows_f, near, far, stats0, norms, own_mods = call(
        split_kernel,
        [cells, row, row, stats, shape(8, C, dtype=F32), shape(2, D, dtype=F32)],
        [SMEM] + [HBM] * 5,
        [
            pltpu.VMEM((FRAMES, 2, 32, C), BF16),
            pltpu.VMEM((3, C), F32),
            pltpu.VMEM((3, C), F32),
            pltpu.VMEM((1, D), F32),
            pltpu.VMEM((1, D), F32),
            pltpu.VMEM((2, CELLS, 128), F32),
            DMA((5,)),
        ],
        0,
        1 << 20,
    )(place, features.reshape(FRAMES, 2, 32, C), norm_gains, norm_shifts, mod_scale, mod_shift)
    near, far = neighbours(near, far)
    mods = swap(own_mods, "clip", 1, CLIPS)
    stats0 = exchange(stats0)
    stats0, mods, beside = lax.optimization_barrier((stats0, mods, beside))
    here = jnp.stack([qkv_weight, beside])
    there = swap(here, "clip", 4, CLIPS)
    hidden, center, near_h, far_h, stats1 = call(
        first_kernel,
        [cells, shape(8, C, dtype=F32), long_row, long_row, stats],
        [SMEM] + [VMEM] * 5 + [HBM],
        [WINDOW, WEIGHT, pltpu.VMEM((CELLS, C), F32), pltpu.VMEM((CELLS, C), BF16), DMA((4,))],
        CONV_FLOPS,
        5 << 20,
        first_out=HBM,
    )(place, stats0, rows_f, near, far, norms, first_conv.reshape(taps, C, C))
    near, far = neighbours(near_h, far_h)

    embed, bias = call(embed_kernel, [shape(128, D), shape(8, D, dtype=F32)], [VMEM] * 2)(
        embed_weight, embed_bias.reshape(1, D)
    )
    folded = shape(4 * QROWS, 128)
    own, other = call(
        fold_kernel,
        [folded, folded],
        [VMEM] * 6,
        [pltpu.VMEM((4 * QPAD, D), BF16), pltpu.VMEM((4 * QROWS, 128), F32)],
    )(here, there, embed, bias, own_mods, mods)
    stats1 = exchange(stats1)
    stats1, own, other = lax.optimization_barrier((stats1, own, other))
    other = swap(other, "clip", 1, CLIPS)

    block, near_b, far_b, stats2 = call(
        second_kernel,
        [cells, row, row, stats],
        [SMEM, VMEM, HBM] + [VMEM] * 5 + [HBM],
        [WINDOW, WEIGHT, pltpu.VMEM((CELLS, C), F32), pltpu.VMEM((CELLS, C), BF16), DMA((4,))],
        CONV_FLOPS,
        6 << 20,
    )(place, stats1, hidden, center, near, far, norms, rows_f, second_conv.reshape(taps, C, C))
    near, far = neighbours(near_b, far_b)
    stats2 = exchange(stats2)
    patches, parcel = call(
        third_kernel,
        [shape(FRAMES * HALF, 4 * LAT, dtype=F32), shape(432, 128)],
        [SMEM] + [VMEM] * 10,
        [WINDOW, pltpu.VMEM((48, 4 * LAT, C), BF16)],
        CONV_FLOPS // 2,
        4 << 20,
    )(
        place, stats2, block, near, far, norms,
        out_conv.transpose(0, 1, 2, 4, 3).reshape(taps, LAT, C), embed, bias, own, other,
    )
    latent = call(latent_kernel, shape(FRAMES, 2, LAT, 2 * HALF, dtype=F32), [VMEM])(patches)
    near, far, latent = gather_seq(parcel, latent)
    asks, keys, values = call(
        sort_kernel,
        [shape(WIDE, 256), shape(WIDE, 512), shape(WIDE, 512)],
        [SMEM] * 2 + [VMEM] * 2,
        [pltpu.VMEM((SEQ, 8 * QROWS, 128), F32), pltpu.VMEM((3 * WIDE, 128), F32)],
    )(place, clip, near, far)
    frame_heads = call(
        attend_kernel,
        shape(SEQ * HALF, WIDE),
        [SMEM] + [VMEM] * 5,
        [
            pltpu.VMEM((SEQ, HEADS, HALF, 256), BF16),
            pltpu.VMEM((2, HEADS, 128, 256), F32),
            pltpu.VMEM((SEQ, 128, HEADS * HALF), F32),
            pltpu.VMEM((SEQ, HEADS * HALF, 128), BF16),
        ],
    )(place, near, far, asks, keys, values)
    latent = latent.transpose(0, 1, 3, 2).reshape(1, FRAMES, 2, 2 * HALF, LAT)
    return (latent, frame_heads.reshape(1, 1, SEQ * HALF, WIDE))


def solution(mesh):
    placed = (
        P("clip", None, "seq", None, None),
        P(),
        P(),
        P(),
        P(),
        P(),
        P(),
        P(),
        P("clip", None),
        P("clip", None),
        P(("clip", "seq"), None),
    )
    return jax.shard_map(
        shards,
        mesh=mesh,
        in_specs=placed,
        out_specs=(P("clip", None, "seq", None, None), P("clip", "seq", None, None)),
        check_vma=False,
    )
```

```python
import functools
import math

import jax
import jax.numpy as jnp
from jax import lax
from jax.experimental import pallas as pl
from jax.experimental.pallas import tpu as pltpu
from jax.sharding import PartitionSpec as P

C = 256
GROUPS = 32
LAT = 16
D = 3072
HEADS = 12
HDIM = 128
FRAMES = 16
HALF = 16
ROW = FRAMES * 2 * HALF
CELLS = 2 * ROW
SEQ = 16
CLIPS = 8
QROWS = 36
QPAD = 48
EPS = 1e-06
F32 = jnp.float32
BF16 = jnp.bfloat16
VMEM = pl.BlockSpec(memory_space=pltpu.VMEM)
SMEM = pl.BlockSpec(memory_space=pltpu.SMEM)
HBM = pl.BlockSpec(memory_space=pltpu.HBM)
DMA = pltpu.SemaphoreType.DMA


def nt_dot(a, b):
    return lax.dot_general(a, b, (((1,), (1,)), ((), ())), preferred_element_type=F32)


def dot(a, b):
    return jnp.dot(a, b, preferred_element_type=F32)


def exact_dot(rows, zero_one):
    high = rows.astype(BF16).astype(F32)
    rest = rows - high
    mid = rest.astype(BF16).astype(F32)
    low = rest - mid
    parts = jnp.concatenate([high, mid, low, jnp.zeros_like(low)], axis=0).astype(BF16)
    out = dot(parts, zero_one)
    return out[0:8] + out[8:16] + out[16:24]


def iota(shape, dim):
    return lax.broadcasted_iota(jnp.int32, shape, dim)


def one_hot(cond):
    return jnp.where(cond, 1.0, 0.0).astype(BF16)


def rows8(first, second=None):
    n = first.shape[1]
    row = iota((8, n), 0)
    out = jnp.where(row == 0, jnp.broadcast_to(first, (8, n)), 0.0)
    if second is not None:
        out = jnp.where(row == 1, jnp.broadcast_to(second, (8, n)), out)
    return out


def write_stats(mean_c, square_c, count, stats_ref):
    same = one_hot((iota((C, C), 0) >> 3) == (iota((C, C), 1) >> 3))
    mean_g = exact_dot(rows8(mean_c), same)[0:1] * (1.0 / 8)
    gap = mean_c - mean_g
    square_c = square_c + count * (gap * gap)
    lane = iota((C, 128), 1)
    pick = one_hot((iota((C, 128), 0) >> 3) == (lane & 31))
    both = exact_dot(rows8(mean_c * (1.0 / 8), square_c), pick)
    row = jnp.where(iota((1, 128), 1) < GROUPS, both[0:1], both[1:2])
    stats_ref[...] = jnp.broadcast_to(row[None], (SEQ, 1, 128))


def read_stats(stats_ref, count):
    each = stats_ref[...].reshape(SEQ, 128)
    lane = iota((1, 128), 1)
    mean = jnp.sum(each, axis=0, keepdims=True) * (1.0 / SEQ)
    off = each - mean
    between = jnp.sum(off * off, axis=0, keepdims=True) * (8.0 * count)
    within = mean * SEQ
    total = jnp.where(lane < GROUPS, between, jnp.where(lane < 2 * GROUPS, within, 0.0))
    mean = jnp.where(lane < GROUPS, mean, 0.0)
    spread = one_hot((iota((128, C), 0) & 31) == (iota((128, C), 1) >> 3))
    both = exact_dot(rows8(mean, total), spread)
    return both[0:1], lax.rsqrt(both[1:2] * (1.0 / (8.0 * count * SEQ)) + EPS)


def own_rows(place_ref, rows_ref, near_ref, far_ref):
    odd = place_ref[0] & 1
    near_ref[...] = rows_ref[pl.ds(pl.multiple_of((1 - odd) * ROW, ROW), ROW)].astype(BF16)
    far_ref[...] = rows_ref[pl.ds(pl.multiple_of(odd * ROW, ROW), ROW)].astype(BF16)


def split_kernel(
    place_ref, feat_hbm, gain_hbm, shift_hbm, scale_hbm, mod_hbm,
    rows_ref, near_ref, far_ref, stats_ref, norms_ref, mods_ref,
    feat_ref, gain_ref, shift_ref, scale_ref, mod_ref, wide, sems,
):
    sources = (feat_hbm, gain_hbm, shift_hbm, scale_hbm, mod_hbm)
    targets = (feat_ref, gain_ref, shift_ref, scale_ref, mod_ref)
    copies = [pltpu.make_async_copy(a, b, sems.at[i]) for i, (a, b) in enumerate(zip(sources, targets))]
    for copy in copies:
        copy.start()
    for copy in copies:
        copy.wait()
    norms_ref[0:3] = gain_ref[...]
    norms_ref[4:7] = shift_ref[...]
    mods_ref[0:1] = scale_ref[...]
    mods_ref[1:2] = mod_ref[...]
    cells = feat_ref[...].astype(F32).reshape(CELLS, C)
    for side in range(2):
        wide[side] = cells[:, side * 128 : (side + 1) * 128]
    for frame in range(FRAMES):
        for row in range(2):
            for parity in range(2):
                base = (frame * 2 + row) * 32 + parity
                at = row * ROW + (frame * 2 + parity) * HALF
                for side in range(2):
                    part = wide[side, pl.ds(base, HALF, stride=2)]
                    rows_ref[at : at + HALF, side * 128 : (side + 1) * 128] = part.astype(BF16)
    own_rows(place_ref, rows_ref, near_ref, far_ref)
    mean = jnp.sum(cells, axis=0, keepdims=True) * (1.0 / CELLS)
    off = cells - mean
    write_stats(mean, jnp.sum(off * off, axis=0, keepdims=True), CELLS, stats_ref)


def fill_window(place_ref, stats_ref, rows_ref, near_ref, far_ref, norms_ref, layer, window, centers=None, load=None):
    mean, rstd = read_stats(stats_ref, CELLS)
    gain = rstd * norms_ref[layer : layer + 1] * 0.5
    shift = norms_ref[4 + layer : 5 + layer] * 0.5
    place = place_ref[0]
    odd = place & 1
    near_at = 3 * (1 - odd)
    far_on = jnp.where((place > 0) & (place < SEQ - 1), 1.0, 0.0).astype(F32)
    window[:, 0:2] = jnp.zeros((4, 2, 4, HALF, C), BF16)
    step = 4
    n = step * HALF
    pair = iota((n, C), 0) & (HALF - 1)
    level = -mean
    levels = [level] * 4 if centers is None else [center + level for center in centers]
    sources = (
        (near_at, near_ref),
        (3 - near_at, far_ref),
        (1, rows_ref.at[0:ROW]),
        (2, rows_ref.at[ROW:CELLS]),
    )
    for which, (row, source) in enumerate(sources):
        if which == 2 and load is not None:
            load.wait()
        for frame in range(0, FRAMES, step):
            x = source[frame * 32 : (frame + step) * 32].astype(F32)
            half = (x + levels[which]) * gain + shift
            act = half + half * jnp.tanh(half)
            if which == 1:
                act = act * far_on
            act = act.reshape(step, 2, HALF, C)
            even = act[:, 0].reshape(n, C)
            odd_ones = act[:, 1].reshape(n, C)
            odd_before = jnp.where(pair == 0, 0.0, pltpu.roll(odd_ones, 1, 0))
            even_after = jnp.where(pair == HALF - 1, 0.0, pltpu.roll(even, n - 1, 0))
            for plane, part in enumerate((odd_before, even, odd_ones, even_after)):
                window[row, 2 + frame : 2 + frame + step, plane] = part.astype(BF16).reshape(
                    step, HALF, C
                )


TILE = 256


def start_weights(source, weight, sems):
    copies = [
        pltpu.make_async_copy(source.at[9 * p : 9 * p + 9], weight.at[9 * p : 9 * p + 9], sems.at[p])
        for p in range(3)
    ]
    for copy in copies:
        copy.start()
    return copies


def convolve(window, weight, copies, total, finish):
    for p in range(3):
        copies[p].wait()
        for tile in range(CELLS // TILE):
            row, frame = tile * TILE // ROW, tile * TILE % ROW // 32
            part = None
            for q in range(3):
                for r in range(3):
                    at = frame + p
                    cells = window[q + row, at : at + TILE // 32, r : r + 2].reshape(TILE, C)
                    term = dot(cells, weight[9 * p + 3 * q + r])
                    part = term if part is None else part + term
            rows = slice(tile * TILE, (tile + 1) * TILE)
            if p > 0:
                part = part + total[rows]
            if p < 2:
                total[rows] = part
            else:
                finish(rows, part)


class Moments:
    def __init__(self):
        self.center = self.first = self.second = None

    def add(self, tile):
        if self.center is None:
            self.center = jnp.sum(tile, axis=0, keepdims=True) * (1.0 / TILE)
        off = tile - self.center
        first = jnp.sum(off, axis=0, keepdims=True)
        second = jnp.sum(off * off, axis=0, keepdims=True)
        self.first = first if self.first is None else self.first + first
        self.second = second if self.second is None else self.second + second
        return off

    def write(self, stats_ref):
        gap = self.first * (1.0 / CELLS)
        square = jnp.maximum(self.second - self.first * gap, 0.0)
        write_stats(self.center + gap, square, CELLS, stats_ref)


def first_kernel(
    place_ref, stats_ref, rows_ref, near_ref, far_ref, norms_ref, weight_hbm,
    hidden_hbm, center_ref, near_out, far_out, stats_out, window, weight, total, hidden_ref, sems,
):
    copies = start_weights(weight_hbm, weight, sems)
    fill_window(place_ref, stats_ref, rows_ref, near_ref, far_ref, norms_ref, 0, window)
    moments = Moments()

    def finish(rows, tile):
        hidden_ref[rows] = moments.add(tile).astype(BF16)

    convolve(window, weight, copies, total, finish)
    copy = pltpu.make_async_copy(hidden_ref, hidden_hbm, sems.at[3])
    copy.start()
    center = moments.center
    center_ref[...] = jnp.broadcast_to(center, (8, C))
    high = center.astype(BF16).astype(F32)
    mid = (center - high).astype(BF16).astype(F32)
    line = iota((16, C), 0)
    terms = jnp.where(line == 0, high, jnp.where(line == 1, mid, jnp.where(line == 2, center - high - mid, 0.0)))
    own_rows(place_ref, hidden_ref, near_out.at[0:ROW], far_out.at[0:ROW])
    near_out[ROW : ROW + 16] = terms.astype(BF16)
    far_out[ROW : ROW + 16] = terms.astype(BF16)
    moments.write(stats_out)
    copy.wait()


def second_kernel(
    place_ref, stats_ref, hidden_hbm, center_ref, near_ref, far_ref, norms_ref, feat_ref, weight_hbm,
    block_ref, near_out, far_out, stats_out, window, weight, total, hidden_ref, sems,
):
    load = pltpu.make_async_copy(hidden_hbm, hidden_ref, sems.at[3])
    load.start()
    copies = start_weights(weight_hbm, weight, sems)
    own = center_ref[0:1]
    centers = [jnp.sum(ref[ROW : ROW + 16].astype(F32), axis=0, keepdims=True) for ref in (near_ref, far_ref)]
    centers += [own, own]
    fill_window(place_ref, stats_ref, hidden_ref, near_ref, far_ref, norms_ref, 1, window, centers, load)
    moments = Moments()

    def finish(rows, tile):
        block = (tile + feat_ref[rows].astype(F32)).astype(BF16)
        block_ref[rows] = block
        moments.add(block.astype(F32))

    convolve(window, weight, copies, total, finish)
    own_rows(place_ref, block_ref, near_out, far_out)
    moments.write(stats_out)


def column_to_row(column):
    square = jnp.broadcast_to(column, (128, 128))
    return jnp.sum(jnp.where(iota((128, 128), 0) == iota((128, 128), 1), square, 0.0), axis=0, keepdims=True)


def third_kernel(
    place_ref, stats_ref, rows_ref, near_ref, far_ref, norms_ref, weight_ref, embed_ref, bias_ref,
    own_ref, other_ref, patches_ref, parcel_ref, window, weight, folds,
):
    n = FRAMES * HALF
    for p in range(3):
        for row in range(4):
            for plane in range(4):
                block = (p * 4 + row) * 4 + plane
                for dh in range(2):
                    for dw in range(2):
                        at = (2 * dh + dw) * LAT
                        q, r = row - dh, plane - dw
                        if 0 <= q < 3 and 0 <= r < 3:
                            weight[block, at : at + LAT] = weight_ref[9 * p + 3 * q + r]
                        else:
                            weight[block, at : at + LAT] = jnp.zeros((LAT, C), BF16)
    fill_window(place_ref, stats_ref, rows_ref, near_ref, far_ref, norms_ref, 2, window)
    patches = None
    for p in range(3):
        for row in range(4):
            for plane in range(4):
                cells = window[row, p : p + FRAMES, plane].reshape(n, C)
                term = nt_dot(cells, weight[(p * 4 + row) * 4 + plane])
                patches = term if patches is None else patches + term
    patches_ref[...] = patches
    rounded = patches.astype(BF16)
    embedded = dot(jnp.concatenate([rounded, rounded], axis=1), embed_ref[...]) + bias_ref[0:1]
    spread = jnp.sum(embedded * embedded, axis=1, keepdims=True) * (1.0 / D)
    rstd = lax.rsqrt(spread + EPS)
    scaled = (rounded.astype(F32) * rstd).reshape(FRAMES, 2, 8, 64)
    rstd = jnp.broadcast_to(rstd, (n, 128)).reshape(FRAMES, 2, 8, 128)
    both = jnp.concatenate([scaled[:, side].reshape(128, 64) for side in range(2)], axis=1)
    parcel_ref[0:128] = both.astype(BF16)
    line = iota((16, 128), 0)
    lines = jnp.where(line == 4, 1.0, 0.0)
    for side in range(2):
        each = column_to_row(rstd[:, side].reshape(128, 128)[:, 0:1])
        high = each.astype(BF16).astype(F32)
        lines = jnp.where(line == 2 * side, high, lines)
        lines = jnp.where(line == 2 * side + 1, each - high, lines)
    parcel_ref[128:144] = lines.astype(BF16)
    own, other = own_ref[...].astype(F32), other_ref[...].astype(F32)
    lane = iota((4 * QROWS, 128), 1)
    parcel_ref[144:288] = jnp.where(lane < 64, own, pltpu.roll(other, 64, 1)).astype(BF16)
    folds[0 : 4 * QROWS] = own
    folds[4 * QROWS : 8 * QROWS] = other
    folds[8 * QROWS :] = jnp.zeros((8, 128), F32)
    lane = iota((40, 128), 1)
    ends = jnp.zeros((40, 128), F32)
    for i in range(8):
        ends = jnp.where((lane >> 3) == i, pltpu.roll(folds[i * QROWS : i * QROWS + 40], (8 * i + 64) % 128, 1), ends)
    parcel_ref[288:336] = jnp.concatenate([ends, jnp.zeros((8, 128), F32)], axis=0).astype(BF16)


def latent_kernel(patches_ref, latent_ref):
    n = FRAMES * HALF
    patches = patches_ref[...]
    turned = jnp.transpose(jnp.concatenate([patches, jnp.zeros_like(patches)], axis=1))
    out = None
    for dw in range(2):
        rows = jnp.concatenate([turned[(2 * dh + dw) * LAT : (2 * dh + dw + 1) * LAT] for dh in range(2)], axis=0)
        high = rows.astype(BF16).astype(F32)
        mid = (rows - high).astype(BF16).astype(F32)
        parts = jnp.concatenate([high, mid, rows - high - mid], axis=0).astype(BF16)
        column = iota((n, 2 * n), 1)
        spread = one_hot(column == iota((n, 2 * n), 0) * 2 + dw)
        term = dot(parts, spread)
        term = term[0:32] + term[32:64] + term[64:96]
        out = term if out is None else out + term
    for frame in range(FRAMES):
        for dh in range(2):
            latent_ref[frame, dh] = out[dh * LAT : (dh + 1) * LAT, frame * 32 : (frame + 1) * 32]


def embed_kernel(embed_ref, bias_ref, embed_out, bias_out):
    embed = embed_ref[...].astype(F32)
    embed = embed - jnp.mean(embed, axis=1, keepdims=True)
    high = embed.astype(BF16)
    embed_out[0:64] = high
    embed_out[64:128] = (embed - high.astype(F32)).astype(BF16)
    bias = bias_ref[...]
    bias_out[...] = jnp.broadcast_to(bias - jnp.mean(bias, axis=1, keepdims=True), (8, D))


def fold_kernel(
    here_ref, there_ref, embed_ref, bias_ref, own_mods_ref, mods_ref, own_ref, other_ref, stacked, wide,
):
    for i in range(4):
        stacked[i * QPAD : i * QPAD + QROWS] = (here_ref, there_ref)[i >> 1][i & 1]
        stacked[i * QPAD + QROWS : (i + 1) * QPAD] = jnp.zeros((QPAD - QROWS, D), BF16)
    embed = embed_ref[0:64].astype(F32) + embed_ref[64:128].astype(F32)
    row = iota((64, D), 0)
    sides = []
    for mod_ref in (own_mods_ref, mods_ref):
        scale, shift = 1.0 + mod_ref[0:1], mod_ref[1:2]
        bias = bias_ref[0:1] * scale
        bias_high = bias.astype(BF16).astype(F32)
        shift_high = shift.astype(BF16).astype(F32)
        ends = jnp.where(row == 0, bias_high, jnp.where(row == 1, bias - bias_high, 0.0))
        ends = jnp.where(row == 2, shift_high, jnp.where(row == 3, shift - shift_high, ends))
        sides += [embed * scale, ends]
    every = jnp.concatenate(sides, axis=0).astype(BF16)
    out = nt_dot(stacked[...], every)
    lane = iota((4 * QPAD, 128), 1)
    for side, target in enumerate((own_ref, other_ref)):
        part = out[:, side * 128 : (side + 1) * 128]
        bias = part[:, 64:65] + part[:, 65:66]
        shift = part[:, 66:67] + part[:, 67:68]
        bias_high = bias.astype(BF16).astype(F32)
        shift_high = shift.astype(BF16).astype(F32)
        part = jnp.where((lane == 64) | (lane == 68), bias_high, part)
        part = jnp.where(lane == 65, bias - bias_high, part)
        part = jnp.where(lane == 66, shift_high, part)
        part = jnp.where(lane == 67, shift - shift_high, part)
        for i in range(4):
            wide[i * QROWS : (i + 1) * QROWS] = part[i * QPAD : i * QPAD + QROWS]
        target[...] = wide[...].astype(BF16)


WIDE = HEADS * HDIM


def sort_kernel(place_ref, clip_ref, near_ref, far_ref, asks_ref, keys_ref, values_ref, loose, wide):
    seq, clip = place_ref[0], clip_ref[0]
    spot = iota((40, 128), 1)
    for j in range(SEQ):
        source = (near_ref, far_ref)[j & 1]
        loose[j] = source[(j >> 1) & 3, j >> 3, 144:336].astype(F32)
        for k in range(CLIPS):
            at = ((clip ^ (2 * (k & 3) + (k >> 2))) * SEQ + (seq ^ j)) * QROWS
            block = loose[j, (k & 3) * QROWS : (k & 3) * QROWS + 40]
            block = pltpu.roll(block, 64, 1) if k >> 2 else block
            ends = pltpu.roll(loose[j, 144:184], (64 - 8 * k) % 128, 1)
            block = jnp.where(spot < 64, block, jnp.where(spot < 69, ends, 0.0))
            wide[pl.ds(at, QROWS)] = block[:QROWS]
    lane = iota((WIDE, 128), 1)
    rows = wide[0:WIDE]
    asks_ref[:, 0:128] = rows.astype(BF16)
    asks_ref[:, 128:256] = pltpu.roll(rows, 64, 1).astype(BF16)
    for part, target in ((1, keys_ref), (2, values_ref)):
        rows = wide[part * WIDE : (part + 1) * WIDE]
        bias = rows[:, 64:65] + rows[:, 65:66]
        shift = rows[:, 66:67] + rows[:, 67:68]
        left = jnp.where(lane < 64, rows, 0.0)
        target[:, 0:128] = left.astype(BF16)
        target[:, 256:384] = pltpu.roll(left, 64, 1).astype(BF16)
        for side in range(2):
            extra = jnp.where((lane == 2 * side) | (lane == 2 * side + 1), bias, 0.0)
            extra = jnp.where(lane == 4, shift, extra)
            target[:, 256 * side + 128 : 256 * side + 256] = extra.astype(BF16)


def attend_kernel(place_ref, near_ref, far_ref, asks_ref, keys_ref, values_ref, out_ref, queries, mixed, scores, weights):
    seq = place_ref[0]
    blocks = [(near_ref, far_ref)[j & 1].at[(j >> 1) & 3, j >> 3] for j in range(SEQ)]
    lane = iota((128, 128), 1)
    pick = one_hot(iota((8, 128), 1) == iota((8, 128), 0) + seq * 8)
    twin = pl.ds(pl.multiple_of((seq >> 1) * 16, 16), 16)
    tokens, scales = [], []
    for block in blocks:
        pair = block[twin].astype(F32)
        tokens.append(jnp.where((seq & 1) == 1, pair[8:16], pair[0:8]))
        scales.append(nt_dot(pick, block[128:144]))
    tokens = jnp.concatenate(tokens, axis=0)
    scales = jnp.concatenate(scales, axis=0)
    asked = []
    for side in range(2):
        high, low = scales[:, 2 * side : 2 * side + 1], scales[:, 2 * side + 1 : 2 * side + 2]
        spot = lane - 64 * (1 - side)
        own = jnp.where((lane >> 6) == side, tokens, 0.0)
        own = jnp.where((spot == 0) | (spot == 1), high, own)
        own = jnp.where((spot == 2) | (spot == 3), 1.0, own)
        own = jnp.where(spot == 4, low, own).astype(BF16)
        asked.append((nt_dot(own, asks_ref[:, 128 * side : 128 * side + 128]) * (1.0 / math.sqrt(HDIM))).astype(BF16))
    for head in range(HEADS):
        cols = slice(head * HDIM, (head + 1) * HDIM)
        keyed = [
            dot(asked[side][:, cols], keys_ref[cols, 256 * side : 256 * side + 256]).reshape(SEQ, 8, 256)
            for side in range(2)
        ]
        queries[:, head] = jnp.concatenate(keyed, axis=1).astype(BF16)
    n = HEADS * HALF
    same = jnp.where(iota((8, n), 0) == (iota((8, n), 1) & 7), 1.0, 0.0)
    for j, block in enumerate(blocks):
        query = queries[j].reshape(n, 256)
        ends = lax.dot_general(block[128:144], query[:, 128:144], (((0,), (1,)), ((), ())), preferred_element_type=F32)
        scores[j] = nt_dot(block[0:128], query[:, 0:128]) + ends
    for j in range(SEQ):
        each = scores[j].reshape(FRAMES, 8, n)
        raised = jnp.exp(each - jnp.max(each, axis=0, keepdims=True))
        shares = raised * (same / jnp.sum(raised, axis=0))
        weights[j] = jnp.transpose(shares.astype(BF16).reshape(128, n))
    for j, block in enumerate(blocks):
        mix = dot(weights[j], block[0:128]).reshape(HEADS, 2, 8, 128)
        ends = nt_dot(weights[j], block[128:144]).reshape(HEADS, 2, 8, 16)
        for side in range(2):
            mixed[side, :, j * 8 : (j + 1) * 8, 0:128] = mix[:, side]
            mixed[side, :, j * 8 : (j + 1) * 8, 128:144] = ends[:, side]
    for head in range(HEADS):
        cols = slice(head * HDIM, (head + 1) * HDIM)
        out = []
        for side in range(2):
            part = nt_dot(mixed[side, head, :, 0:128].astype(BF16), values_ref[cols, 256 * side : 256 * side + 128])
            at = 256 * side + 128
            part = part + nt_dot(mixed[side, head, :, 128:144].astype(BF16), values_ref[cols, at : at + 16])
            out.append(part.reshape(SEQ, 8, HDIM))
        out = jnp.concatenate(out, axis=1).astype(BF16)
        for j in range(SEQ):
            out_ref[pl.ds(pl.multiple_of((seq ^ j) * HALF, HALF), HALF), cols] = out[j]


def shape(*dims, dtype=BF16):
    return jax.ShapeDtypeStruct(dims, dtype)


def call(body, outs, ins, scratch=(), flops=0, moved=0, limit=32, first_out=VMEM):
    outs = list(outs) if isinstance(outs, list) else outs
    if first_out is HBM:
        outs[0] = pltpu.HBM(outs[0].shape, outs[0].dtype)
    kernel = pl.pallas_call(
        body,
        out_shape=outs,
        in_specs=ins,
        out_specs=[first_out] + [VMEM] * (len(outs) - 1) if isinstance(outs, list) else VMEM,
        scratch_shapes=list(scratch),
        compiler_params=pltpu.CompilerParams(vmem_limit_bytes=limit << 20),
        cost_estimate=pl.CostEstimate(flops=flops, bytes_accessed=moved, transcendentals=0),
        name=body.__name__,
    )

    def run(*args):
        return kernel(
            *(pltpu.with_memory_space_constraint(x, pltpu.HBM) if spec is HBM else x for x, spec in zip(args, ins))
        )

    return run


def swap(values, axis, bits, count):
    return lax.ppermute(values, axis, [(i, i ^ bits) for i in range(count)])


CHIP_PAIRS = [(i, i ^ 1) for i in range(SEQ)]
NEXT_PAIRS = [(i, (i + 1 if i & 1 else i - 1) % SEQ) for i in range(SEQ)]


def neighbours(near, far):
    far = lax.ppermute(far, "seq", NEXT_PAIRS)
    return lax.ppermute(near, "seq", CHIP_PAIRS), far


def exchange(stats):
    return lax.all_to_all(stats, "seq", 0, 0, tiled=True)


def gather_seq(block, beside):
    over = swap(block, "seq", 8, SEQ)
    over, beside = lax.optimization_barrier((over, beside))
    pair = jnp.stack([block, over])
    near = jnp.stack([pair] + [swap(pair, "seq", bits, SEQ) for bits in (2, 4, 6)])
    return near, swap(near, "seq", 1, SEQ), beside


WINDOW = pltpu.VMEM((4, FRAMES + 2, 4, HALF, C), BF16)
WEIGHT = pltpu.VMEM((27, C, C), BF16)
CONV_FLOPS = 2 * CELLS * 27 * C * C


def shards(
    features,
    first_conv,
    second_conv,
    out_conv,
    norm_gains,
    norm_shifts,
    embed_weight,
    embed_bias,
    mod_shift,
    mod_scale,
    qkv_weight,
):
    place = lax.axis_index("seq").astype(jnp.int32).reshape(1)
    clip = lax.axis_index("clip").astype(jnp.int32).reshape(1)
    row = shape(ROW, C)
    stats = shape(SEQ, 1, 128, dtype=F32)
    taps = 27

    beside = swap(qkv_weight, "clip", 2, CLIPS)
    cells = shape(CELLS, C)
    long_row = shape(ROW + 16, C)
    rows_f, near, far, stats0, norms, own_mods = call(
        split_kernel,
        [cells, row, row, stats, shape(8, C, dtype=F32), shape(2, D, dtype=F32)],
        [SMEM] + [HBM] * 5,
        [
            pltpu.VMEM((FRAMES, 2, 32, C), BF16),
            pltpu.VMEM((3, C), F32),
            pltpu.VMEM((3, C), F32),
            pltpu.VMEM((1, D), F32),
            pltpu.VMEM((1, D), F32),
            pltpu.VMEM((2, CELLS, 128), F32),
            DMA((5,)),
        ],
        0,
        1 << 20,
    )(place, features.reshape(FRAMES, 2, 32, C), norm_gains, norm_shifts, mod_scale, mod_shift)
    near, far = neighbours(near, far)
    mods = swap(own_mods, "clip", 1, CLIPS)
    stats0 = exchange(stats0)
    stats0, mods, beside = lax.optimization_barrier((stats0, mods, beside))
    here = jnp.stack([qkv_weight, beside])
    there = swap(here, "clip", 4, CLIPS)
    hidden, center, near_h, far_h, stats1 = call(
        first_kernel,
        [cells, shape(8, C, dtype=F32), long_row, long_row, stats],
        [SMEM] + [VMEM] * 5 + [HBM],
        [WINDOW, WEIGHT, pltpu.VMEM((CELLS, C), F32), pltpu.VMEM((CELLS, C), BF16), DMA((4,))],
        CONV_FLOPS,
        5 << 20,
        first_out=HBM,
    )(place, stats0, rows_f, near, far, norms, first_conv.reshape(taps, C, C))
    near, far = neighbours(near_h, far_h)

    embed, bias = call(embed_kernel, [shape(128, D), shape(8, D, dtype=F32)], [VMEM] * 2)(
        embed_weight, embed_bias.reshape(1, D)
    )
    folded = shape(4 * QROWS, 128)
    own, other = call(
        fold_kernel,
        [folded, folded],
        [VMEM] * 6,
        [pltpu.VMEM((4 * QPAD, D), BF16), pltpu.VMEM((4 * QROWS, 128), F32)],
    )(here, there, embed, bias, own_mods, mods)
    stats1 = exchange(stats1)
    stats1, own, other = lax.optimization_barrier((stats1, own, other))
    other = swap(other, "clip", 1, CLIPS)

    block, near_b, far_b, stats2 = call(
        second_kernel,
        [cells, row, row, stats],
        [SMEM, VMEM, HBM] + [VMEM] * 5 + [HBM],
        [WINDOW, WEIGHT, pltpu.VMEM((CELLS, C), F32), pltpu.VMEM((CELLS, C), BF16), DMA((4,))],
        CONV_FLOPS,
        6 << 20,
    )(place, stats1, hidden, center, near, far, norms, rows_f, second_conv.reshape(taps, C, C))
    near, far = neighbours(near_b, far_b)
    stats2 = exchange(stats2)
    patches, parcel = call(
        third_kernel,
        [shape(FRAMES * HALF, 4 * LAT, dtype=F32), shape(336, 128)],
        [SMEM] + [VMEM] * 10,
        [WINDOW, pltpu.VMEM((48, 4 * LAT, C), BF16), pltpu.VMEM((8 * QROWS + 8, 128), F32)],
        CONV_FLOPS // 2,
        4 << 20,
    )(
        place, stats2, block, near, far, norms,
        out_conv.transpose(0, 1, 2, 4, 3).reshape(taps, LAT, C), embed, bias, own, other,
    )
    latent = call(latent_kernel, shape(FRAMES, 2, LAT, 2 * HALF, dtype=F32), [VMEM])(patches)
    near, far, latent = gather_seq(parcel, latent)
    asks, keys, values = call(
        sort_kernel,
        [shape(WIDE, 256), shape(WIDE, 512), shape(WIDE, 512)],
        [SMEM] * 2 + [VMEM] * 2,
        [pltpu.VMEM((SEQ, 192, 128), F32), pltpu.VMEM((3 * WIDE, 128), F32)],
    )(place, clip, near, far)
    frame_heads = call(
        attend_kernel,
        shape(SEQ * HALF, WIDE),
        [SMEM] + [VMEM] * 5,
        [
            pltpu.VMEM((SEQ, HEADS, HALF, 256), BF16),
            pltpu.VMEM((2, HEADS, 128, 256), F32),
            pltpu.VMEM((SEQ, 128, HEADS * HALF), F32),
            pltpu.VMEM((SEQ, HEADS * HALF, 128), BF16),
        ],
    )(place, near, far, asks, keys, values)
    latent = latent.transpose(0, 1, 3, 2).reshape(1, FRAMES, 2, 2 * HALF, LAT)
    return (latent, frame_heads.reshape(1, 1, SEQ * HALF, WIDE))


def solution(mesh):
    placed = (
        P("clip", None, "seq", None, None),
        P(),
        P(),
        P(),
        P(),
        P(),
        P(),
        P(),
        P("clip", None),
        P("clip", None),
        P(("clip", "seq"), None),
    )
    return jax.shard_map(
        shards,
        mesh=mesh,
        in_specs=placed,
        out_specs=(P("clip", None, "seq", None, None), P("clip", "seq", None, None)),
        check_vma=False,
    )
```

```python
import functools
import math

import jax
import jax.numpy as jnp
from jax import lax
from jax.experimental import pallas as pl
from jax.experimental.pallas import tpu as pltpu
from jax.sharding import PartitionSpec as P

C = 256
GROUPS = 32
LAT = 16
D = 3072
HEADS = 12
HDIM = 128
FRAMES = 16
HALF = 16
ROW = FRAMES * 2 * HALF
CELLS = 2 * ROW
SEQ = 16
CLIPS = 8
QROWS = 36
QPAD = 48
EPS = 1e-06
F32 = jnp.float32
BF16 = jnp.bfloat16
VMEM = pl.BlockSpec(memory_space=pltpu.VMEM)
SMEM = pl.BlockSpec(memory_space=pltpu.SMEM)
HBM = pl.BlockSpec(memory_space=pltpu.HBM)
DMA = pltpu.SemaphoreType.DMA


def nt_dot(a, b):
    return lax.dot_general(a, b, (((1,), (1,)), ((), ())), preferred_element_type=F32)


def dot(a, b):
    return jnp.dot(a, b, preferred_element_type=F32)


def exact_dot(rows, zero_one):
    high = rows.astype(BF16).astype(F32)
    rest = rows - high
    mid = rest.astype(BF16).astype(F32)
    low = rest - mid
    parts = jnp.concatenate([high, mid, low, jnp.zeros_like(low)], axis=0).astype(BF16)
    out = dot(parts, zero_one)
    return out[0:8] + out[8:16] + out[16:24]


def iota(shape, dim):
    return lax.broadcasted_iota(jnp.int32, shape, dim)


def one_hot(cond):
    return jnp.where(cond, 1.0, 0.0).astype(BF16)


def rows8(first, second=None):
    n = first.shape[1]
    row = iota((8, n), 0)
    out = jnp.where(row == 0, jnp.broadcast_to(first, (8, n)), 0.0)
    if second is not None:
        out = jnp.where(row == 1, jnp.broadcast_to(second, (8, n)), out)
    return out


def write_stats(mean_c, square_c, count, stats_ref):
    same = one_hot((iota((C, C), 0) >> 3) == (iota((C, C), 1) >> 3))
    mean_g = exact_dot(rows8(mean_c), same)[0:1] * (1.0 / 8)
    gap = mean_c - mean_g
    square_c = square_c + count * (gap * gap)
    lane = iota((C, 128), 1)
    pick = one_hot((iota((C, 128), 0) >> 3) == (lane & 31))
    both = exact_dot(rows8(mean_c * (1.0 / 8), square_c), pick)
    row = jnp.where(iota((1, 128), 1) < GROUPS, both[0:1], both[1:2])
    stats_ref[...] = jnp.broadcast_to(row[None], (SEQ, 1, 128))


def read_stats(stats_ref, count):
    each = stats_ref[...].reshape(SEQ, 128)
    lane = iota((1, 128), 1)
    mean = jnp.sum(each, axis=0, keepdims=True) * (1.0 / SEQ)
    off = each - mean
    between = jnp.sum(off * off, axis=0, keepdims=True) * (8.0 * count)
    within = mean * SEQ
    total = jnp.where(lane < GROUPS, between, jnp.where(lane < 2 * GROUPS, within, 0.0))
    mean = jnp.where(lane < GROUPS, mean, 0.0)
    spread = one_hot((iota((128, C), 0) & 31) == (iota((128, C), 1) >> 3))
    both = exact_dot(rows8(mean, total), spread)
    return both[0:1], lax.rsqrt(both[1:2] * (1.0 / (8.0 * count * SEQ)) + EPS)


def own_rows(place_ref, rows_ref, near_ref, far_ref):
    odd = place_ref[0] & 1
    near_ref[...] = rows_ref[pl.ds(pl.multiple_of((1 - odd) * ROW, ROW), ROW)].astype(BF16)
    far_ref[...] = rows_ref[pl.ds(pl.multiple_of(odd * ROW, ROW), ROW)].astype(BF16)


def split_kernel(
    place_ref, feat_hbm, gain_hbm, shift_hbm, scale_hbm, mod_hbm,
    rows_ref, near_ref, far_ref, stats_ref, norms_ref, mods_ref,
    feat_ref, gain_ref, shift_ref, scale_ref, mod_ref, wide, sems,
):
    sources = (feat_hbm, gain_hbm, shift_hbm, scale_hbm, mod_hbm)
    targets = (feat_ref, gain_ref, shift_ref, scale_ref, mod_ref)
    copies = [pltpu.make_async_copy(a, b, sems.at[i]) for i, (a, b) in enumerate(zip(sources, targets))]
    for copy in copies:
        copy.start()
    for copy in copies:
        copy.wait()
    norms_ref[0:3] = gain_ref[...]
    norms_ref[4:7] = shift_ref[...]
    mods_ref[0:1] = scale_ref[...]
    mods_ref[1:2] = mod_ref[...]
    cells = feat_ref[...].astype(F32).reshape(CELLS, C)
    for side in range(2):
        wide[side] = cells[:, side * 128 : (side + 1) * 128]
    for frame in range(FRAMES):
        for row in range(2):
            for parity in range(2):
                base = (frame * 2 + row) * 32 + parity
                at = row * ROW + (frame * 2 + parity) * HALF
                for side in range(2):
                    part = wide[side, pl.ds(base, HALF, stride=2)]
                    rows_ref[at : at + HALF, side * 128 : (side + 1) * 128] = part.astype(BF16)
    own_rows(place_ref, rows_ref, near_ref, far_ref)
    mean = jnp.sum(cells, axis=0, keepdims=True) * (1.0 / CELLS)
    off = cells - mean
    write_stats(mean, jnp.sum(off * off, axis=0, keepdims=True), CELLS, stats_ref)


def fill_window(place_ref, stats_ref, rows_ref, near_ref, far_ref, norms_ref, layer, window, centers=None, load=None):
    mean, rstd = read_stats(stats_ref, CELLS)
    gain = rstd * norms_ref[layer : layer + 1] * 0.5
    shift = norms_ref[4 + layer : 5 + layer] * 0.5
    place = place_ref[0]
    odd = place & 1
    near_at = 3 * (1 - odd)
    far_on = jnp.where((place > 0) & (place < SEQ - 1), 1.0, 0.0).astype(F32)
    window[:, 0:2] = jnp.zeros((4, 2, 4, HALF, C), BF16)
    step = 4
    n = step * HALF
    pair = iota((n, C), 0) & (HALF - 1)
    level = -mean
    levels = [level] * 4 if centers is None else [center + level for center in centers]
    sources = (
        (near_at, near_ref),
        (3 - near_at, far_ref),
        (1, rows_ref.at[0:ROW]),
        (2, rows_ref.at[ROW:CELLS]),
    )
    for which, (row, source) in enumerate(sources):
        if which == 2 and load is not None:
            load.wait()
        for frame in range(0, FRAMES, step):
            x = source[frame * 32 : (frame + step) * 32].astype(F32)
            half = (x + levels[which]) * gain + shift
            act = half + half * jnp.tanh(half)
            if which == 1:
                act = act * far_on
            act = act.reshape(step, 2, HALF, C)
            even = act[:, 0].reshape(n, C)
            odd_ones = act[:, 1].reshape(n, C)
            odd_before = jnp.where(pair == 0, 0.0, pltpu.roll(odd_ones, 1, 0))
            even_after = jnp.where(pair == HALF - 1, 0.0, pltpu.roll(even, n - 1, 0))
            for plane, part in enumerate((odd_before, even, odd_ones, even_after)):
                window[row, 2 + frame : 2 + frame + step, plane] = part.astype(BF16).reshape(
                    step, HALF, C
                )


TILE = 256


def start_weights(source, weight, sems):
    copies = [
        pltpu.make_async_copy(source.at[9 * p : 9 * p + 9], weight.at[9 * p : 9 * p + 9], sems.at[p])
        for p in range(3)
    ]
    for copy in copies:
        copy.start()
    return copies


def convolve(window, weight, copies, total, finish):
    for p in range(3):
        copies[p].wait()
        for tile in range(CELLS // TILE):
            row, frame = tile * TILE // ROW, tile * TILE % ROW // 32
            part = None
            for q in range(3):
                for r in range(3):
                    at = frame + p
                    cells = window[q + row, at : at + TILE // 32, r : r + 2].reshape(TILE, C)
                    term = dot(cells, weight[9 * p + 3 * q + r])
                    part = term if part is None else part + term
            rows = slice(tile * TILE, (tile + 1) * TILE)
            if p > 0:
                part = part + total[rows]
            if p < 2:
                total[rows] = part
            else:
                finish(rows, part)


class Moments:
    def __init__(self):
        self.center = self.first = self.second = None

    def add(self, tile):
        if self.center is None:
            self.center = jnp.sum(tile, axis=0, keepdims=True) * (1.0 / TILE)
        off = tile - self.center
        first = jnp.sum(off, axis=0, keepdims=True)
        second = jnp.sum(off * off, axis=0, keepdims=True)
        self.first = first if self.first is None else self.first + first
        self.second = second if self.second is None else self.second + second
        return off

    def write(self, stats_ref):
        gap = self.first * (1.0 / CELLS)
        square = jnp.maximum(self.second - self.first * gap, 0.0)
        write_stats(self.center + gap, square, CELLS, stats_ref)


def first_kernel(
    place_ref, stats_ref, rows_ref, near_ref, far_ref, norms_ref, weight_hbm,
    hidden_hbm, center_ref, near_out, far_out, stats_out, window, weight, total, hidden_ref, sems,
):
    copies = start_weights(weight_hbm, weight, sems)
    fill_window(place_ref, stats_ref, rows_ref, near_ref, far_ref, norms_ref, 0, window)
    moments = Moments()

    def finish(rows, tile):
        hidden_ref[rows] = moments.add(tile).astype(BF16)

    convolve(window, weight, copies, total, finish)
    copy = pltpu.make_async_copy(hidden_ref, hidden_hbm, sems.at[3])
    copy.start()
    center = moments.center
    center_ref[...] = jnp.broadcast_to(center, (8, C))
    high = center.astype(BF16).astype(F32)
    mid = (center - high).astype(BF16).astype(F32)
    line = iota((16, C), 0)
    terms = jnp.where(line == 0, high, jnp.where(line == 1, mid, jnp.where(line == 2, center - high - mid, 0.0)))
    own_rows(place_ref, hidden_ref, near_out.at[0:ROW], far_out.at[0:ROW])
    near_out[ROW : ROW + 16] = terms.astype(BF16)
    far_out[ROW : ROW + 16] = terms.astype(BF16)
    moments.write(stats_out)
    copy.wait()


def second_kernel(
    place_ref, stats_ref, hidden_hbm, center_ref, near_ref, far_ref, norms_ref, feat_ref, weight_hbm,
    block_ref, near_out, far_out, stats_out, window, weight, total, hidden_ref, sems,
):
    load = pltpu.make_async_copy(hidden_hbm, hidden_ref, sems.at[3])
    load.start()
    copies = start_weights(weight_hbm, weight, sems)
    own = center_ref[0:1]
    centers = [jnp.sum(ref[ROW : ROW + 16].astype(F32), axis=0, keepdims=True) for ref in (near_ref, far_ref)]
    centers += [own, own]
    fill_window(place_ref, stats_ref, hidden_ref, near_ref, far_ref, norms_ref, 1, window, centers, load)
    moments = Moments()

    def finish(rows, tile):
        block = (tile + feat_ref[rows].astype(F32)).astype(BF16)
        block_ref[rows] = block
        moments.add(block.astype(F32))

    convolve(window, weight, copies, total, finish)
    own_rows(place_ref, block_ref, near_out, far_out)
    moments.write(stats_out)


def column_to_row(column):
    square = jnp.broadcast_to(column, (128, 128))
    return jnp.sum(jnp.where(iota((128, 128), 0) == iota((128, 128), 1), square, 0.0), axis=0, keepdims=True)


def third_kernel(
    place_ref, stats_ref, rows_ref, near_ref, far_ref, norms_ref, weight_ref, embed_ref, bias_ref,
    own_ref, other_ref, patches_ref, parcel_ref, window, weight, folds,
):
    n = FRAMES * HALF
    for p in range(3):
        for row in range(4):
            for plane in range(4):
                block = (p * 4 + row) * 4 + plane
                for dh in range(2):
                    for dw in range(2):
                        at = (2 * dh + dw) * LAT
                        q, r = row - dh, plane - dw
                        if 0 <= q < 3 and 0 <= r < 3:
                            weight[block, at : at + LAT] = weight_ref[9 * p + 3 * q + r]
                        else:
                            weight[block, at : at + LAT] = jnp.zeros((LAT, C), BF16)
    fill_window(place_ref, stats_ref, rows_ref, near_ref, far_ref, norms_ref, 2, window)
    patches = None
    for p in range(3):
        for row in range(4):
            for plane in range(4):
                cells = window[row, p : p + FRAMES, plane].reshape(n, C)
                term = nt_dot(cells, weight[(p * 4 + row) * 4 + plane])
                patches = term if patches is None else patches + term
    patches_ref[...] = patches
    rounded = patches.astype(BF16)
    embedded = dot(jnp.concatenate([rounded, rounded], axis=1), embed_ref[...]) + bias_ref[0:1]
    spread = jnp.sum(embedded * embedded, axis=1, keepdims=True) * (1.0 / D)
    rstd = lax.rsqrt(spread + EPS)
    scaled = (rounded.astype(F32) * rstd).reshape(FRAMES, 2, 8, 64)
    rstd = jnp.broadcast_to(rstd, (n, 128)).reshape(FRAMES, 2, 8, 128)
    both = jnp.concatenate([scaled[:, side].reshape(128, 64) for side in range(2)], axis=1)
    parcel_ref[0:128] = both.astype(BF16)
    line = iota((16, 128), 0)
    lines = jnp.where(line == 4, 1.0, 0.0)
    for side in range(2):
        each = column_to_row(rstd[:, side].reshape(128, 128)[:, 0:1])
        high = each.astype(BF16).astype(F32)
        lines = jnp.where(line == 2 * side, high, lines)
        lines = jnp.where(line == 2 * side + 1, each - high, lines)
    parcel_ref[128:144] = lines.astype(BF16)
    own, other = own_ref[...].astype(F32), other_ref[...].astype(F32)
    lane = iota((4 * QROWS, 128), 1)
    parcel_ref[144:288] = jnp.where(lane < 64, own, pltpu.roll(other, 64, 1)).astype(BF16)
    folds[0 : 4 * QROWS] = own
    folds[4 * QROWS : 8 * QROWS] = other
    folds[8 * QROWS :] = jnp.zeros((8, 128), F32)
    lane = iota((40, 128), 1)
    ends = jnp.zeros((40, 128), F32)
    for i in range(8):
        ends = jnp.where((lane >> 3) == i, pltpu.roll(folds[i * QROWS : i * QROWS + 40], (8 * i + 64) % 128, 1), ends)
    parcel_ref[288:336] = jnp.concatenate([ends, jnp.zeros((8, 128), F32)], axis=0).astype(BF16)


def latent_kernel(patches_ref, latent_ref):
    n = FRAMES * HALF
    patches = patches_ref[...]
    turned = jnp.transpose(jnp.concatenate([patches, jnp.zeros_like(patches)], axis=1))
    out = None
    for dw in range(2):
        rows = jnp.concatenate([turned[(2 * dh + dw) * LAT : (2 * dh + dw + 1) * LAT] for dh in range(2)], axis=0)
        high = rows.astype(BF16).astype(F32)
        mid = (rows - high).astype(BF16).astype(F32)
        parts = jnp.concatenate([high, mid, rows - high - mid], axis=0).astype(BF16)
        column = iota((n, 2 * n), 1)
        spread = one_hot(column == iota((n, 2 * n), 0) * 2 + dw)
        term = dot(parts, spread)
        term = term[0:32] + term[32:64] + term[64:96]
        out = term if out is None else out + term
    for frame in range(FRAMES):
        for dh in range(2):
            latent_ref[frame, dh] = out[dh * LAT : (dh + 1) * LAT, frame * 32 : (frame + 1) * 32]


def fold_kernel(
    w0_ref, w1_ref, w2_ref, w3_ref, embed_ref, bias_ref, own_mods_ref, mods_ref,
    own_ref, other_ref, embed_out, bias_out, stacked, wide,
):
    embed = embed_ref[...].astype(F32)
    embed = embed - jnp.mean(embed, axis=1, keepdims=True)
    high = embed.astype(BF16)
    embed_out[0:64] = high
    embed_out[64:128] = (embed - high.astype(F32)).astype(BF16)
    center = bias_ref[...] - jnp.mean(bias_ref[...], axis=1, keepdims=True)
    bias_out[...] = jnp.broadcast_to(center, (8, D))
    for i in range(4):
        block = (w0_ref, w1_ref, w2_ref, w3_ref)[i][...].astype(F32)
        block = jnp.concatenate([block, jnp.zeros((QPAD - QROWS, D), F32)], axis=0)
        stacked[i * QPAD : (i + 1) * QPAD] = block.astype(BF16)
    row = iota((64, D), 0)
    sides = []
    for mod_ref in (own_mods_ref, mods_ref):
        scale, shift = 1.0 + mod_ref[0:1], mod_ref[1:2]
        bias = center * scale
        bias_high = bias.astype(BF16).astype(F32)
        shift_high = shift.astype(BF16).astype(F32)
        ends = jnp.where(row == 0, bias_high, jnp.where(row == 1, bias - bias_high, 0.0))
        ends = jnp.where(row == 2, shift_high, jnp.where(row == 3, shift - shift_high, ends))
        sides += [embed * scale, ends]
    every = jnp.concatenate(sides, axis=0).astype(BF16)
    out = nt_dot(stacked[...], every)
    lane = iota((4 * QPAD, 128), 1)
    for side, target in enumerate((own_ref, other_ref)):
        part = out[:, side * 128 : (side + 1) * 128]
        bias = part[:, 64:65] + part[:, 65:66]
        shift = part[:, 66:67] + part[:, 67:68]
        bias_high = bias.astype(BF16).astype(F32)
        shift_high = shift.astype(BF16).astype(F32)
        part = jnp.where((lane == 64) | (lane == 68), bias_high, part)
        part = jnp.where(lane == 65, bias - bias_high, part)
        part = jnp.where(lane == 66, shift_high, part)
        part = jnp.where(lane == 67, shift - shift_high, part)
        for i in range(4):
            wide[i * QROWS : (i + 1) * QROWS] = part[i * QPAD : i * QPAD + QROWS]
        target[...] = wide[...].astype(BF16)


WIDE = HEADS * HDIM


def sort_kernel(place_ref, clip_ref, near_ref, far_ref, asks_ref, keys_ref, values_ref, loose, wide):
    seq, clip = place_ref[0], clip_ref[0]
    spot = iota((40, 128), 1)
    for j in range(SEQ):
        source = (near_ref, far_ref)[j & 1]
        loose[j] = source[(j >> 1) & 3, j >> 3, 144:336].astype(F32)
        for k in range(CLIPS):
            at = ((clip ^ (2 * (k & 3) + (k >> 2))) * SEQ + (seq ^ j)) * QROWS
            block = loose[j, (k & 3) * QROWS : (k & 3) * QROWS + 40]
            block = pltpu.roll(block, 64, 1) if k >> 2 else block
            ends = pltpu.roll(loose[j, 144:184], (64 - 8 * k) % 128, 1)
            block = jnp.where(spot < 64, block, jnp.where(spot < 69, ends, 0.0))
            wide[pl.ds(at, QROWS)] = block[:QROWS]
    lane = iota((WIDE, 128), 1)
    rows = wide[0:WIDE]
    asks_ref[:, 0:128] = rows.astype(BF16)
    asks_ref[:, 128:256] = pltpu.roll(rows, 64, 1).astype(BF16)
    for part, target in ((1, keys_ref), (2, values_ref)):
        rows = wide[part * WIDE : (part + 1) * WIDE]
        bias = rows[:, 64:65] + rows[:, 65:66]
        shift = rows[:, 66:67] + rows[:, 67:68]
        left = jnp.where(lane < 64, rows, 0.0)
        target[:, 0:128] = left.astype(BF16)
        target[:, 256:384] = pltpu.roll(left, 64, 1).astype(BF16)
        for side in range(2):
            extra = jnp.where((lane == 2 * side) | (lane == 2 * side + 1), bias, 0.0)
            extra = jnp.where(lane == 4, shift, extra)
            target[:, 256 * side + 128 : 256 * side + 256] = extra.astype(BF16)


def attend_kernel(place_ref, near_ref, far_ref, asks_ref, keys_ref, values_ref, out_ref, queries, mixed, scores, weights):
    seq = place_ref[0]
    blocks = [(near_ref, far_ref)[j & 1].at[(j >> 1) & 3, j >> 3] for j in range(SEQ)]
    lane = iota((128, 128), 1)
    pick = one_hot(iota((8, 128), 1) == iota((8, 128), 0) + seq * 8)
    twin = pl.ds(pl.multiple_of((seq >> 1) * 16, 16), 16)
    tokens, scales = [], []
    for block in blocks:
        pair = block[twin].astype(F32)
        tokens.append(jnp.where((seq & 1) == 1, pair[8:16], pair[0:8]))
        scales.append(nt_dot(pick, block[128:144]))
    tokens = jnp.concatenate(tokens, axis=0)
    scales = jnp.concatenate(scales, axis=0)
    asked = []
    for side in range(2):
        high, low = scales[:, 2 * side : 2 * side + 1], scales[:, 2 * side + 1 : 2 * side + 2]
        spot = lane - 64 * (1 - side)
        own = jnp.where((lane >> 6) == side, tokens, 0.0)
        own = jnp.where((spot == 0) | (spot == 1), high, own)
        own = jnp.where((spot == 2) | (spot == 3), 1.0, own)
        own = jnp.where(spot == 4, low, own).astype(BF16)
        asked.append((nt_dot(own, asks_ref[:, 128 * side : 128 * side + 128]) * (1.0 / math.sqrt(HDIM))).astype(BF16))
    for head in range(HEADS):
        cols = slice(head * HDIM, (head + 1) * HDIM)
        keyed = [
            dot(asked[side][:, cols], keys_ref[cols, 256 * side : 256 * side + 256]).reshape(SEQ, 8, 256)
            for side in range(2)
        ]
        queries[:, head] = jnp.concatenate(keyed, axis=1).astype(BF16)
    n = HEADS * HALF
    same = jnp.where(iota((8, n), 0) == (iota((8, n), 1) & 7), 1.0, 0.0)
    for j, block in enumerate(blocks):
        query = queries[j].reshape(n, 256)
        ends = lax.dot_general(block[128:144], query[:, 128:144], (((0,), (1,)), ((), ())), preferred_element_type=F32)
        scores[j] = nt_dot(block[0:128], query[:, 0:128]) + ends
    for j in range(SEQ):
        each = scores[j].reshape(FRAMES, 8, n)
        raised = jnp.exp(each - jnp.max(each, axis=0, keepdims=True))
        shares = raised * (same / jnp.sum(raised, axis=0))
        weights[j] = jnp.transpose(shares.astype(BF16).reshape(128, n))
    for j, block in enumerate(blocks):
        mix = dot(weights[j], block[0:128]).reshape(HEADS, 2, 8, 128)
        ends = nt_dot(weights[j], block[128:144]).reshape(HEADS, 2, 8, 16)
        for side in range(2):
            mixed[side, :, j * 8 : (j + 1) * 8, 0:128] = mix[:, side]
            mixed[side, :, j * 8 : (j + 1) * 8, 128:144] = ends[:, side]
    for head in range(HEADS):
        cols = slice(head * HDIM, (head + 1) * HDIM)
        out = []
        for side in range(2):
            part = nt_dot(mixed[side, head, :, 0:128].astype(BF16), values_ref[cols, 256 * side : 256 * side + 128])
            at = 256 * side + 128
            part = part + nt_dot(mixed[side, head, :, 128:144].astype(BF16), values_ref[cols, at : at + 16])
            out.append(part.reshape(SEQ, 8, HDIM))
        out = jnp.concatenate(out, axis=1).astype(BF16)
        for j in range(SEQ):
            out_ref[pl.ds(pl.multiple_of((seq ^ j) * HALF, HALF), HALF), cols] = out[j]


def shape(*dims, dtype=BF16):
    return jax.ShapeDtypeStruct(dims, dtype)


def call(body, outs, ins, scratch=(), flops=0, moved=0, limit=32, first_out=VMEM):
    outs = list(outs) if isinstance(outs, list) else outs
    if first_out is HBM:
        outs[0] = pltpu.HBM(outs[0].shape, outs[0].dtype)
    kernel = pl.pallas_call(
        body,
        out_shape=outs,
        in_specs=ins,
        out_specs=[first_out] + [VMEM] * (len(outs) - 1) if isinstance(outs, list) else VMEM,
        scratch_shapes=list(scratch),
        compiler_params=pltpu.CompilerParams(vmem_limit_bytes=limit << 20),
        cost_estimate=pl.CostEstimate(flops=flops, bytes_accessed=moved, transcendentals=0),
        name=body.__name__,
    )

    def run(*args):
        return kernel(
            *(pltpu.with_memory_space_constraint(x, pltpu.HBM) if spec is HBM else x for x, spec in zip(args, ins))
        )

    return run


def swap(values, axis, bits, count):
    return lax.ppermute(values, axis, [(i, i ^ bits) for i in range(count)])


CHIP_PAIRS = [(i, i ^ 1) for i in range(SEQ)]
NEXT_PAIRS = [(i, (i + 1 if i & 1 else i - 1) % SEQ) for i in range(SEQ)]


def neighbours(near, far):
    far = lax.ppermute(far, "seq", NEXT_PAIRS)
    return lax.ppermute(near, "seq", CHIP_PAIRS), far


def exchange(stats):
    return lax.all_to_all(stats, "seq", 0, 0, tiled=True)


def gather_seq(block, beside):
    over = swap(block, "seq", 8, SEQ)
    over, beside = lax.optimization_barrier((over, beside))
    pair = jnp.stack([block, over])
    near = jnp.stack([pair] + [swap(pair, "seq", bits, SEQ) for bits in (2, 4, 6)])
    return near, swap(near, "seq", 1, SEQ), beside


WINDOW = pltpu.VMEM((4, FRAMES + 2, 4, HALF, C), BF16)
WEIGHT = pltpu.VMEM((27, C, C), BF16)
CONV_FLOPS = 2 * CELLS * 27 * C * C


def shards(
    features,
    first_conv,
    second_conv,
    out_conv,
    norm_gains,
    norm_shifts,
    embed_weight,
    embed_bias,
    mod_shift,
    mod_scale,
    qkv_weight,
):
    place = lax.axis_index("seq").astype(jnp.int32).reshape(1)
    clip = lax.axis_index("clip").astype(jnp.int32).reshape(1)
    row = shape(ROW, C)
    stats = shape(SEQ, 1, 128, dtype=F32)
    taps = 27

    beside = swap(qkv_weight, "clip", 2, CLIPS)
    cells = shape(CELLS, C)
    long_row = shape(ROW + 16, C)
    rows_f, near, far, stats0, norms, own_mods = call(
        split_kernel,
        [cells, row, row, stats, shape(8, C, dtype=F32), shape(2, D, dtype=F32)],
        [SMEM] + [HBM] * 5,
        [
            pltpu.VMEM((FRAMES, 2, 32, C), BF16),
            pltpu.VMEM((3, C), F32),
            pltpu.VMEM((3, C), F32),
            pltpu.VMEM((1, D), F32),
            pltpu.VMEM((1, D), F32),
            pltpu.VMEM((2, CELLS, 128), F32),
            DMA((5,)),
        ],
        0,
        1 << 20,
    )(place, features.reshape(FRAMES, 2, 32, C), norm_gains, norm_shifts, mod_scale, mod_shift)
    near, far = neighbours(near, far)
    mods = swap(own_mods, "clip", 1, CLIPS)
    stats0 = exchange(stats0)
    stats0, mods, beside = lax.optimization_barrier((stats0, mods, beside))
    stats0, mine = lax.optimization_barrier((stats0, qkv_weight))
    rows = [qkv_weight, beside] + [swap(mine, "clip", bits, CLIPS) for bits in (4, 6)]
    hidden, center, near_h, far_h, stats1 = call(
        first_kernel,
        [cells, shape(8, C, dtype=F32), long_row, long_row, stats],
        [SMEM] + [VMEM] * 5 + [HBM],
        [WINDOW, WEIGHT, pltpu.VMEM((CELLS, C), F32), pltpu.VMEM((CELLS, C), BF16), DMA((4,))],
        CONV_FLOPS,
        5 << 20,
        first_out=HBM,
    )(place, stats0, rows_f, near, far, norms, first_conv.reshape(taps, C, C))
    near, far = neighbours(near_h, far_h)

    stats1 = exchange(stats1)
    stats1, *rows = lax.optimization_barrier((stats1, *rows))

    block, near_b, far_b, stats2 = call(
        second_kernel,
        [cells, row, row, stats],
        [SMEM, VMEM, HBM] + [VMEM] * 5 + [HBM],
        [WINDOW, WEIGHT, pltpu.VMEM((CELLS, C), F32), pltpu.VMEM((CELLS, C), BF16), DMA((4,))],
        CONV_FLOPS,
        6 << 20,
    )(place, stats1, hidden, center, near, far, norms, rows_f, second_conv.reshape(taps, C, C))
    near, far = neighbours(near_b, far_b)
    stats2, *rows = lax.optimization_barrier((stats2, *rows))
    folded = shape(4 * QROWS, 128)
    own, other, embed, bias = call(
        fold_kernel,
        [folded, folded, shape(128, D), shape(8, D, dtype=F32)],
        [VMEM] * 8,
        [pltpu.VMEM((4 * QPAD, D), BF16), pltpu.VMEM((4 * QROWS, 128), F32)],
    )(*rows, embed_weight, embed_bias.reshape(1, D), own_mods, mods)
    other = swap(other, "clip", 1, CLIPS)
    stats2 = exchange(stats2)
    patches, parcel = call(
        third_kernel,
        [shape(FRAMES * HALF, 4 * LAT, dtype=F32), shape(336, 128)],
        [SMEM] + [VMEM] * 10,
        [WINDOW, pltpu.VMEM((48, 4 * LAT, C), BF16), pltpu.VMEM((8 * QROWS + 8, 128), F32)],
        CONV_FLOPS // 2,
        4 << 20,
    )(
        place, stats2, block, near, far, norms,
        out_conv.transpose(0, 1, 2, 4, 3).reshape(taps, LAT, C), embed, bias, own, other,
    )
    latent = call(latent_kernel, shape(FRAMES, 2, LAT, 2 * HALF, dtype=F32), [VMEM])(patches)
    near, far, latent = gather_seq(parcel, latent)
    asks, keys, values = call(
        sort_kernel,
        [shape(WIDE, 256), shape(WIDE, 512), shape(WIDE, 512)],
        [SMEM] * 2 + [VMEM] * 2,
        [pltpu.VMEM((SEQ, 192, 128), F32), pltpu.VMEM((3 * WIDE, 128), F32)],
    )(place, clip, near, far)
    frame_heads = call(
        attend_kernel,
        shape(SEQ * HALF, WIDE),
        [SMEM] + [VMEM] * 5,
        [
            pltpu.VMEM((SEQ, HEADS, HALF, 256), BF16),
            pltpu.VMEM((2, HEADS, 128, 256), F32),
            pltpu.VMEM((SEQ, 128, HEADS * HALF), F32),
            pltpu.VMEM((SEQ, HEADS * HALF, 128), BF16),
        ],
    )(place, near, far, asks, keys, values)
    latent = latent.transpose(0, 1, 3, 2).reshape(1, FRAMES, 2, 2 * HALF, LAT)
    return (latent, frame_heads.reshape(1, 1, SEQ * HALF, WIDE))


def solution(mesh):
    placed = (
        P("clip", None, "seq", None, None),
        P(),
        P(),
        P(),
        P(),
        P(),
        P(),
        P(),
        P("clip", None),
        P("clip", None),
        P(("clip", "seq"), None),
    )
    return jax.shard_map(
        shards,
        mesh=mesh,
        in_specs=placed,
        out_specs=(P("clip", None, "seq", None, None), P("clip", "seq", None, None)),
        check_vma=False,
    )
```

```python
import functools
import math

import jax
import jax.numpy as jnp
from jax import lax
from jax.experimental import pallas as pl
from jax.experimental.pallas import tpu as pltpu
from jax.sharding import PartitionSpec as P

C = 256
GROUPS = 32
LAT = 16
D = 3072
HEADS = 12
HDIM = 128
FRAMES = 16
HALF = 16
ROW = FRAMES * 2 * HALF
CELLS = 2 * ROW
SEQ = 16
CLIPS = 8
QROWS = 36
QPAD = 48
EPS = 1e-06
F32 = jnp.float32
BF16 = jnp.bfloat16
VMEM = pl.BlockSpec(memory_space=pltpu.VMEM)
SMEM = pl.BlockSpec(memory_space=pltpu.SMEM)
HBM = pl.BlockSpec(memory_space=pltpu.HBM)
DMA = pltpu.SemaphoreType.DMA


def nt_dot(a, b):
    return lax.dot_general(a, b, (((1,), (1,)), ((), ())), preferred_element_type=F32)


def dot(a, b):
    return jnp.dot(a, b, preferred_element_type=F32)


def exact_dot(rows, zero_one):
    high = rows.astype(BF16).astype(F32)
    rest = rows - high
    mid = rest.astype(BF16).astype(F32)
    low = rest - mid
    parts = jnp.concatenate([high, mid, low, jnp.zeros_like(low)], axis=0).astype(BF16)
    out = dot(parts, zero_one)
    return out[0:8] + out[8:16] + out[16:24]


def iota(shape, dim):
    return lax.broadcasted_iota(jnp.int32, shape, dim)


def one_hot(cond):
    return jnp.where(cond, 1.0, 0.0).astype(BF16)


def rows8(first, second=None):
    n = first.shape[1]
    row = iota((8, n), 0)
    out = jnp.where(row == 0, jnp.broadcast_to(first, (8, n)), 0.0)
    if second is not None:
        out = jnp.where(row == 1, jnp.broadcast_to(second, (8, n)), out)
    return out


def write_stats(mean_c, square_c, count, stats_ref):
    same = one_hot((iota((C, C), 0) >> 3) == (iota((C, C), 1) >> 3))
    mean_g = exact_dot(rows8(mean_c), same)[0:1] * (1.0 / 8)
    gap = mean_c - mean_g
    square_c = square_c + count * (gap * gap)
    lane = iota((C, 128), 1)
    pick = one_hot((iota((C, 128), 0) >> 3) == (lane & 31))
    both = exact_dot(rows8(mean_c * (1.0 / 8), square_c), pick)
    row = jnp.where(iota((1, 128), 1) < GROUPS, both[0:1], both[1:2])
    stats_ref[...] = jnp.broadcast_to(row[None], (SEQ, 1, 128))


def read_stats(stats_ref, count):
    each = stats_ref[...].reshape(SEQ, 128)
    lane = iota((1, 128), 1)
    mean = jnp.sum(each, axis=0, keepdims=True) * (1.0 / SEQ)
    off = each - mean
    between = jnp.sum(off * off, axis=0, keepdims=True) * (8.0 * count)
    within = mean * SEQ
    total = jnp.where(lane < GROUPS, between, jnp.where(lane < 2 * GROUPS, within, 0.0))
    mean = jnp.where(lane < GROUPS, mean, 0.0)
    spread = one_hot((iota((128, C), 0) & 31) == (iota((128, C), 1) >> 3))
    both = exact_dot(rows8(mean, total), spread)
    return both[0:1], lax.rsqrt(both[1:2] * (1.0 / (8.0 * count * SEQ)) + EPS)


def own_rows(place_ref, rows_ref, near_ref, far_ref):
    odd = place_ref[0] & 1
    near_ref[...] = rows_ref[pl.ds(pl.multiple_of((1 - odd) * ROW, ROW), ROW)].astype(BF16)
    far_ref[...] = rows_ref[pl.ds(pl.multiple_of(odd * ROW, ROW), ROW)].astype(BF16)


def split_kernel(
    place_ref, feat_hbm, gain_hbm, shift_hbm, scale_hbm, mod_hbm,
    rows_ref, near_ref, far_ref, stats_ref, norms_ref, mods_ref,
    feat_ref, gain_ref, shift_ref, scale_ref, mod_ref, wide, sems,
):
    sources = (feat_hbm, gain_hbm, shift_hbm, scale_hbm, mod_hbm)
    targets = (feat_ref, gain_ref, shift_ref, scale_ref, mod_ref)
    copies = [pltpu.make_async_copy(a, b, sems.at[i]) for i, (a, b) in enumerate(zip(sources, targets))]
    for copy in copies:
        copy.start()
    for copy in copies:
        copy.wait()
    norms_ref[0:3] = gain_ref[...]
    norms_ref[4:7] = shift_ref[...]
    mods_ref[0:1] = scale_ref[...]
    mods_ref[1:2] = mod_ref[...]
    cells = feat_ref[...].astype(F32).reshape(CELLS, C)
    for side in range(2):
        wide[side] = cells[:, side * 128 : (side + 1) * 128]
    for frame in range(FRAMES):
        for row in range(2):
            for parity in range(2):
                base = (frame * 2 + row) * 32 + parity
                at = row * ROW + (frame * 2 + parity) * HALF
                for side in range(2):
                    part = wide[side, pl.ds(base, HALF, stride=2)]
                    rows_ref[at : at + HALF, side * 128 : (side + 1) * 128] = part.astype(BF16)
    own_rows(place_ref, rows_ref, near_ref, far_ref)
    mean = jnp.sum(cells, axis=0, keepdims=True) * (1.0 / CELLS)
    off = cells - mean
    write_stats(mean, jnp.sum(off * off, axis=0, keepdims=True), CELLS, stats_ref)


def fill_window(place_ref, stats_ref, rows_ref, near_ref, far_ref, norms_ref, layer, window, centers=None, load=None):
    mean, rstd = read_stats(stats_ref, CELLS)
    gain = rstd * norms_ref[layer : layer + 1] * 0.5
    shift = norms_ref[4 + layer : 5 + layer] * 0.5
    place = place_ref[0]
    odd = place & 1
    near_at = 3 * (1 - odd)
    far_on = jnp.where((place > 0) & (place < SEQ - 1), 1.0, 0.0).astype(F32)
    window[:, 0:2] = jnp.zeros((4, 2, 4, HALF, C), BF16)
    step = 4
    n = step * HALF
    pair = iota((n, C), 0) & (HALF - 1)
    level = -mean
    levels = [level] * 4 if centers is None else [center + level for center in centers]
    sources = (
        (near_at, near_ref),
        (3 - near_at, far_ref),
        (1, rows_ref.at[0:ROW]),
        (2, rows_ref.at[ROW:CELLS]),
    )
    for which, (row, source) in enumerate(sources):
        if which == 2 and load is not None:
            load.wait()
        for frame in range(0, FRAMES, step):
            x = source[frame * 32 : (frame + step) * 32].astype(F32)
            half = (x + levels[which]) * gain + shift
            act = half + half * jnp.tanh(half)
            if which == 1:
                act = act * far_on
            act = act.reshape(step, 2, HALF, C)
            even = act[:, 0].reshape(n, C)
            odd_ones = act[:, 1].reshape(n, C)
            odd_before = jnp.where(pair == 0, 0.0, pltpu.roll(odd_ones, 1, 0))
            even_after = jnp.where(pair == HALF - 1, 0.0, pltpu.roll(even, n - 1, 0))
            for plane, part in enumerate((odd_before, even, odd_ones, even_after)):
                window[row, 2 + frame : 2 + frame + step, plane] = part.astype(BF16).reshape(
                    step, HALF, C
                )


TILE = 256


def start_weights(source, weight, sems):
    copies = [
        pltpu.make_async_copy(source.at[9 * p : 9 * p + 9], weight.at[9 * p : 9 * p + 9], sems.at[p])
        for p in range(3)
    ]
    for copy in copies:
        copy.start()
    return copies


def convolve(window, weight, copies, total, finish):
    for p in range(3):
        copies[p].wait()
        for tile in range(CELLS // TILE):
            row, frame = tile * TILE // ROW, tile * TILE % ROW // 32
            part = None
            for q in range(3):
                for r in range(3):
                    at = frame + p
                    cells = window[q + row, at : at + TILE // 32, r : r + 2].reshape(TILE, C)
                    term = dot(cells, weight[9 * p + 3 * q + r])
                    part = term if part is None else part + term
            rows = slice(tile * TILE, (tile + 1) * TILE)
            if p > 0:
                part = part + total[rows]
            if p < 2:
                total[rows] = part
            else:
                finish(rows, part)


class Moments:
    def __init__(self):
        self.center = self.first = self.second = None

    def add(self, tile):
        if self.center is None:
            self.center = jnp.sum(tile, axis=0, keepdims=True) * (1.0 / TILE)
        off = tile - self.center
        first = jnp.sum(off, axis=0, keepdims=True)
        second = jnp.sum(off * off, axis=0, keepdims=True)
        self.first = first if self.first is None else self.first + first
        self.second = second if self.second is None else self.second + second
        return off

    def write(self, stats_ref):
        gap = self.first * (1.0 / CELLS)
        square = jnp.maximum(self.second - self.first * gap, 0.0)
        write_stats(self.center + gap, square, CELLS, stats_ref)


def first_kernel(
    place_ref, stats_ref, rows_ref, near_ref, far_ref, norms_ref, weight_hbm,
    hidden_hbm, center_ref, near_out, far_out, stats_out, window, weight, total, hidden_ref, sems,
):
    copies = start_weights(weight_hbm, weight, sems)
    fill_window(place_ref, stats_ref, rows_ref, near_ref, far_ref, norms_ref, 0, window)
    moments = Moments()

    def finish(rows, tile):
        hidden_ref[rows] = moments.add(tile).astype(BF16)

    convolve(window, weight, copies, total, finish)
    copy = pltpu.make_async_copy(hidden_ref, hidden_hbm, sems.at[3])
    copy.start()
    center = moments.center
    center_ref[...] = jnp.broadcast_to(center, (8, C))
    high = center.astype(BF16).astype(F32)
    mid = (center - high).astype(BF16).astype(F32)
    line = iota((16, C), 0)
    terms = jnp.where(line == 0, high, jnp.where(line == 1, mid, jnp.where(line == 2, center - high - mid, 0.0)))
    own_rows(place_ref, hidden_ref, near_out.at[0:ROW], far_out.at[0:ROW])
    near_out[ROW : ROW + 16] = terms.astype(BF16)
    far_out[ROW : ROW + 16] = terms.astype(BF16)
    moments.write(stats_out)
    copy.wait()


def second_kernel(
    place_ref, stats_ref, hidden_hbm, center_ref, near_ref, far_ref, norms_ref, feat_ref, weight_hbm,
    block_ref, near_out, far_out, stats_out, window, weight, total, hidden_ref, sems,
):
    load = pltpu.make_async_copy(hidden_hbm, hidden_ref, sems.at[3])
    load.start()
    copies = start_weights(weight_hbm, weight, sems)
    own = center_ref[0:1]
    centers = [jnp.sum(ref[ROW : ROW + 16].astype(F32), axis=0, keepdims=True) for ref in (near_ref, far_ref)]
    centers += [own, own]
    fill_window(place_ref, stats_ref, hidden_ref, near_ref, far_ref, norms_ref, 1, window, centers, load)
    moments = Moments()

    def finish(rows, tile):
        block = (tile + feat_ref[rows].astype(F32)).astype(BF16)
        block_ref[rows] = block
        moments.add(block.astype(F32))

    convolve(window, weight, copies, total, finish)
    own_rows(place_ref, block_ref, near_out, far_out)
    moments.write(stats_out)


def column_to_row(column):
    square = jnp.broadcast_to(column, (128, 128))
    return jnp.sum(jnp.where(iota((128, 128), 0) == iota((128, 128), 1), square, 0.0), axis=0, keepdims=True)


def third_kernel(
    place_ref, stats_ref, rows_ref, near_ref, far_ref, norms_ref, weight_ref, embed_ref, bias_ref,
    own_ref, other_ref, patches_ref, parcel_ref, window, weight, folds,
):
    n = FRAMES * HALF
    for p in range(3):
        for row in range(4):
            for plane in range(4):
                block = (p * 4 + row) * 4 + plane
                for dh in range(2):
                    for dw in range(2):
                        at = (2 * dh + dw) * LAT
                        q, r = row - dh, plane - dw
                        if 0 <= q < 3 and 0 <= r < 3:
                            weight[block, at : at + LAT] = weight_ref[9 * p + 3 * q + r]
                        else:
                            weight[block, at : at + LAT] = jnp.zeros((LAT, C), BF16)
    fill_window(place_ref, stats_ref, rows_ref, near_ref, far_ref, norms_ref, 2, window)
    patches = None
    for p in range(3):
        for row in range(4):
            for plane in range(4):
                cells = window[row, p : p + FRAMES, plane].reshape(n, C)
                term = nt_dot(cells, weight[(p * 4 + row) * 4 + plane])
                patches = term if patches is None else patches + term
    patches_ref[...] = patches
    rounded = patches.astype(BF16)
    embedded = dot(jnp.concatenate([rounded, rounded], axis=1), embed_ref[...]) + bias_ref[0:1]
    spread = jnp.sum(embedded * embedded, axis=1, keepdims=True) * (1.0 / D)
    rstd = lax.rsqrt(spread + EPS)
    scaled = (rounded.astype(F32) * rstd).reshape(FRAMES, 2, 8, 64)
    rstd = jnp.broadcast_to(rstd, (n, 128)).reshape(FRAMES, 2, 8, 128)
    both = jnp.concatenate([scaled[:, side].reshape(128, 64) for side in range(2)], axis=1)
    parcel_ref[0:128] = both.astype(BF16)
    line = iota((16, 128), 0)
    lines = jnp.where(line == 4, 1.0, 0.0)
    for side in range(2):
        each = column_to_row(rstd[:, side].reshape(128, 128)[:, 0:1])
        high = each.astype(BF16).astype(F32)
        lines = jnp.where(line == 2 * side, high, lines)
        lines = jnp.where(line == 2 * side + 1, each - high, lines)
    parcel_ref[128:144] = lines.astype(BF16)
    own, other = own_ref[...].astype(F32), other_ref[...].astype(F32)
    lane = iota((4 * QROWS, 128), 1)
    parcel_ref[144:288] = jnp.where(lane < 64, own, pltpu.roll(other, 64, 1)).astype(BF16)
    folds[0 : 4 * QROWS] = own
    folds[4 * QROWS : 8 * QROWS] = other
    folds[8 * QROWS :] = jnp.zeros((8, 128), F32)
    lane = iota((40, 128), 1)
    ends = jnp.zeros((40, 128), F32)
    for i in range(8):
        ends = jnp.where((lane >> 3) == i, pltpu.roll(folds[i * QROWS : i * QROWS + 40], (8 * i + 64) % 128, 1), ends)
    parcel_ref[288:336] = jnp.concatenate([ends, jnp.zeros((8, 128), F32)], axis=0).astype(BF16)


def latent_kernel(patches_ref, latent_ref):
    n = FRAMES * HALF
    patches = patches_ref[...]
    turned = jnp.transpose(jnp.concatenate([patches, jnp.zeros_like(patches)], axis=1))
    out = None
    for dw in range(2):
        rows = jnp.concatenate([turned[(2 * dh + dw) * LAT : (2 * dh + dw + 1) * LAT] for dh in range(2)], axis=0)
        high = rows.astype(BF16).astype(F32)
        mid = (rows - high).astype(BF16).astype(F32)
        parts = jnp.concatenate([high, mid, rows - high - mid], axis=0).astype(BF16)
        column = iota((n, 2 * n), 1)
        spread = one_hot(column == iota((n, 2 * n), 0) * 2 + dw)
        term = dot(parts, spread)
        term = term[0:32] + term[32:64] + term[64:96]
        out = term if out is None else out + term
    for frame in range(FRAMES):
        for dh in range(2):
            latent_ref[frame, dh] = out[dh * LAT : (dh + 1) * LAT, frame * 32 : (frame + 1) * 32]


def fold_kernel(
    w0_ref, w1_ref, w2_ref, w3_ref, embed_ref, bias_ref, own_mods_ref, mods_ref,
    own_ref, other_ref, embed_out, bias_out, stacked, wide,
):
    embed = embed_ref[...].astype(F32)
    embed = embed - jnp.mean(embed, axis=1, keepdims=True)
    high = embed.astype(BF16)
    embed_out[0:64] = high
    embed_out[64:128] = (embed - high.astype(F32)).astype(BF16)
    center = bias_ref[...] - jnp.mean(bias_ref[...], axis=1, keepdims=True)
    bias_out[...] = jnp.broadcast_to(center, (8, D))
    for i in range(4):
        block = (w0_ref, w1_ref, w2_ref, w3_ref)[i][...].astype(F32)
        block = jnp.concatenate([block, jnp.zeros((QPAD - QROWS, D), F32)], axis=0)
        stacked[i * QPAD : (i + 1) * QPAD] = block.astype(BF16)
    row = iota((64, D), 0)
    sides = []
    for mod_ref in (own_mods_ref, mods_ref):
        scale, shift = 1.0 + mod_ref[0:1], mod_ref[1:2]
        bias = center * scale
        bias_high = bias.astype(BF16).astype(F32)
        shift_high = shift.astype(BF16).astype(F32)
        ends = jnp.where(row == 0, bias_high, jnp.where(row == 1, bias - bias_high, 0.0))
        ends = jnp.where(row == 2, shift_high, jnp.where(row == 3, shift - shift_high, ends))
        sides += [embed * scale, ends]
    every = jnp.concatenate(sides, axis=0).astype(BF16)
    out = nt_dot(stacked[...], every)
    lane = iota((4 * QPAD, 128), 1)
    for side, target in enumerate((own_ref, other_ref)):
        part = out[:, side * 128 : (side + 1) * 128]
        bias = part[:, 64:65] + part[:, 65:66]
        shift = part[:, 66:67] + part[:, 67:68]
        bias_high = bias.astype(BF16).astype(F32)
        shift_high = shift.astype(BF16).astype(F32)
        part = jnp.where((lane == 64) | (lane == 68), bias_high, part)
        part = jnp.where(lane == 65, bias - bias_high, part)
        part = jnp.where(lane == 66, shift_high, part)
        part = jnp.where(lane == 67, shift - shift_high, part)
        for i in range(4):
            wide[i * QROWS : (i + 1) * QROWS] = part[i * QPAD : i * QPAD + QROWS]
        target[...] = wide[...].astype(BF16)


WIDE = HEADS * HDIM


def sort_kernel(place_ref, clip_ref, near_ref, far_ref, asks_ref, keys_ref, values_ref, loose, wide):
    seq, clip = place_ref[0], clip_ref[0]
    spot = iota((40, 128), 1)
    for j in range(SEQ):
        source = (near_ref, far_ref)[j & 1]
        loose[j] = source[(j >> 1) & 3, j >> 3, 144:336].astype(F32)
        for k in range(CLIPS):
            at = ((clip ^ (2 * (k & 3) + (k >> 2))) * SEQ + (seq ^ j)) * QROWS
            block = loose[j, (k & 3) * QROWS : (k & 3) * QROWS + 40]
            block = pltpu.roll(block, 64, 1) if k >> 2 else block
            ends = pltpu.roll(loose[j, 144:184], (64 - 8 * k) % 128, 1)
            block = jnp.where(spot < 64, block, jnp.where(spot < 69, ends, 0.0))
            wide[pl.ds(at, QROWS)] = block[:QROWS]
    lane = iota((WIDE, 128), 1)
    rows = wide[0:WIDE]
    asks_ref[:, 0:128] = rows.astype(BF16)
    asks_ref[:, 128:256] = pltpu.roll(rows, 64, 1).astype(BF16)
    for part, target in ((1, keys_ref), (2, values_ref)):
        rows = wide[part * WIDE : (part + 1) * WIDE]
        bias = rows[:, 64:65] + rows[:, 65:66]
        shift = rows[:, 66:67] + rows[:, 67:68]
        left = jnp.where(lane < 64, rows, 0.0)
        target[:, 0:128] = left.astype(BF16)
        target[:, 256:384] = pltpu.roll(left, 64, 1).astype(BF16)
        for side in range(2):
            extra = jnp.where((lane == 2 * side) | (lane == 2 * side + 1), bias, 0.0)
            extra = jnp.where(lane == 4, shift, extra)
            target[:, 256 * side + 128 : 256 * side + 256] = extra.astype(BF16)


def attend_kernel(place_ref, near_ref, far_ref, asks_ref, keys_ref, values_ref, out_ref, queries, mixed, scores, weights):
    seq = place_ref[0]
    blocks = [(near_ref, far_ref)[j & 1].at[(j >> 1) & 3, j >> 3] for j in range(SEQ)]
    lane = iota((128, 128), 1)
    pick = one_hot(iota((8, 128), 1) == iota((8, 128), 0) + seq * 8)
    twin = pl.ds(pl.multiple_of((seq >> 1) * 16, 16), 16)
    tokens, scales = [], []
    for block in blocks:
        pair = block[twin].astype(F32)
        tokens.append(jnp.where((seq & 1) == 1, pair[8:16], pair[0:8]))
        scales.append(nt_dot(pick, block[128:144]))
    tokens = jnp.concatenate(tokens, axis=0)
    scales = jnp.concatenate(scales, axis=0)
    asked = []
    for side in range(2):
        high, low = scales[:, 2 * side : 2 * side + 1], scales[:, 2 * side + 1 : 2 * side + 2]
        spot = lane - 64 * (1 - side)
        own = jnp.where((lane >> 6) == side, tokens, 0.0)
        own = jnp.where((spot == 0) | (spot == 1), high, own)
        own = jnp.where((spot == 2) | (spot == 3), 1.0, own)
        own = jnp.where(spot == 4, low, own).astype(BF16)
        asked.append((nt_dot(own, asks_ref[:, 128 * side : 128 * side + 128]) * (1.0 / math.sqrt(HDIM))).astype(BF16))
    for head in range(HEADS):
        cols = slice(head * HDIM, (head + 1) * HDIM)
        keyed = [
            dot(asked[side][:, cols], keys_ref[cols, 256 * side : 256 * side + 256]).reshape(SEQ, 8, 256)
            for side in range(2)
        ]
        queries[:, head] = jnp.concatenate(keyed, axis=1).astype(BF16)
    n = HEADS * HALF
    same = jnp.where(iota((8, n), 0) == (iota((8, n), 1) & 7), 1.0, 0.0)
    for j, block in enumerate(blocks):
        query = queries[j].reshape(n, 256)
        ends = lax.dot_general(block[128:144], query[:, 128:144], (((0,), (1,)), ((), ())), preferred_element_type=F32)
        scores[j] = nt_dot(block[0:128], query[:, 0:128]) + ends
    for j in range(SEQ):
        each = scores[j].reshape(FRAMES, 8, n)
        raised = jnp.exp(each - jnp.max(each, axis=0, keepdims=True))
        shares = raised * (same / jnp.sum(raised, axis=0))
        weights[j] = jnp.transpose(shares.astype(BF16).reshape(128, n))
    for j, block in enumerate(blocks):
        mix = dot(weights[j], block[0:128]).reshape(HEADS, 2, 8, 128)
        ends = nt_dot(weights[j], block[128:144]).reshape(HEADS, 2, 8, 16)
        for side in range(2):
            mixed[side, :, j * 8 : (j + 1) * 8, 0:128] = mix[:, side]
            mixed[side, :, j * 8 : (j + 1) * 8, 128:144] = ends[:, side]
    for head in range(HEADS):
        cols = slice(head * HDIM, (head + 1) * HDIM)
        out = []
        for side in range(2):
            part = nt_dot(mixed[side, head, :, 0:128].astype(BF16), values_ref[cols, 256 * side : 256 * side + 128])
            at = 256 * side + 128
            part = part + nt_dot(mixed[side, head, :, 128:144].astype(BF16), values_ref[cols, at : at + 16])
            out.append(part.reshape(SEQ, 8, HDIM))
        out = jnp.concatenate(out, axis=1).astype(BF16)
        for j in range(SEQ):
            out_ref[pl.ds(pl.multiple_of((seq ^ j) * HALF, HALF), HALF), cols] = out[j]


def shape(*dims, dtype=BF16):
    return jax.ShapeDtypeStruct(dims, dtype)


def call(body, outs, ins, scratch=(), flops=0, moved=0, limit=32, first_out=VMEM):
    outs = list(outs) if isinstance(outs, list) else outs
    if first_out is HBM:
        outs[0] = pltpu.HBM(outs[0].shape, outs[0].dtype)
    kernel = pl.pallas_call(
        body,
        out_shape=outs,
        in_specs=ins,
        out_specs=[first_out] + [VMEM] * (len(outs) - 1) if isinstance(outs, list) else VMEM,
        scratch_shapes=list(scratch),
        compiler_params=pltpu.CompilerParams(vmem_limit_bytes=limit << 20),
        cost_estimate=pl.CostEstimate(flops=flops, bytes_accessed=moved, transcendentals=0),
        name=body.__name__,
    )

    def run(*args):
        return kernel(
            *(pltpu.with_memory_space_constraint(x, pltpu.HBM) if spec is HBM else x for x, spec in zip(args, ins))
        )

    return run


def swap(values, axis, bits, count):
    return lax.ppermute(values, axis, [(i, i ^ bits) for i in range(count)])


CHIP_PAIRS = [(i, i ^ 1) for i in range(SEQ)]
NEXT_PAIRS = [(i, (i + 1 if i & 1 else i - 1) % SEQ) for i in range(SEQ)]


def neighbours(near, far):
    far = lax.ppermute(far, "seq", NEXT_PAIRS)
    return lax.ppermute(near, "seq", CHIP_PAIRS), far


def exchange(stats):
    return lax.all_to_all(stats, "seq", 0, 0, tiled=True)


def gather_seq(block, beside):
    over = swap(block, "seq", 8, SEQ)
    over, beside = lax.optimization_barrier((over, beside))
    pair = jnp.stack([block, over])
    near = jnp.stack([pair] + [swap(pair, "seq", bits, SEQ) for bits in (2, 4, 6)])
    return near, swap(near, "seq", 1, SEQ), beside


WINDOW = pltpu.VMEM((4, FRAMES + 2, 4, HALF, C), BF16)
WEIGHT = pltpu.VMEM((27, C, C), BF16)
CONV_FLOPS = 2 * CELLS * 27 * C * C


def shards(
    features,
    first_conv,
    second_conv,
    out_conv,
    norm_gains,
    norm_shifts,
    embed_weight,
    embed_bias,
    mod_shift,
    mod_scale,
    qkv_weight,
):
    place = lax.axis_index("seq").astype(jnp.int32).reshape(1)
    clip = lax.axis_index("clip").astype(jnp.int32).reshape(1)
    row = shape(ROW, C)
    stats = shape(SEQ, 1, 128, dtype=F32)
    taps = 27

    cells = shape(CELLS, C)
    long_row = shape(ROW + 16, C)
    rows_f, near, far, stats0, norms, own_mods = call(
        split_kernel,
        [cells, row, row, stats, shape(8, C, dtype=F32), shape(2, D, dtype=F32)],
        [SMEM] + [HBM] * 5,
        [
            pltpu.VMEM((FRAMES, 2, 32, C), BF16),
            pltpu.VMEM((3, C), F32),
            pltpu.VMEM((3, C), F32),
            pltpu.VMEM((1, D), F32),
            pltpu.VMEM((1, D), F32),
            pltpu.VMEM((2, CELLS, 128), F32),
            DMA((5,)),
        ],
        0,
        1 << 20,
    )(place, features.reshape(FRAMES, 2, 32, C), norm_gains, norm_shifts, mod_scale, mod_shift)
    near, far = neighbours(near, far)
    mods = swap(own_mods, "clip", 1, CLIPS)
    stats0 = exchange(stats0)
    stats0, mods = lax.optimization_barrier((stats0, mods))
    stats0, mine = lax.optimization_barrier((stats0, qkv_weight))
    rows = [qkv_weight] + [swap(mine, "clip", bits, CLIPS) for bits in (2, 4, 6)]
    hidden, center, near_h, far_h, stats1 = call(
        first_kernel,
        [cells, shape(8, C, dtype=F32), long_row, long_row, stats],
        [SMEM] + [VMEM] * 5 + [HBM],
        [WINDOW, WEIGHT, pltpu.VMEM((CELLS, C), F32), pltpu.VMEM((CELLS, C), BF16), DMA((4,))],
        CONV_FLOPS,
        5 << 20,
        first_out=HBM,
    )(place, stats0, rows_f, near, far, norms, first_conv.reshape(taps, C, C))
    near, far = neighbours(near_h, far_h)

    stats1 = exchange(stats1)
    stats1, *rows = lax.optimization_barrier((stats1, *rows))

    block, near_b, far_b, stats2 = call(
        second_kernel,
        [cells, row, row, stats],
        [SMEM, VMEM, HBM] + [VMEM] * 5 + [HBM],
        [WINDOW, WEIGHT, pltpu.VMEM((CELLS, C), F32), pltpu.VMEM((CELLS, C), BF16), DMA((4,))],
        CONV_FLOPS,
        6 << 20,
    )(place, stats1, hidden, center, near, far, norms, rows_f, second_conv.reshape(taps, C, C))
    near, far = neighbours(near_b, far_b)
    stats2, *rows = lax.optimization_barrier((stats2, *rows))
    folded = shape(4 * QROWS, 128)
    own, other, embed, bias = call(
        fold_kernel,
        [folded, folded, shape(128, D), shape(8, D, dtype=F32)],
        [VMEM] * 8,
        [pltpu.VMEM((4 * QPAD, D), BF16), pltpu.VMEM((4 * QROWS, 128), F32)],
    )(*rows, embed_weight, embed_bias.reshape(1, D), own_mods, mods)
    other = swap(other, "clip", 1, CLIPS)
    stats2 = exchange(stats2)
    patches, parcel = call(
        third_kernel,
        [shape(FRAMES * HALF, 4 * LAT, dtype=F32), shape(336, 128)],
        [SMEM] + [VMEM] * 10,
        [WINDOW, pltpu.VMEM((48, 4 * LAT, C), BF16), pltpu.VMEM((8 * QROWS + 8, 128), F32)],
        CONV_FLOPS // 2,
        4 << 20,
    )(
        place, stats2, block, near, far, norms,
        out_conv.transpose(0, 1, 2, 4, 3).reshape(taps, LAT, C), embed, bias, own, other,
    )
    latent = call(latent_kernel, shape(FRAMES, 2, LAT, 2 * HALF, dtype=F32), [VMEM])(patches)
    near, far, latent = gather_seq(parcel, latent)
    asks, keys, values = call(
        sort_kernel,
        [shape(WIDE, 256), shape(WIDE, 512), shape(WIDE, 512)],
        [SMEM] * 2 + [VMEM] * 2,
        [pltpu.VMEM((SEQ, 192, 128), F32), pltpu.VMEM((3 * WIDE, 128), F32)],
    )(place, clip, near, far)
    frame_heads = call(
        attend_kernel,
        shape(SEQ * HALF, WIDE),
        [SMEM] + [VMEM] * 5,
        [
            pltpu.VMEM((SEQ, HEADS, HALF, 256), BF16),
            pltpu.VMEM((2, HEADS, 128, 256), F32),
            pltpu.VMEM((SEQ, 128, HEADS * HALF), F32),
            pltpu.VMEM((SEQ, HEADS * HALF, 128), BF16),
        ],
    )(place, near, far, asks, keys, values)
    latent = latent.transpose(0, 1, 3, 2).reshape(1, FRAMES, 2, 2 * HALF, LAT)
    return (latent, frame_heads.reshape(1, 1, SEQ * HALF, WIDE))


def solution(mesh):
    placed = (
        P("clip", None, "seq", None, None),
        P(),
        P(),
        P(),
        P(),
        P(),
        P(),
        P(),
        P("clip", None),
        P("clip", None),
        P(("clip", "seq"), None),
    )
    return jax.shard_map(
        shards,
        mesh=mesh,
        in_specs=placed,
        out_specs=(P("clip", None, "seq", None, None), P("clip", "seq", None, None)),
        check_vma=False,
    )
```

```python
import functools
import math

import jax
import jax.numpy as jnp
from jax import lax
from jax.experimental import pallas as pl
from jax.experimental.pallas import tpu as pltpu
from jax.sharding import PartitionSpec as P

C = 256
GROUPS = 32
LAT = 16
D = 3072
HEADS = 12
HDIM = 128
FRAMES = 16
HALF = 16
ROW = FRAMES * 2 * HALF
CELLS = 2 * ROW
SEQ = 16
CLIPS = 8
QROWS = 36
QPAD = 48
EPS = 1e-06
F32 = jnp.float32
BF16 = jnp.bfloat16
VMEM = pl.BlockSpec(memory_space=pltpu.VMEM)
SMEM = pl.BlockSpec(memory_space=pltpu.SMEM)
HBM = pl.BlockSpec(memory_space=pltpu.HBM)
DMA = pltpu.SemaphoreType.DMA


def nt_dot(a, b):
    return lax.dot_general(a, b, (((1,), (1,)), ((), ())), preferred_element_type=F32)


def dot(a, b):
    return jnp.dot(a, b, preferred_element_type=F32)


def exact_dot(rows, zero_one):
    high = rows.astype(BF16).astype(F32)
    rest = rows - high
    mid = rest.astype(BF16).astype(F32)
    low = rest - mid
    parts = jnp.concatenate([high, mid, low, jnp.zeros_like(low)], axis=0).astype(BF16)
    out = dot(parts, zero_one)
    return out[0:8] + out[8:16] + out[16:24]


def iota(shape, dim):
    return lax.broadcasted_iota(jnp.int32, shape, dim)


def one_hot(cond):
    return jnp.where(cond, 1.0, 0.0).astype(BF16)


def rows8(first, second=None):
    n = first.shape[1]
    row = iota((8, n), 0)
    out = jnp.where(row == 0, jnp.broadcast_to(first, (8, n)), 0.0)
    if second is not None:
        out = jnp.where(row == 1, jnp.broadcast_to(second, (8, n)), out)
    return out


def write_stats(mean_c, square_c, count, stats_ref):
    same = one_hot((iota((C, C), 0) >> 3) == (iota((C, C), 1) >> 3))
    mean_g = exact_dot(rows8(mean_c), same)[0:1] * (1.0 / 8)
    gap = mean_c - mean_g
    square_c = square_c + count * (gap * gap)
    lane = iota((C, 128), 1)
    pick = one_hot((iota((C, 128), 0) >> 3) == (lane & 31))
    both = exact_dot(rows8(mean_c * (1.0 / 8), square_c), pick)
    row = jnp.where(iota((1, 128), 1) < GROUPS, both[0:1], both[1:2])
    stats_ref[...] = jnp.broadcast_to(row[None], (SEQ, 1, 128))


def read_stats(stats_ref, count):
    each = stats_ref[...].reshape(SEQ, 128)
    lane = iota((1, 128), 1)
    mean = jnp.sum(each, axis=0, keepdims=True) * (1.0 / SEQ)
    off = each - mean
    between = jnp.sum(off * off, axis=0, keepdims=True) * (8.0 * count)
    within = mean * SEQ
    total = jnp.where(lane < GROUPS, between, jnp.where(lane < 2 * GROUPS, within, 0.0))
    mean = jnp.where(lane < GROUPS, mean, 0.0)
    spread = one_hot((iota((128, C), 0) & 31) == (iota((128, C), 1) >> 3))
    both = exact_dot(rows8(mean, total), spread)
    return both[0:1], lax.rsqrt(both[1:2] * (1.0 / (8.0 * count * SEQ)) + EPS)


def own_rows(place_ref, rows_ref, near_ref, far_ref):
    odd = place_ref[0] & 1
    near_ref[...] = rows_ref[pl.ds(pl.multiple_of((1 - odd) * ROW, ROW), ROW)].astype(BF16)
    far_ref[...] = rows_ref[pl.ds(pl.multiple_of(odd * ROW, ROW), ROW)].astype(BF16)


def split_kernel(
    place_ref, feat_hbm, gain_hbm, shift_hbm, scale_hbm, mod_hbm,
    rows_ref, near_ref, far_ref, stats_ref, norms_ref, mods_ref,
    feat_ref, gain_ref, shift_ref, scale_ref, mod_ref, wide, sems,
):
    sources = (feat_hbm, gain_hbm, shift_hbm, scale_hbm, mod_hbm)
    targets = (feat_ref, gain_ref, shift_ref, scale_ref, mod_ref)
    copies = [pltpu.make_async_copy(a, b, sems.at[i]) for i, (a, b) in enumerate(zip(sources, targets))]
    for copy in copies:
        copy.start()
    for copy in copies:
        copy.wait()
    norms_ref[0:3] = gain_ref[...]
    norms_ref[4:7] = shift_ref[...]
    mods_ref[0:1] = scale_ref[...]
    mods_ref[1:2] = mod_ref[...]
    cells = feat_ref[...].astype(F32).reshape(CELLS, C)
    for side in range(2):
        wide[side] = cells[:, side * 128 : (side + 1) * 128]
    for frame in range(FRAMES):
        for row in range(2):
            for parity in range(2):
                base = (frame * 2 + row) * 32 + parity
                at = row * ROW + (frame * 2 + parity) * HALF
                for side in range(2):
                    part = wide[side, pl.ds(base, HALF, stride=2)]
                    rows_ref[at : at + HALF, side * 128 : (side + 1) * 128] = part.astype(BF16)
    own_rows(place_ref, rows_ref, near_ref, far_ref)
    mean = jnp.sum(cells, axis=0, keepdims=True) * (1.0 / CELLS)
    off = cells - mean
    write_stats(mean, jnp.sum(off * off, axis=0, keepdims=True), CELLS, stats_ref)


def fill_window(place_ref, stats_ref, rows_ref, near_ref, far_ref, norms_ref, layer, window, centers=None, load=None):
    mean, rstd = read_stats(stats_ref, CELLS)
    gain = rstd * norms_ref[layer : layer + 1] * 0.5
    shift = norms_ref[4 + layer : 5 + layer] * 0.5
    place = place_ref[0]
    odd = place & 1
    near_at = 3 * (1 - odd)
    far_on = jnp.where((place > 0) & (place < SEQ - 1), 1.0, 0.0).astype(F32)
    window[:, 0:2] = jnp.zeros((4, 2, 4, HALF, C), BF16)
    step = 4
    n = step * HALF
    pair = iota((n, C), 0) & (HALF - 1)
    level = -mean
    levels = [level] * 4 if centers is None else [center + level for center in centers]
    sources = (
        (near_at, near_ref),
        (3 - near_at, far_ref),
        (1, rows_ref.at[0:ROW]),
        (2, rows_ref.at[ROW:CELLS]),
    )
    for which, (row, source) in enumerate(sources):
        if which == 2 and load is not None:
            load.wait()
        for frame in range(0, FRAMES, step):
            x = source[frame * 32 : (frame + step) * 32].astype(F32)
            half = (x + levels[which]) * gain + shift
            act = half + half * jnp.tanh(half)
            if which == 1:
                act = act * far_on
            act = act.reshape(step, 2, HALF, C)
            even = act[:, 0].reshape(n, C)
            odd_ones = act[:, 1].reshape(n, C)
            odd_before = jnp.where(pair == 0, 0.0, pltpu.roll(odd_ones, 1, 0))
            even_after = jnp.where(pair == HALF - 1, 0.0, pltpu.roll(even, n - 1, 0))
            for plane, part in enumerate((odd_before, even, odd_ones, even_after)):
                window[row, 2 + frame : 2 + frame + step, plane] = part.astype(BF16).reshape(
                    step, HALF, C
                )


TILE = 256


def start_weights(source, weight, sems):
    copies = [
        pltpu.make_async_copy(source.at[9 * p : 9 * p + 9], weight.at[9 * p : 9 * p + 9], sems.at[p])
        for p in range(3)
    ]
    for copy in copies:
        copy.start()
    return copies


def convolve(window, weight, copies, total, finish):
    for p in range(3):
        copies[p].wait()
        for tile in range(CELLS // TILE):
            row, frame = tile * TILE // ROW, tile * TILE % ROW // 32
            part = None
            for q in range(3):
                for r in range(3):
                    at = frame + p
                    cells = window[q + row, at : at + TILE // 32, r : r + 2].reshape(TILE, C)
                    term = dot(cells, weight[9 * p + 3 * q + r])
                    part = term if part is None else part + term
            rows = slice(tile * TILE, (tile + 1) * TILE)
            if p > 0:
                part = part + total[rows]
            if p < 2:
                total[rows] = part
            else:
                finish(rows, part)


class Moments:
    def __init__(self):
        self.center = self.first = self.second = None

    def add(self, tile):
        if self.center is None:
            self.center = jnp.sum(tile, axis=0, keepdims=True) * (1.0 / TILE)
        off = tile - self.center
        first = jnp.sum(off, axis=0, keepdims=True)
        second = jnp.sum(off * off, axis=0, keepdims=True)
        self.first = first if self.first is None else self.first + first
        self.second = second if self.second is None else self.second + second
        return off

    def write(self, stats_ref):
        gap = self.first * (1.0 / CELLS)
        square = jnp.maximum(self.second - self.first * gap, 0.0)
        write_stats(self.center + gap, square, CELLS, stats_ref)


def first_kernel(
    place_ref, stats_ref, rows_ref, near_ref, far_ref, norms_ref, weight_hbm,
    hidden_hbm, center_ref, near_out, far_out, stats_out, window, weight, total, hidden_ref, sems,
):
    copies = start_weights(weight_hbm, weight, sems)
    fill_window(place_ref, stats_ref, rows_ref, near_ref, far_ref, norms_ref, 0, window)
    moments = Moments()

    def finish(rows, tile):
        hidden_ref[rows] = moments.add(tile).astype(BF16)

    convolve(window, weight, copies, total, finish)
    copy = pltpu.make_async_copy(hidden_ref, hidden_hbm, sems.at[3])
    copy.start()
    center = moments.center
    center_ref[...] = jnp.broadcast_to(center, (8, C))
    high = center.astype(BF16).astype(F32)
    mid = (center - high).astype(BF16).astype(F32)
    line = iota((16, C), 0)
    terms = jnp.where(line == 0, high, jnp.where(line == 1, mid, jnp.where(line == 2, center - high - mid, 0.0)))
    own_rows(place_ref, hidden_ref, near_out.at[0:ROW], far_out.at[0:ROW])
    near_out[ROW : ROW + 16] = terms.astype(BF16)
    far_out[ROW : ROW + 16] = terms.astype(BF16)
    moments.write(stats_out)
    copy.wait()


def second_kernel(
    place_ref, stats_ref, hidden_hbm, center_ref, near_ref, far_ref, norms_ref, feat_ref, weight_hbm,
    block_ref, near_out, far_out, stats_out, window, weight, total, hidden_ref, sems,
):
    load = pltpu.make_async_copy(hidden_hbm, hidden_ref, sems.at[3])
    load.start()
    copies = start_weights(weight_hbm, weight, sems)
    own = center_ref[0:1]
    centers = [jnp.sum(ref[ROW : ROW + 16].astype(F32), axis=0, keepdims=True) for ref in (near_ref, far_ref)]
    centers += [own, own]
    fill_window(place_ref, stats_ref, hidden_ref, near_ref, far_ref, norms_ref, 1, window, centers, load)
    moments = Moments()

    def finish(rows, tile):
        block = (tile + feat_ref[rows].astype(F32)).astype(BF16)
        block_ref[rows] = block
        moments.add(block.astype(F32))

    convolve(window, weight, copies, total, finish)
    own_rows(place_ref, block_ref, near_out, far_out)
    moments.write(stats_out)


def column_to_row(column):
    square = jnp.broadcast_to(column, (128, 128))
    return jnp.sum(jnp.where(iota((128, 128), 0) == iota((128, 128), 1), square, 0.0), axis=0, keepdims=True)


def third_kernel(
    place_ref, stats_ref, rows_ref, near_ref, far_ref, norms_ref, weight_ref, embed_ref, bias_ref,
    own_ref, other_ref, patches_ref, parcel_ref, window, weight, folds,
):
    n = FRAMES * HALF
    for p in range(3):
        for row in range(4):
            for plane in range(4):
                block = (p * 4 + row) * 4 + plane
                for dh in range(2):
                    for dw in range(2):
                        at = (2 * dh + dw) * LAT
                        q, r = row - dh, plane - dw
                        if 0 <= q < 3 and 0 <= r < 3:
                            weight[block, at : at + LAT] = weight_ref[9 * p + 3 * q + r]
                        else:
                            weight[block, at : at + LAT] = jnp.zeros((LAT, C), BF16)
    fill_window(place_ref, stats_ref, rows_ref, near_ref, far_ref, norms_ref, 2, window)
    patches = None
    for p in range(3):
        for row in range(4):
            for plane in range(4):
                cells = window[row, p : p + FRAMES, plane].reshape(n, C)
                term = nt_dot(cells, weight[(p * 4 + row) * 4 + plane])
                patches = term if patches is None else patches + term
    patches_ref[...] = patches
    rounded = patches.astype(BF16)
    embedded = dot(jnp.concatenate([rounded, rounded], axis=1), embed_ref[...]) + bias_ref[0:1]
    spread = jnp.sum(embedded * embedded, axis=1, keepdims=True) * (1.0 / D)
    rstd = lax.rsqrt(spread + EPS)
    scaled = (rounded.astype(F32) * rstd).reshape(FRAMES, 2, 8, 64)
    rstd = jnp.broadcast_to(rstd, (n, 128)).reshape(FRAMES, 2, 8, 128)
    both = jnp.concatenate([scaled[:, side].reshape(128, 64) for side in range(2)], axis=1)
    parcel_ref[0:128] = both.astype(BF16)
    line = iota((16, 128), 0)
    lines = jnp.where(line == 4, 1.0, 0.0)
    for side in range(2):
        each = column_to_row(rstd[:, side].reshape(128, 128)[:, 0:1])
        high = each.astype(BF16).astype(F32)
        lines = jnp.where(line == 2 * side, high, lines)
        lines = jnp.where(line == 2 * side + 1, each - high, lines)
    parcel_ref[128:144] = lines.astype(BF16)
    own, other = own_ref[...].astype(F32), other_ref[...].astype(F32)
    lane = iota((4 * QROWS, 128), 1)
    parcel_ref[144:288] = jnp.where(lane < 64, own, pltpu.roll(other, 64, 1)).astype(BF16)
    folds[0 : 4 * QROWS] = own
    folds[4 * QROWS : 8 * QROWS] = other
    folds[8 * QROWS :] = jnp.zeros((8, 128), F32)
    lane = iota((40, 128), 1)
    ends = jnp.zeros((40, 128), F32)
    for i in range(8):
        ends = jnp.where((lane >> 3) == i, pltpu.roll(folds[i * QROWS : i * QROWS + 40], (8 * i + 64) % 128, 1), ends)
    parcel_ref[288:336] = jnp.concatenate([ends, jnp.zeros((8, 128), F32)], axis=0).astype(BF16)


def latent_kernel(patches_ref, latent_ref):
    n = FRAMES * HALF
    patches = patches_ref[...]
    turned = jnp.transpose(jnp.concatenate([patches, jnp.zeros_like(patches)], axis=1))
    out = None
    for dw in range(2):
        rows = jnp.concatenate([turned[(2 * dh + dw) * LAT : (2 * dh + dw + 1) * LAT] for dh in range(2)], axis=0)
        high = rows.astype(BF16).astype(F32)
        mid = (rows - high).astype(BF16).astype(F32)
        parts = jnp.concatenate([high, mid, rows - high - mid], axis=0).astype(BF16)
        column = iota((n, 2 * n), 1)
        spread = one_hot(column == iota((n, 2 * n), 0) * 2 + dw)
        term = dot(parts, spread)
        term = term[0:32] + term[32:64] + term[64:96]
        out = term if out is None else out + term
    for frame in range(FRAMES):
        for dh in range(2):
            latent_ref[frame, dh] = out[dh * LAT : (dh + 1) * LAT, frame * 32 : (frame + 1) * 32]


def fold_kernel(
    w0_ref, w1_ref, w2_ref, w3_ref, embed_ref, bias_ref, own_mods_ref, mods_ref,
    own_ref, other_ref, embed_out, bias_out, stacked, wide,
):
    embed = embed_ref[...].astype(F32)
    embed = embed - jnp.mean(embed, axis=1, keepdims=True)
    high = embed.astype(BF16)
    embed_out[0:64] = high
    embed_out[64:128] = (embed - high.astype(F32)).astype(BF16)
    center = bias_ref[...] - jnp.mean(bias_ref[...], axis=1, keepdims=True)
    bias_out[...] = jnp.broadcast_to(center, (8, D))
    for i in range(4):
        block = (w0_ref, w1_ref, w2_ref, w3_ref)[i][...].astype(F32)
        block = jnp.concatenate([block, jnp.zeros((QPAD - QROWS, D), F32)], axis=0)
        stacked[i * QPAD : (i + 1) * QPAD] = block.astype(BF16)
    row = iota((64, D), 0)
    sides = []
    for mod_ref in (own_mods_ref, mods_ref):
        scale, shift = 1.0 + mod_ref[0:1], mod_ref[1:2]
        bias = center * scale
        bias_high = bias.astype(BF16).astype(F32)
        shift_high = shift.astype(BF16).astype(F32)
        ends = jnp.where(row == 0, bias_high, jnp.where(row == 1, bias - bias_high, 0.0))
        ends = jnp.where(row == 2, shift_high, jnp.where(row == 3, shift - shift_high, ends))
        sides += [embed * scale, ends]
    every = jnp.concatenate(sides, axis=0).astype(BF16)
    out = nt_dot(stacked[...], every)
    lane = iota((4 * QPAD, 128), 1)
    for side, target in enumerate((own_ref, other_ref)):
        part = out[:, side * 128 : (side + 1) * 128]
        bias = part[:, 64:65] + part[:, 65:66]
        shift = part[:, 66:67] + part[:, 67:68]
        bias_high = bias.astype(BF16).astype(F32)
        shift_high = shift.astype(BF16).astype(F32)
        part = jnp.where((lane == 64) | (lane == 68), bias_high, part)
        part = jnp.where(lane == 65, bias - bias_high, part)
        part = jnp.where(lane == 66, shift_high, part)
        part = jnp.where(lane == 67, shift - shift_high, part)
        for i in range(4):
            wide[i * QROWS : (i + 1) * QROWS] = part[i * QPAD : i * QPAD + QROWS]
        target[...] = wide[...].astype(BF16)


WIDE = HEADS * HDIM


def sort_kernel(place_ref, clip_ref, *refs):
    asks_ref, keys_ref, values_ref, loose, wide = refs[8:]
    seq, clip = place_ref[0], clip_ref[0]
    spot = iota((40, 128), 1)
    for j in range(SEQ):
        loose[j] = refs[4 * (j & 1) + ((j >> 1) & 3)][j >> 3, 144:336].astype(F32)
        for k in range(CLIPS):
            at = ((clip ^ (2 * (k & 3) + (k >> 2))) * SEQ + (seq ^ j)) * QROWS
            block = loose[j, (k & 3) * QROWS : (k & 3) * QROWS + 40]
            block = pltpu.roll(block, 64, 1) if k >> 2 else block
            ends = pltpu.roll(loose[j, 144:184], (64 - 8 * k) % 128, 1)
            block = jnp.where(spot < 64, block, jnp.where(spot < 69, ends, 0.0))
            wide[pl.ds(at, QROWS)] = block[:QROWS]
    lane = iota((WIDE, 128), 1)
    rows = wide[0:WIDE]
    asks_ref[:, 0:128] = rows.astype(BF16)
    asks_ref[:, 128:256] = pltpu.roll(rows, 64, 1).astype(BF16)
    for part, target in ((1, keys_ref), (2, values_ref)):
        rows = wide[part * WIDE : (part + 1) * WIDE]
        bias = rows[:, 64:65] + rows[:, 65:66]
        shift = rows[:, 66:67] + rows[:, 67:68]
        left = jnp.where(lane < 64, rows, 0.0)
        target[:, 0:128] = left.astype(BF16)
        target[:, 256:384] = pltpu.roll(left, 64, 1).astype(BF16)
        for side in range(2):
            extra = jnp.where((lane == 2 * side) | (lane == 2 * side + 1), bias, 0.0)
            extra = jnp.where(lane == 4, shift, extra)
            target[:, 256 * side + 128 : 256 * side + 256] = extra.astype(BF16)


def attend_kernel(place_ref, *refs):
    asks_ref, keys_ref, values_ref, out_ref, queries, mixed, scores, weights = refs[8:]
    seq = place_ref[0]
    blocks = [refs[4 * (j & 1) + ((j >> 1) & 3)].at[j >> 3] for j in range(SEQ)]
    lane = iota((128, 128), 1)
    pick = one_hot(iota((8, 128), 1) == iota((8, 128), 0) + seq * 8)
    twin = pl.ds(pl.multiple_of((seq >> 1) * 16, 16), 16)
    tokens, scales = [], []
    for block in blocks:
        pair = block[twin].astype(F32)
        tokens.append(jnp.where((seq & 1) == 1, pair[8:16], pair[0:8]))
        scales.append(nt_dot(pick, block[128:144]))
    tokens = jnp.concatenate(tokens, axis=0)
    scales = jnp.concatenate(scales, axis=0)
    asked = []
    for side in range(2):
        high, low = scales[:, 2 * side : 2 * side + 1], scales[:, 2 * side + 1 : 2 * side + 2]
        spot = lane - 64 * (1 - side)
        own = jnp.where((lane >> 6) == side, tokens, 0.0)
        own = jnp.where((spot == 0) | (spot == 1), high, own)
        own = jnp.where((spot == 2) | (spot == 3), 1.0, own)
        own = jnp.where(spot == 4, low, own).astype(BF16)
        asked.append((nt_dot(own, asks_ref[:, 128 * side : 128 * side + 128]) * (1.0 / math.sqrt(HDIM))).astype(BF16))
    for head in range(HEADS):
        cols = slice(head * HDIM, (head + 1) * HDIM)
        keyed = [
            dot(asked[side][:, cols], keys_ref[cols, 256 * side : 256 * side + 256]).reshape(SEQ, 8, 256)
            for side in range(2)
        ]
        queries[:, head] = jnp.concatenate(keyed, axis=1).astype(BF16)
    n = HEADS * HALF
    same = jnp.where(iota((8, n), 0) == (iota((8, n), 1) & 7), 1.0, 0.0)
    for j, block in enumerate(blocks):
        query = queries[j].reshape(n, 256)
        ends = lax.dot_general(block[128:144], query[:, 128:144], (((0,), (1,)), ((), ())), preferred_element_type=F32)
        scores[j] = nt_dot(block[0:128], query[:, 0:128]) + ends
    for j in range(SEQ):
        each = scores[j].reshape(FRAMES, 8, n)
        raised = jnp.exp(each - jnp.max(each, axis=0, keepdims=True))
        shares = raised * (same / jnp.sum(raised, axis=0))
        weights[j] = jnp.transpose(shares.astype(BF16).reshape(128, n))
    for j, block in enumerate(blocks):
        mix = dot(weights[j], block[0:128]).reshape(HEADS, 2, 8, 128)
        ends = nt_dot(weights[j], block[128:144]).reshape(HEADS, 2, 8, 16)
        for side in range(2):
            mixed[side, :, j * 8 : (j + 1) * 8, 0:128] = mix[:, side]
            mixed[side, :, j * 8 : (j + 1) * 8, 128:144] = ends[:, side]
    for head in range(HEADS):
        cols = slice(head * HDIM, (head + 1) * HDIM)
        out = []
        for side in range(2):
            part = nt_dot(mixed[side, head, :, 0:128].astype(BF16), values_ref[cols, 256 * side : 256 * side + 128])
            at = 256 * side + 128
            part = part + nt_dot(mixed[side, head, :, 128:144].astype(BF16), values_ref[cols, at : at + 16])
            out.append(part.reshape(SEQ, 8, HDIM))
        out = jnp.concatenate(out, axis=1).astype(BF16)
        for j in range(SEQ):
            out_ref[pl.ds(pl.multiple_of((seq ^ j) * HALF, HALF), HALF), cols] = out[j]


def shape(*dims, dtype=BF16):
    return jax.ShapeDtypeStruct(dims, dtype)


def call(body, outs, ins, scratch=(), flops=0, moved=0, limit=32, first_out=VMEM):
    outs = list(outs) if isinstance(outs, list) else outs
    if first_out is HBM:
        outs[0] = pltpu.HBM(outs[0].shape, outs[0].dtype)
    kernel = pl.pallas_call(
        body,
        out_shape=outs,
        in_specs=ins,
        out_specs=[first_out] + [VMEM] * (len(outs) - 1) if isinstance(outs, list) else VMEM,
        scratch_shapes=list(scratch),
        compiler_params=pltpu.CompilerParams(vmem_limit_bytes=limit << 20),
        cost_estimate=pl.CostEstimate(flops=flops, bytes_accessed=moved, transcendentals=0),
        name=body.__name__,
    )

    def run(*args):
        return kernel(
            *(pltpu.with_memory_space_constraint(x, pltpu.HBM) if spec is HBM else x for x, spec in zip(args, ins))
        )

    return run


def swap(values, axis, bits, count):
    return lax.ppermute(values, axis, [(i, i ^ bits) for i in range(count)])


CHIP_PAIRS = [(i, i ^ 1) for i in range(SEQ)]
NEXT_PAIRS = [(i, (i + 1 if i & 1 else i - 1) % SEQ) for i in range(SEQ)]


def neighbours(near, far):
    far = lax.ppermute(far, "seq", NEXT_PAIRS)
    return lax.ppermute(near, "seq", CHIP_PAIRS), far


def exchange(stats):
    return lax.all_to_all(stats, "seq", 0, 0, tiled=True)


def gather_seq(block, beside):
    over = swap(block, "seq", 8, SEQ)
    over, beside = lax.optimization_barrier((over, beside))
    pair = jnp.stack([block, over])
    near = [pair] + [swap(pair, "seq", bits, SEQ) for bits in (2, 4, 6)]
    return near + [swap(x, "seq", 1, SEQ) for x in near], beside


WINDOW = pltpu.VMEM((4, FRAMES + 2, 4, HALF, C), BF16)
WEIGHT = pltpu.VMEM((27, C, C), BF16)
CONV_FLOPS = 2 * CELLS * 27 * C * C


def shards(
    features,
    first_conv,
    second_conv,
    out_conv,
    norm_gains,
    norm_shifts,
    embed_weight,
    embed_bias,
    mod_shift,
    mod_scale,
    qkv_weight,
):
    place = lax.axis_index("seq").astype(jnp.int32).reshape(1)
    clip = lax.axis_index("clip").astype(jnp.int32).reshape(1)
    row = shape(ROW, C)
    stats = shape(SEQ, 1, 128, dtype=F32)
    taps = 27

    cells = shape(CELLS, C)
    long_row = shape(ROW + 16, C)
    rows_f, near, far, stats0, norms, own_mods = call(
        split_kernel,
        [cells, row, row, stats, shape(8, C, dtype=F32), shape(2, D, dtype=F32)],
        [SMEM] + [HBM] * 5,
        [
            pltpu.VMEM((FRAMES, 2, 32, C), BF16),
            pltpu.VMEM((3, C), F32),
            pltpu.VMEM((3, C), F32),
            pltpu.VMEM((1, D), F32),
            pltpu.VMEM((1, D), F32),
            pltpu.VMEM((2, CELLS, 128), F32),
            DMA((5,)),
        ],
        0,
        1 << 20,
    )(place, features.reshape(FRAMES, 2, 32, C), norm_gains, norm_shifts, mod_scale, mod_shift)
    near, far = neighbours(near, far)
    mods = swap(own_mods, "clip", 1, CLIPS)
    stats0 = exchange(stats0)
    stats0, mods = lax.optimization_barrier((stats0, mods))
    stats0, mine = lax.optimization_barrier((stats0, qkv_weight))
    rows = [qkv_weight] + [swap(mine, "clip", bits, CLIPS) for bits in (2, 4, 6)]
    hidden, center, near_h, far_h, stats1 = call(
        first_kernel,
        [cells, shape(8, C, dtype=F32), long_row, long_row, stats],
        [SMEM] + [VMEM] * 5 + [HBM],
        [WINDOW, WEIGHT, pltpu.VMEM((CELLS, C), F32), pltpu.VMEM((CELLS, C), BF16), DMA((4,))],
        CONV_FLOPS,
        5 << 20,
        first_out=HBM,
    )(place, stats0, rows_f, near, far, norms, first_conv.reshape(taps, C, C))
    near, far = neighbours(near_h, far_h)

    stats1 = exchange(stats1)
    stats1, *rows = lax.optimization_barrier((stats1, *rows))

    block, near_b, far_b, stats2 = call(
        second_kernel,
        [cells, row, row, stats],
        [SMEM, VMEM, HBM] + [VMEM] * 5 + [HBM],
        [WINDOW, WEIGHT, pltpu.VMEM((CELLS, C), F32), pltpu.VMEM((CELLS, C), BF16), DMA((4,))],
        CONV_FLOPS,
        6 << 20,
    )(place, stats1, hidden, center, near, far, norms, rows_f, second_conv.reshape(taps, C, C))
    near, far = neighbours(near_b, far_b)
    stats2, *rows = lax.optimization_barrier((stats2, *rows))
    folded = shape(4 * QROWS, 128)
    own, other, embed, bias = call(
        fold_kernel,
        [folded, folded, shape(128, D), shape(8, D, dtype=F32)],
        [VMEM] * 8,
        [pltpu.VMEM((4 * QPAD, D), BF16), pltpu.VMEM((4 * QROWS, 128), F32)],
    )(*rows, embed_weight, embed_bias.reshape(1, D), own_mods, mods)
    other = swap(other, "clip", 1, CLIPS)
    stats2 = exchange(stats2)
    patches, parcel = call(
        third_kernel,
        [shape(FRAMES * HALF, 4 * LAT, dtype=F32), shape(336, 128)],
        [SMEM] + [VMEM] * 10,
        [WINDOW, pltpu.VMEM((48, 4 * LAT, C), BF16), pltpu.VMEM((8 * QROWS + 8, 128), F32)],
        CONV_FLOPS // 2,
        4 << 20,
    )(
        place, stats2, block, near, far, norms,
        out_conv.transpose(0, 1, 2, 4, 3).reshape(taps, LAT, C), embed, bias, own, other,
    )
    latent = call(latent_kernel, shape(FRAMES, 2, LAT, 2 * HALF, dtype=F32), [VMEM])(patches)
    parcels, latent = gather_seq(parcel, latent)
    asks, keys, values = call(
        sort_kernel,
        [shape(WIDE, 256), shape(WIDE, 512), shape(WIDE, 512)],
        [SMEM] * 2 + [VMEM] * 8,
        [pltpu.VMEM((SEQ, 192, 128), F32), pltpu.VMEM((3 * WIDE, 128), F32)],
    )(place, clip, *parcels)
    frame_heads = call(
        attend_kernel,
        shape(SEQ * HALF, WIDE),
        [SMEM] + [VMEM] * 11,
        [
            pltpu.VMEM((SEQ, HEADS, HALF, 256), BF16),
            pltpu.VMEM((2, HEADS, 128, 256), F32),
            pltpu.VMEM((SEQ, 128, HEADS * HALF), F32),
            pltpu.VMEM((SEQ, HEADS * HALF, 128), BF16),
        ],
    )(place, *parcels, asks, keys, values)
    latent = latent.transpose(0, 1, 3, 2).reshape(1, FRAMES, 2, 2 * HALF, LAT)
    return (latent, frame_heads.reshape(1, 1, SEQ * HALF, WIDE))


def solution(mesh):
    placed = (
        P("clip", None, "seq", None, None),
        P(),
        P(),
        P(),
        P(),
        P(),
        P(),
        P(),
        P("clip", None),
        P("clip", None),
        P(("clip", "seq"), None),
    )
    return jax.shard_map(
        shards,
        mesh=mesh,
        in_specs=placed,
        out_specs=(P("clip", None, "seq", None, None), P("clip", "seq", None, None)),
        check_vma=False,
    )
```

```python
import functools
import math

import jax
import jax.numpy as jnp
from jax import lax
from jax.experimental import pallas as pl
from jax.experimental.pallas import tpu as pltpu
from jax.sharding import PartitionSpec as P

C = 256
GROUPS = 32
LAT = 16
D = 3072
HEADS = 12
HDIM = 128
FRAMES = 16
HALF = 16
ROW = FRAMES * 2 * HALF
CELLS = 2 * ROW
SEQ = 16
CLIPS = 8
QROWS = 36
QPAD = 48
EPS = 1e-06
F32 = jnp.float32
BF16 = jnp.bfloat16
VMEM = pl.BlockSpec(memory_space=pltpu.VMEM)
SMEM = pl.BlockSpec(memory_space=pltpu.SMEM)
HBM = pl.BlockSpec(memory_space=pltpu.HBM)
DMA = pltpu.SemaphoreType.DMA


def nt_dot(a, b):
    return lax.dot_general(a, b, (((1,), (1,)), ((), ())), preferred_element_type=F32)


def dot(a, b):
    return jnp.dot(a, b, preferred_element_type=F32)


def exact_dot(rows, zero_one):
    high = rows.astype(BF16).astype(F32)
    rest = rows - high
    mid = rest.astype(BF16).astype(F32)
    low = rest - mid
    parts = jnp.concatenate([high, mid, low, jnp.zeros_like(low)], axis=0).astype(BF16)
    out = dot(parts, zero_one)
    return out[0:8] + out[8:16] + out[16:24]


def iota(shape, dim):
    return lax.broadcasted_iota(jnp.int32, shape, dim)


def one_hot(cond):
    return jnp.where(cond, 1.0, 0.0).astype(BF16)


def rows8(first, second=None):
    n = first.shape[1]
    row = iota((8, n), 0)
    out = jnp.where(row == 0, jnp.broadcast_to(first, (8, n)), 0.0)
    if second is not None:
        out = jnp.where(row == 1, jnp.broadcast_to(second, (8, n)), out)
    return out


def write_stats(mean_c, square_c, count, stats_ref):
    same = one_hot((iota((C, C), 0) >> 3) == (iota((C, C), 1) >> 3))
    mean_g = exact_dot(rows8(mean_c), same)[0:1] * (1.0 / 8)
    gap = mean_c - mean_g
    square_c = square_c + count * (gap * gap)
    lane = iota((C, 128), 1)
    pick = one_hot((iota((C, 128), 0) >> 3) == (lane & 31))
    both = exact_dot(rows8(mean_c * (1.0 / 8), square_c), pick)
    row = jnp.where(iota((1, 128), 1) < GROUPS, both[0:1], both[1:2])
    stats_ref[...] = jnp.broadcast_to(row[None], (SEQ, 1, 128))


def read_stats(stats_ref, count):
    each = stats_ref[...].reshape(SEQ, 128)
    lane = iota((1, 128), 1)
    mean = jnp.sum(each, axis=0, keepdims=True) * (1.0 / SEQ)
    off = each - mean
    between = jnp.sum(off * off, axis=0, keepdims=True) * (8.0 * count)
    within = mean * SEQ
    total = jnp.where(lane < GROUPS, between, jnp.where(lane < 2 * GROUPS, within, 0.0))
    mean = jnp.where(lane < GROUPS, mean, 0.0)
    spread = one_hot((iota((128, C), 0) & 31) == (iota((128, C), 1) >> 3))
    both = exact_dot(rows8(mean, total), spread)
    return both[0:1], lax.rsqrt(both[1:2] * (1.0 / (8.0 * count * SEQ)) + EPS)


def own_rows(place_ref, rows_ref, near_ref, far_ref):
    odd = place_ref[0] & 1
    near_ref[...] = rows_ref[pl.ds(pl.multiple_of((1 - odd) * ROW, ROW), ROW)].astype(BF16)
    far_ref[...] = rows_ref[pl.ds(pl.multiple_of(odd * ROW, ROW), ROW)].astype(BF16)


def split_kernel(
    place_ref, feat_hbm, gain_hbm, shift_hbm, scale_hbm, mod_hbm,
    rows_ref, near_ref, far_ref, stats_ref, norms_ref, mods_ref,
    feat_ref, gain_ref, shift_ref, scale_ref, mod_ref, wide, sems,
):
    sources = (feat_hbm, gain_hbm, shift_hbm, scale_hbm, mod_hbm)
    targets = (feat_ref, gain_ref, shift_ref, scale_ref, mod_ref)
    copies = [pltpu.make_async_copy(a, b, sems.at[i]) for i, (a, b) in enumerate(zip(sources, targets))]
    for copy in copies:
        copy.start()
    for copy in copies:
        copy.wait()
    norms_ref[0:3] = gain_ref[...]
    norms_ref[4:7] = shift_ref[...]
    mods_ref[0:1] = scale_ref[...]
    mods_ref[1:2] = mod_ref[...]
    cells = feat_ref[...].astype(F32).reshape(CELLS, C)
    for side in range(2):
        wide[side] = cells[:, side * 128 : (side + 1) * 128]
    for frame in range(FRAMES):
        for row in range(2):
            for parity in range(2):
                base = (frame * 2 + row) * 32 + parity
                at = row * ROW + (frame * 2 + parity) * HALF
                for side in range(2):
                    part = wide[side, pl.ds(base, HALF, stride=2)]
                    rows_ref[at : at + HALF, side * 128 : (side + 1) * 128] = part.astype(BF16)
    own_rows(place_ref, rows_ref, near_ref, far_ref)
    mean = jnp.sum(cells, axis=0, keepdims=True) * (1.0 / CELLS)
    off = cells - mean
    write_stats(mean, jnp.sum(off * off, axis=0, keepdims=True), CELLS, stats_ref)


def fill_window(place_ref, stats_ref, rows_ref, near_ref, far_ref, norms_ref, layer, window, centers=None, load=None):
    mean, rstd = read_stats(stats_ref, CELLS)
    gain = rstd * norms_ref[layer : layer + 1] * 0.5
    shift = norms_ref[4 + layer : 5 + layer] * 0.5
    place = place_ref[0]
    odd = place & 1
    near_at = 3 * (1 - odd)
    far_on = jnp.where((place > 0) & (place < SEQ - 1), 1.0, 0.0).astype(F32)
    window[:, 0:2] = jnp.zeros((4, 2, 4, HALF, C), BF16)
    step = 4
    n = step * HALF
    pair = iota((n, C), 0) & (HALF - 1)
    level = -mean
    levels = [level] * 4 if centers is None else [center + level for center in centers]
    sources = (
        (near_at, near_ref),
        (3 - near_at, far_ref),
        (1, rows_ref.at[0:ROW]),
        (2, rows_ref.at[ROW:CELLS]),
    )
    for which, (row, source) in enumerate(sources):
        if which == 2 and load is not None:
            load.wait()
        for frame in range(0, FRAMES, step):
            x = source[frame * 32 : (frame + step) * 32].astype(F32)
            half = (x + levels[which]) * gain + shift
            act = half + half * jnp.tanh(half)
            if which == 1:
                act = act * far_on
            act = act.reshape(step, 2, HALF, C)
            even = act[:, 0].reshape(n, C)
            odd_ones = act[:, 1].reshape(n, C)
            odd_before = jnp.where(pair == 0, 0.0, pltpu.roll(odd_ones, 1, 0))
            even_after = jnp.where(pair == HALF - 1, 0.0, pltpu.roll(even, n - 1, 0))
            for plane, part in enumerate((odd_before, even, odd_ones, even_after)):
                window[row, 2 + frame : 2 + frame + step, plane] = part.astype(BF16).reshape(
                    step, HALF, C
                )


TILE = 256


def start_weights(source, weight, sems):
    copies = [
        pltpu.make_async_copy(source.at[9 * p : 9 * p + 9], weight.at[9 * p : 9 * p + 9], sems.at[p])
        for p in range(3)
    ]
    for copy in copies:
        copy.start()
    return copies


def convolve(window, weight, copies, total, finish):
    for p in range(3):
        copies[p].wait()
        for tile in range(CELLS // TILE):
            row, frame = tile * TILE // ROW, tile * TILE % ROW // 32
            part = None
            for q in range(3):
                for r in range(3):
                    at = frame + p
                    cells = window[q + row, at : at + TILE // 32, r : r + 2].reshape(TILE, C)
                    term = dot(cells, weight[9 * p + 3 * q + r])
                    part = term if part is None else part + term
            rows = slice(tile * TILE, (tile + 1) * TILE)
            if p > 0:
                part = part + total[rows]
            if p < 2:
                total[rows] = part
            else:
                finish(rows, part)


class Moments:
    def __init__(self):
        self.center = self.first = self.second = None

    def add(self, tile):
        if self.center is None:
            self.center = jnp.sum(tile, axis=0, keepdims=True) * (1.0 / TILE)
        off = tile - self.center
        first = jnp.sum(off, axis=0, keepdims=True)
        second = jnp.sum(off * off, axis=0, keepdims=True)
        self.first = first if self.first is None else self.first + first
        self.second = second if self.second is None else self.second + second
        return off

    def write(self, stats_ref):
        gap = self.first * (1.0 / CELLS)
        square = jnp.maximum(self.second - self.first * gap, 0.0)
        write_stats(self.center + gap, square, CELLS, stats_ref)


def first_kernel(
    place_ref, stats_ref, rows_ref, near_ref, far_ref, norms_ref, weight_hbm,
    hidden_hbm, center_ref, near_out, far_out, stats_out, window, weight, total, hidden_ref, sems,
):
    copies = start_weights(weight_hbm, weight, sems)
    fill_window(place_ref, stats_ref, rows_ref, near_ref, far_ref, norms_ref, 0, window)
    moments = Moments()

    def finish(rows, tile):
        hidden_ref[rows] = moments.add(tile).astype(BF16)

    convolve(window, weight, copies, total, finish)
    copy = pltpu.make_async_copy(hidden_ref, hidden_hbm, sems.at[3])
    copy.start()
    center = moments.center
    center_ref[...] = jnp.broadcast_to(center, (8, C))
    high = center.astype(BF16).astype(F32)
    mid = (center - high).astype(BF16).astype(F32)
    line = iota((16, C), 0)
    terms = jnp.where(line == 0, high, jnp.where(line == 1, mid, jnp.where(line == 2, center - high - mid, 0.0)))
    own_rows(place_ref, hidden_ref, near_out.at[0:ROW], far_out.at[0:ROW])
    near_out[ROW : ROW + 16] = terms.astype(BF16)
    far_out[ROW : ROW + 16] = terms.astype(BF16)
    moments.write(stats_out)
    copy.wait()


def second_kernel(
    place_ref, stats_ref, hidden_hbm, center_ref, near_ref, far_ref, norms_ref, feat_ref, weight_hbm,
    block_ref, near_out, far_out, stats_out, window, weight, total, hidden_ref, sems,
):
    load = pltpu.make_async_copy(hidden_hbm, hidden_ref, sems.at[3])
    load.start()
    copies = start_weights(weight_hbm, weight, sems)
    own = center_ref[0:1]
    centers = [jnp.sum(ref[ROW : ROW + 16].astype(F32), axis=0, keepdims=True) for ref in (near_ref, far_ref)]
    centers += [own, own]
    fill_window(place_ref, stats_ref, hidden_ref, near_ref, far_ref, norms_ref, 1, window, centers, load)
    moments = Moments()

    def finish(rows, tile):
        block = (tile + feat_ref[rows].astype(F32)).astype(BF16)
        block_ref[rows] = block
        moments.add(block.astype(F32))

    convolve(window, weight, copies, total, finish)
    own_rows(place_ref, block_ref, near_out, far_out)
    moments.write(stats_out)


def column_to_row(column):
    square = jnp.broadcast_to(column, (128, 128))
    return jnp.sum(jnp.where(iota((128, 128), 0) == iota((128, 128), 1), square, 0.0), axis=0, keepdims=True)


def third_kernel(
    place_ref, stats_ref, rows_ref, near_ref, far_ref, norms_ref, weight_ref, embed_ref, bias_ref,
    own_ref, other_ref, patches_ref, parcel_ref, window, weight, folds,
):
    n = FRAMES * HALF
    for p in range(3):
        for row in range(4):
            for plane in range(4):
                block = (p * 4 + row) * 4 + plane
                for dh in range(2):
                    for dw in range(2):
                        at = (2 * dh + dw) * LAT
                        q, r = row - dh, plane - dw
                        if 0 <= q < 3 and 0 <= r < 3:
                            weight[block, at : at + LAT] = weight_ref[9 * p + 3 * q + r]
                        else:
                            weight[block, at : at + LAT] = jnp.zeros((LAT, C), BF16)
    fill_window(place_ref, stats_ref, rows_ref, near_ref, far_ref, norms_ref, 2, window)
    patches = None
    for p in range(3):
        for row in range(4):
            for plane in range(4):
                cells = window[row, p : p + FRAMES, plane].reshape(n, C)
                term = nt_dot(cells, weight[(p * 4 + row) * 4 + plane])
                patches = term if patches is None else patches + term
    patches_ref[...] = patches
    rounded = patches.astype(BF16)
    twice = jnp.concatenate([rounded, rounded], axis=1)
    spread = jnp.zeros((n, 128), F32)
    for at in range(0, D, C):
        embedded = dot(twice, embed_ref[:, at : at + C]) + bias_ref[0:1, at : at + C]
        embedded = embedded * embedded
        spread = spread + (embedded[:, 0:128] + embedded[:, 128:256])
    spread = jnp.sum(spread, axis=1, keepdims=True) * (1.0 / D)
    rstd = lax.rsqrt(spread + EPS)
    scaled = (rounded.astype(F32) * rstd).reshape(FRAMES, 2, 8, 64)
    rstd = jnp.broadcast_to(rstd, (n, 128)).reshape(FRAMES, 2, 8, 128)
    both = jnp.concatenate([scaled[:, side].reshape(128, 64) for side in range(2)], axis=1)
    parcel_ref[0:128] = both.astype(BF16)
    line = iota((16, 128), 0)
    lines = jnp.where(line == 4, 1.0, 0.0)
    for side in range(2):
        each = column_to_row(rstd[:, side].reshape(128, 128)[:, 0:1])
        high = each.astype(BF16).astype(F32)
        lines = jnp.where(line == 2 * side, high, lines)
        lines = jnp.where(line == 2 * side + 1, each - high, lines)
    parcel_ref[128:144] = lines.astype(BF16)
    own, other = own_ref[...].astype(F32), other_ref[...].astype(F32)
    lane = iota((4 * QROWS, 128), 1)
    parcel_ref[144:288] = jnp.where(lane < 64, own, pltpu.roll(other, 64, 1)).astype(BF16)
    folds[0 : 4 * QROWS] = own
    folds[4 * QROWS : 8 * QROWS] = other
    folds[8 * QROWS :] = jnp.zeros((8, 128), F32)
    lane = iota((40, 128), 1)
    ends = jnp.zeros((40, 128), F32)
    for i in range(8):
        ends = jnp.where((lane >> 3) == i, pltpu.roll(folds[i * QROWS : i * QROWS + 40], (8 * i + 64) % 128, 1), ends)
    parcel_ref[288:336] = jnp.concatenate([ends, jnp.zeros((8, 128), F32)], axis=0).astype(BF16)


def latent_kernel(patches_ref, latent_ref):
    n = FRAMES * HALF
    patches = patches_ref[...]
    turned = jnp.transpose(jnp.concatenate([patches, jnp.zeros_like(patches)], axis=1))
    out = None
    for dw in range(2):
        rows = jnp.concatenate([turned[(2 * dh + dw) * LAT : (2 * dh + dw + 1) * LAT] for dh in range(2)], axis=0)
        high = rows.astype(BF16).astype(F32)
        mid = (rows - high).astype(BF16).astype(F32)
        parts = jnp.concatenate([high, mid, rows - high - mid], axis=0).astype(BF16)
        column = iota((n, 2 * n), 1)
        spread = one_hot(column == iota((n, 2 * n), 0) * 2 + dw)
        term = dot(parts, spread)
        term = term[0:32] + term[32:64] + term[64:96]
        out = term if out is None else out + term
    for frame in range(FRAMES):
        for dh in range(2):
            latent_ref[frame, dh] = out[dh * LAT : (dh + 1) * LAT, frame * 32 : (frame + 1) * 32]


def fold_kernel(
    w0_ref, w1_ref, w2_ref, w3_ref, embed_ref, bias_ref, own_mods_ref, mods_ref,
    own_ref, other_ref, embed_out, bias_out, stacked, wide,
):
    embed = embed_ref[...].astype(F32)
    embed = embed - jnp.mean(embed, axis=1, keepdims=True)
    high = embed.astype(BF16)
    embed_out[0:64] = high
    embed_out[64:128] = (embed - high.astype(F32)).astype(BF16)
    center = bias_ref[...] - jnp.mean(bias_ref[...], axis=1, keepdims=True)
    bias_out[...] = jnp.broadcast_to(center, (8, D))
    for i in range(4):
        block = (w0_ref, w1_ref, w2_ref, w3_ref)[i][...].astype(F32)
        block = jnp.concatenate([block, jnp.zeros((QPAD - QROWS, D), F32)], axis=0)
        stacked[i * QPAD : (i + 1) * QPAD] = block.astype(BF16)
    row = iota((64, D), 0)
    sides = []
    for mod_ref in (own_mods_ref, mods_ref):
        scale, shift = 1.0 + mod_ref[0:1], mod_ref[1:2]
        bias = center * scale
        bias_high = bias.astype(BF16).astype(F32)
        shift_high = shift.astype(BF16).astype(F32)
        ends = jnp.where(row == 0, bias_high, jnp.where(row == 1, bias - bias_high, 0.0))
        ends = jnp.where(row == 2, shift_high, jnp.where(row == 3, shift - shift_high, ends))
        sides += [embed * scale, ends]
    every = jnp.concatenate(sides, axis=0).astype(BF16)
    out = nt_dot(stacked[...], every)
    lane = iota((4 * QPAD, 128), 1)
    for side, target in enumerate((own_ref, other_ref)):
        part = out[:, side * 128 : (side + 1) * 128]
        bias = part[:, 64:65] + part[:, 65:66]
        shift = part[:, 66:67] + part[:, 67:68]
        bias_high = bias.astype(BF16).astype(F32)
        shift_high = shift.astype(BF16).astype(F32)
        part = jnp.where((lane == 64) | (lane == 68), bias_high, part)
        part = jnp.where(lane == 65, bias - bias_high, part)
        part = jnp.where(lane == 66, shift_high, part)
        part = jnp.where(lane == 67, shift - shift_high, part)
        for i in range(4):
            wide[i * QROWS : (i + 1) * QROWS] = part[i * QPAD : i * QPAD + QROWS]
        target[...] = wide[...].astype(BF16)


WIDE = HEADS * HDIM


def sort_folds(place_ref, clip_ref, *refs):
    asks_ref, keys_ref, values_ref, loose, wide = refs[8:]
    seq, clip = place_ref[0], clip_ref[0]
    spot = iota((40, 128), 1)
    for j in range(SEQ):
        loose[j] = refs[4 * (j & 1) + ((j >> 1) & 3)][j >> 3, 144:336].astype(F32)
        for k in range(CLIPS):
            at = ((clip ^ (2 * (k & 3) + (k >> 2))) * SEQ + (seq ^ j)) * QROWS
            block = loose[j, (k & 3) * QROWS : (k & 3) * QROWS + 40]
            block = pltpu.roll(block, 64, 1) if k >> 2 else block
            ends = pltpu.roll(loose[j, 144:184], (64 - 8 * k) % 128, 1)
            block = jnp.where(spot < 64, block, jnp.where(spot < 69, ends, 0.0))
            wide[pl.ds(at, QROWS)] = block[:QROWS]
    lane = iota((WIDE, 128), 1)
    rows = wide[0:WIDE]
    asks_ref[:, 0:128] = rows.astype(BF16)
    asks_ref[:, 128:256] = pltpu.roll(rows, 64, 1).astype(BF16)
    for part, target in ((1, keys_ref), (2, values_ref)):
        rows = wide[part * WIDE : (part + 1) * WIDE]
        bias = rows[:, 64:65] + rows[:, 65:66]
        shift = rows[:, 66:67] + rows[:, 67:68]
        left = jnp.where(lane < 64, rows, 0.0)
        target[:, 0:128] = left.astype(BF16)
        target[:, 256:384] = pltpu.roll(left, 64, 1).astype(BF16)
        for side in range(2):
            extra = jnp.where((lane == 2 * side) | (lane == 2 * side + 1), bias, 0.0)
            extra = jnp.where(lane == 4, shift, extra)
            target[:, 256 * side + 128 : 256 * side + 256] = extra.astype(BF16)


def attend_kernel(place_ref, clip_ref, *refs):
    out_ref, asks_ref, keys_ref, values_ref, loose, wide, queries, mixed, scores, weights = refs[8:]
    sort_folds(place_ref, clip_ref, *refs[:8], asks_ref, keys_ref, values_ref, loose, wide)
    seq = place_ref[0]
    blocks = [refs[4 * (j & 1) + ((j >> 1) & 3)].at[j >> 3] for j in range(SEQ)]
    lane = iota((128, 128), 1)
    pick = one_hot(iota((8, 128), 1) == iota((8, 128), 0) + seq * 8)
    twin = pl.ds(pl.multiple_of((seq >> 1) * 16, 16), 16)
    tokens, scales = [], []
    for block in blocks:
        pair = block[twin].astype(F32)
        tokens.append(jnp.where((seq & 1) == 1, pair[8:16], pair[0:8]))
        scales.append(nt_dot(pick, block[128:144]))
    tokens = jnp.concatenate(tokens, axis=0)
    scales = jnp.concatenate(scales, axis=0)
    asked = []
    for side in range(2):
        high, low = scales[:, 2 * side : 2 * side + 1], scales[:, 2 * side + 1 : 2 * side + 2]
        spot = lane - 64 * (1 - side)
        own = jnp.where((lane >> 6) == side, tokens, 0.0)
        own = jnp.where((spot == 0) | (spot == 1), high, own)
        own = jnp.where((spot == 2) | (spot == 3), 1.0, own)
        own = jnp.where(spot == 4, low, own).astype(BF16)
        asked.append((nt_dot(own, asks_ref[:, 128 * side : 128 * side + 128]) * (1.0 / math.sqrt(HDIM))).astype(BF16))
    for head in range(HEADS):
        cols = slice(head * HDIM, (head + 1) * HDIM)
        keyed = [
            dot(asked[side][:, cols], keys_ref[cols, 256 * side : 256 * side + 256]).reshape(SEQ, 8, 256)
            for side in range(2)
        ]
        queries[:, head] = jnp.concatenate(keyed, axis=1).astype(BF16)
    n = HEADS * HALF
    same = jnp.where(iota((8, n), 0) == (iota((8, n), 1) & 7), 1.0, 0.0)
    for j, block in enumerate(blocks):
        query = queries[j].reshape(n, 256)
        ends = lax.dot_general(block[128:144], query[:, 128:144], (((0,), (1,)), ((), ())), preferred_element_type=F32)
        scores[j] = nt_dot(block[0:128], query[:, 0:128]) + ends
    for j in range(SEQ):
        each = scores[j].reshape(FRAMES, 8, n)
        raised = jnp.exp(each - jnp.max(each, axis=0, keepdims=True))
        shares = raised * (same / jnp.sum(raised, axis=0))
        weights[j] = jnp.transpose(shares.astype(BF16).reshape(128, n))
    for j, block in enumerate(blocks):
        mix = dot(weights[j], block[0:128]).reshape(HEADS, 2, 8, 128)
        ends = nt_dot(weights[j], block[128:144]).reshape(HEADS, 2, 8, 16)
        for side in range(2):
            mixed[side, :, j * 8 : (j + 1) * 8, 0:128] = mix[:, side]
            mixed[side, :, j * 8 : (j + 1) * 8, 128:144] = ends[:, side]
    for head in range(HEADS):
        cols = slice(head * HDIM, (head + 1) * HDIM)
        out = []
        for side in range(2):
            part = nt_dot(mixed[side, head, :, 0:128].astype(BF16), values_ref[cols, 256 * side : 256 * side + 128])
            at = 256 * side + 128
            part = part + nt_dot(mixed[side, head, :, 128:144].astype(BF16), values_ref[cols, at : at + 16])
            out.append(part.reshape(SEQ, 8, HDIM))
        out = jnp.concatenate(out, axis=1).astype(BF16)
        for j in range(SEQ):
            out_ref[pl.ds(pl.multiple_of((seq ^ j) * HALF, HALF), HALF), cols] = out[j]


def shape(*dims, dtype=BF16):
    return jax.ShapeDtypeStruct(dims, dtype)


def call(body, outs, ins, scratch=(), flops=0, moved=0, limit=32, first_out=VMEM):
    outs = list(outs) if isinstance(outs, list) else outs
    if first_out is HBM:
        outs[0] = pltpu.HBM(outs[0].shape, outs[0].dtype)
    kernel = pl.pallas_call(
        body,
        out_shape=outs,
        in_specs=ins,
        out_specs=[first_out] + [VMEM] * (len(outs) - 1) if isinstance(outs, list) else VMEM,
        scratch_shapes=list(scratch),
        compiler_params=pltpu.CompilerParams(vmem_limit_bytes=limit << 20),
        cost_estimate=pl.CostEstimate(flops=flops, bytes_accessed=moved, transcendentals=0),
        name=body.__name__,
    )

    def run(*args):
        return kernel(
            *(pltpu.with_memory_space_constraint(x, pltpu.HBM) if spec is HBM else x for x, spec in zip(args, ins))
        )

    return run


def swap(values, axis, bits, count):
    return lax.ppermute(values, axis, [(i, i ^ bits) for i in range(count)])


CHIP_PAIRS = [(i, i ^ 1) for i in range(SEQ)]
NEXT_PAIRS = [(i, (i + 1 if i & 1 else i - 1) % SEQ) for i in range(SEQ)]


def neighbours(near, far):
    far = lax.ppermute(far, "seq", NEXT_PAIRS)
    return lax.ppermute(near, "seq", CHIP_PAIRS), far


def exchange(stats):
    return lax.all_to_all(stats, "seq", 0, 0, tiled=True)


def gather_seq(block, beside):
    over = swap(block, "seq", 8, SEQ)
    over, beside = lax.optimization_barrier((over, beside))
    pair = jnp.stack([block, over])
    near = [pair] + [swap(pair, "seq", bits, SEQ) for bits in (2, 4, 6)]
    return near + [swap(x, "seq", 1, SEQ) for x in near], beside


WINDOW = pltpu.VMEM((4, FRAMES + 2, 4, HALF, C), BF16)
WEIGHT = pltpu.VMEM((27, C, C), BF16)
CONV_FLOPS = 2 * CELLS * 27 * C * C


def shards(
    features,
    first_conv,
    second_conv,
    out_conv,
    norm_gains,
    norm_shifts,
    embed_weight,
    embed_bias,
    mod_shift,
    mod_scale,
    qkv_weight,
):
    place = lax.axis_index("seq").astype(jnp.int32).reshape(1)
    clip = lax.axis_index("clip").astype(jnp.int32).reshape(1)
    row = shape(ROW, C)
    stats = shape(SEQ, 1, 128, dtype=F32)
    taps = 27

    cells = shape(CELLS, C)
    long_row = shape(ROW + 16, C)
    rows_f, near, far, stats0, norms, own_mods = call(
        split_kernel,
        [cells, row, row, stats, shape(8, C, dtype=F32), shape(2, D, dtype=F32)],
        [SMEM] + [HBM] * 5,
        [
            pltpu.VMEM((FRAMES, 2, 32, C), BF16),
            pltpu.VMEM((3, C), F32),
            pltpu.VMEM((3, C), F32),
            pltpu.VMEM((1, D), F32),
            pltpu.VMEM((1, D), F32),
            pltpu.VMEM((2, CELLS, 128), F32),
            DMA((5,)),
        ],
        0,
        1 << 20,
    )(place, features.reshape(FRAMES, 2, 32, C), norm_gains, norm_shifts, mod_scale, mod_shift)
    near, far = neighbours(near, far)
    mods = swap(own_mods, "clip", 1, CLIPS)
    stats0 = exchange(stats0)
    stats0, mods = lax.optimization_barrier((stats0, mods))
    stats0, mine = lax.optimization_barrier((stats0, qkv_weight))
    rows = [qkv_weight] + [swap(mine, "clip", bits, CLIPS) for bits in (2, 4, 6)]
    hidden, center, near_h, far_h, stats1 = call(
        first_kernel,
        [cells, shape(8, C, dtype=F32), long_row, long_row, stats],
        [SMEM] + [VMEM] * 5 + [HBM],
        [WINDOW, WEIGHT, pltpu.VMEM((CELLS, C), F32), pltpu.VMEM((CELLS, C), BF16), DMA((4,))],
        CONV_FLOPS,
        5 << 20,
        first_out=HBM,
    )(place, stats0, rows_f, near, far, norms, first_conv.reshape(taps, C, C))
    near, far = neighbours(near_h, far_h)

    stats1 = exchange(stats1)
    stats1, *rows = lax.optimization_barrier((stats1, *rows))

    block, near_b, far_b, stats2 = call(
        second_kernel,
        [cells, row, row, stats],
        [SMEM, VMEM, HBM] + [VMEM] * 5 + [HBM],
        [WINDOW, WEIGHT, pltpu.VMEM((CELLS, C), F32), pltpu.VMEM((CELLS, C), BF16), DMA((4,))],
        CONV_FLOPS,
        6 << 20,
    )(place, stats1, hidden, center, near, far, norms, rows_f, second_conv.reshape(taps, C, C))
    near, far = neighbours(near_b, far_b)
    stats2, *rows = lax.optimization_barrier((stats2, *rows))
    folded = shape(4 * QROWS, 128)
    own, other, embed, bias = call(
        fold_kernel,
        [folded, folded, shape(128, D), shape(8, D, dtype=F32)],
        [VMEM] * 8,
        [pltpu.VMEM((4 * QPAD, D), BF16), pltpu.VMEM((4 * QROWS, 128), F32)],
    )(*rows, embed_weight, embed_bias.reshape(1, D), own_mods, mods)
    other = swap(other, "clip", 1, CLIPS)
    stats2 = exchange(stats2)
    patches, parcel = call(
        third_kernel,
        [shape(FRAMES * HALF, 4 * LAT, dtype=F32), shape(336, 128)],
        [SMEM] + [VMEM] * 10,
        [WINDOW, pltpu.VMEM((48, 4 * LAT, C), BF16), pltpu.VMEM((8 * QROWS + 8, 128), F32)],
        CONV_FLOPS // 2,
        4 << 20,
    )(
        place, stats2, block, near, far, norms,
        out_conv.transpose(0, 1, 2, 4, 3).reshape(taps, LAT, C), embed, bias, own, other,
    )
    latent = call(latent_kernel, shape(FRAMES, 2, LAT, 2 * HALF, dtype=F32), [VMEM])(patches)
    parcels, latent = gather_seq(parcel, latent)
    frame_heads = call(
        attend_kernel,
        shape(SEQ * HALF, WIDE),
        [SMEM] * 2 + [VMEM] * 8,
        [
            pltpu.VMEM((WIDE, 256), BF16),
            pltpu.VMEM((WIDE, 512), BF16),
            pltpu.VMEM((WIDE, 512), BF16),
            pltpu.VMEM((SEQ, 192, 128), F32),
            pltpu.VMEM((3 * WIDE, 128), F32),
            pltpu.VMEM((SEQ, HEADS, HALF, 256), BF16),
            pltpu.VMEM((2, HEADS, 128, 256), F32),
            pltpu.VMEM((SEQ, 128, HEADS * HALF), F32),
            pltpu.VMEM((SEQ, HEADS * HALF, 128), BF16),
        ],
    )(place, clip, *parcels)
    latent = latent.transpose(0, 1, 3, 2).reshape(1, FRAMES, 2, 2 * HALF, LAT)
    return (latent, frame_heads.reshape(1, 1, SEQ * HALF, WIDE))


def solution(mesh):
    placed = (
        P("clip", None, "seq", None, None),
        P(),
        P(),
        P(),
        P(),
        P(),
        P(),
        P(),
        P("clip", None),
        P("clip", None),
        P(("clip", "seq"), None),
    )
    return jax.shard_map(
        shards,
        mesh=mesh,
        in_specs=placed,
        out_specs=(P("clip", None, "seq", None, None), P("clip", "seq", None, None)),
        check_vma=False,
    )
```

```python
import functools
import math

import jax
import jax.numpy as jnp
from jax import lax
from jax.experimental import pallas as pl
from jax.experimental.pallas import tpu as pltpu
from jax.sharding import PartitionSpec as P

C = 256
GROUPS = 32
LAT = 16
D = 3072
HEADS = 12
HDIM = 128
FRAMES = 16
HALF = 16
ROW = FRAMES * 2 * HALF
CELLS = 2 * ROW
SEQ = 16
CLIPS = 8
QROWS = 36
QPAD = 48
EPS = 1e-06
F32 = jnp.float32
BF16 = jnp.bfloat16
VMEM = pl.BlockSpec(memory_space=pltpu.VMEM)
SMEM = pl.BlockSpec(memory_space=pltpu.SMEM)
HBM = pl.BlockSpec(memory_space=pltpu.HBM)
DMA = pltpu.SemaphoreType.DMA


def nt_dot(a, b):
    return lax.dot_general(a, b, (((1,), (1,)), ((), ())), preferred_element_type=F32)


def dot(a, b):
    return jnp.dot(a, b, preferred_element_type=F32)


def exact_dot(rows, zero_one):
    high = rows.astype(BF16).astype(F32)
    rest = rows - high
    mid = rest.astype(BF16).astype(F32)
    low = rest - mid
    parts = jnp.concatenate([high, mid, low, jnp.zeros_like(low)], axis=0).astype(BF16)
    out = dot(parts, zero_one)
    return out[0:8] + out[8:16] + out[16:24]


def iota(shape, dim):
    return lax.broadcasted_iota(jnp.int32, shape, dim)


def one_hot(cond):
    return jnp.where(cond, 1.0, 0.0).astype(BF16)


def rows8(first, second=None):
    n = first.shape[1]
    row = iota((8, n), 0)
    out = jnp.where(row == 0, jnp.broadcast_to(first, (8, n)), 0.0)
    if second is not None:
        out = jnp.where(row == 1, jnp.broadcast_to(second, (8, n)), out)
    return out


def write_stats(mean_c, square_c, count, stats_ref):
    same = one_hot((iota((C, C), 0) >> 3) == (iota((C, C), 1) >> 3))
    mean_g = exact_dot(rows8(mean_c), same)[0:1] * (1.0 / 8)
    gap = mean_c - mean_g
    square_c = square_c + count * (gap * gap)
    lane = iota((C, 128), 1)
    pick = one_hot((iota((C, 128), 0) >> 3) == (lane & 31))
    both = exact_dot(rows8(mean_c * (1.0 / 8), square_c), pick)
    row = jnp.where(iota((1, 128), 1) < GROUPS, both[0:1], both[1:2])
    stats_ref[...] = jnp.broadcast_to(row[None], (SEQ, 1, 128))


def read_stats(stats_ref, count):
    each = stats_ref[...].reshape(SEQ, 128)
    lane = iota((1, 128), 1)
    mean = jnp.sum(each, axis=0, keepdims=True) * (1.0 / SEQ)
    off = each - mean
    between = jnp.sum(off * off, axis=0, keepdims=True) * (8.0 * count)
    within = mean * SEQ
    total = jnp.where(lane < GROUPS, between, jnp.where(lane < 2 * GROUPS, within, 0.0))
    mean = jnp.where(lane < GROUPS, mean, 0.0)
    spread = one_hot((iota((128, C), 0) & 31) == (iota((128, C), 1) >> 3))
    both = exact_dot(rows8(mean, total), spread)
    return both[0:1], lax.rsqrt(both[1:2] * (1.0 / (8.0 * count * SEQ)) + EPS)


def own_rows(place_ref, rows_ref, near_ref, far_ref):
    odd = place_ref[0] & 1
    near_ref[...] = rows_ref[pl.ds(pl.multiple_of((1 - odd) * ROW, ROW), ROW)].astype(BF16)
    far_ref[...] = rows_ref[pl.ds(pl.multiple_of(odd * ROW, ROW), ROW)].astype(BF16)


def split_kernel(
    place_ref, feat_hbm, gain_hbm, shift_hbm, scale_hbm, mod_hbm,
    rows_ref, near_ref, far_ref, stats_ref, norms_ref, mods_ref,
    feat_ref, gain_ref, shift_ref, scale_ref, mod_ref, wide, sems,
):
    sources = (feat_hbm, gain_hbm, shift_hbm, scale_hbm, mod_hbm)
    targets = (feat_ref, gain_ref, shift_ref, scale_ref, mod_ref)
    copies = [pltpu.make_async_copy(a, b, sems.at[i]) for i, (a, b) in enumerate(zip(sources, targets))]
    for copy in copies:
        copy.start()
    for copy in copies:
        copy.wait()
    norms_ref[0:3] = gain_ref[...]
    norms_ref[4:7] = shift_ref[...]
    mods_ref[0:1] = scale_ref[...]
    mods_ref[1:2] = mod_ref[...]
    cells = feat_ref[...].astype(F32).reshape(CELLS, C)
    for side in range(2):
        wide[side] = cells[:, side * 128 : (side + 1) * 128]
    for frame in range(FRAMES):
        for row in range(2):
            for parity in range(2):
                base = (frame * 2 + row) * 32 + parity
                at = row * ROW + (frame * 2 + parity) * HALF
                for side in range(2):
                    part = wide[side, pl.ds(base, HALF, stride=2)]
                    rows_ref[at : at + HALF, side * 128 : (side + 1) * 128] = part.astype(BF16)
    own_rows(place_ref, rows_ref, near_ref, far_ref)
    mean = jnp.sum(cells, axis=0, keepdims=True) * (1.0 / CELLS)
    off = cells - mean
    write_stats(mean, jnp.sum(off * off, axis=0, keepdims=True), CELLS, stats_ref)


def fill_window(place_ref, stats_ref, rows_ref, near_ref, far_ref, norms_ref, layer, window, centers=None, load=None):
    mean, rstd = read_stats(stats_ref, CELLS)
    gain = rstd * norms_ref[layer : layer + 1] * 0.5
    shift = norms_ref[4 + layer : 5 + layer] * 0.5
    place = place_ref[0]
    odd = place & 1
    near_at = 3 * (1 - odd)
    far_on = jnp.where((place > 0) & (place < SEQ - 1), 1.0, 0.0).astype(F32)
    window[:, 0:2] = jnp.zeros((4, 2, 4, HALF, C), BF16)
    step = 4
    n = step * HALF
    pair = iota((n, C), 0) & (HALF - 1)
    level = -mean
    levels = [level] * 4 if centers is None else [center + level for center in centers]
    sources = (
        (near_at, near_ref),
        (3 - near_at, far_ref),
        (1, rows_ref.at[0:ROW]),
        (2, rows_ref.at[ROW:CELLS]),
    )
    for which, (row, source) in enumerate(sources):
        if which == 2 and load is not None:
            load.wait()
        for frame in range(0, FRAMES, step):
            x = source[frame * 32 : (frame + step) * 32].astype(F32)
            half = (x + levels[which]) * gain + shift
            act = half + half * jnp.tanh(half)
            if which == 1:
                act = act * far_on
            act = act.reshape(step, 2, HALF, C)
            even = act[:, 0].reshape(n, C)
            odd_ones = act[:, 1].reshape(n, C)
            odd_before = jnp.where(pair == 0, 0.0, pltpu.roll(odd_ones, 1, 0))
            even_after = jnp.where(pair == HALF - 1, 0.0, pltpu.roll(even, n - 1, 0))
            for plane, part in enumerate((odd_before, even, odd_ones, even_after)):
                window[row, 2 + frame : 2 + frame + step, plane] = part.astype(BF16).reshape(
                    step, HALF, C
                )


TILE = 256


def start_weights(source, weight, sems):
    copies = [
        pltpu.make_async_copy(source.at[9 * p : 9 * p + 9], weight.at[9 * p : 9 * p + 9], sems.at[p])
        for p in range(3)
    ]
    for copy in copies:
        copy.start()
    return copies


def convolve(window, weight, copies, total, finish):
    for p in range(3):
        copies[p].wait()
        for tile in range(CELLS // TILE):
            row, frame = tile * TILE // ROW, tile * TILE % ROW // 32
            part = None
            for q in range(3):
                for r in range(3):
                    at = frame + p
                    cells = window[q + row, at : at + TILE // 32, r : r + 2].reshape(TILE, C)
                    term = dot(cells, weight[9 * p + 3 * q + r])
                    part = term if part is None else part + term
            rows = slice(tile * TILE, (tile + 1) * TILE)
            if p > 0:
                part = part + total[rows]
            if p < 2:
                total[rows] = part
            else:
                finish(rows, part)


class Moments:
    def __init__(self):
        self.center = self.first = self.second = None

    def add(self, tile):
        if self.center is None:
            self.center = jnp.sum(tile, axis=0, keepdims=True) * (1.0 / TILE)
        off = tile - self.center
        first = jnp.sum(off, axis=0, keepdims=True)
        second = jnp.sum(off * off, axis=0, keepdims=True)
        self.first = first if self.first is None else self.first + first
        self.second = second if self.second is None else self.second + second
        return off

    def write(self, stats_ref):
        gap = self.first * (1.0 / CELLS)
        square = jnp.maximum(self.second - self.first * gap, 0.0)
        write_stats(self.center + gap, square, CELLS, stats_ref)


def first_kernel(
    place_ref, stats_ref, rows_ref, near_ref, far_ref, norms_ref, weight_hbm,
    hidden_hbm, center_ref, near_out, far_out, stats_out, window, weight, total, hidden_ref, sems,
):
    copies = start_weights(weight_hbm, weight, sems)
    fill_window(place_ref, stats_ref, rows_ref, near_ref, far_ref, norms_ref, 0, window)
    moments = Moments()

    def finish(rows, tile):
        hidden_ref[rows] = moments.add(tile).astype(BF16)

    convolve(window, weight, copies, total, finish)
    copy = pltpu.make_async_copy(hidden_ref, hidden_hbm, sems.at[3])
    copy.start()
    center = moments.center
    center_ref[...] = jnp.broadcast_to(center, (8, C))
    high = center.astype(BF16).astype(F32)
    mid = (center - high).astype(BF16).astype(F32)
    line = iota((16, C), 0)
    terms = jnp.where(line == 0, high, jnp.where(line == 1, mid, jnp.where(line == 2, center - high - mid, 0.0)))
    own_rows(place_ref, hidden_ref, near_out.at[0:ROW], far_out.at[0:ROW])
    near_out[ROW : ROW + 16] = terms.astype(BF16)
    far_out[ROW : ROW + 16] = terms.astype(BF16)
    moments.write(stats_out)
    copy.wait()


def second_kernel(
    place_ref, stats_ref, hidden_hbm, center_ref, near_ref, far_ref, norms_ref, feat_ref, weight_hbm,
    w0_ref, w1_ref, w2_ref, w3_ref, embed_ref, bias_ref, own_mods_ref, mods_ref,
    block_ref, near_out, far_out, stats_out, own_out, other_out, embed_out, bias_out,
    window, weight, total, hidden_ref, sems, stacked, wide,
):
    load = pltpu.make_async_copy(hidden_hbm, hidden_ref, sems.at[3])
    load.start()
    copies = start_weights(weight_hbm, weight, sems)
    fold_kernel(
        w0_ref, w1_ref, w2_ref, w3_ref, embed_ref, bias_ref, own_mods_ref, mods_ref,
        own_out, other_out, embed_out, bias_out, stacked, wide,
    )
    own = center_ref[0:1]
    centers = [jnp.sum(ref[ROW : ROW + 16].astype(F32), axis=0, keepdims=True) for ref in (near_ref, far_ref)]
    centers += [own, own]
    fill_window(place_ref, stats_ref, hidden_ref, near_ref, far_ref, norms_ref, 1, window, centers, load)
    moments = Moments()

    def finish(rows, tile):
        block = (tile + feat_ref[rows].astype(F32)).astype(BF16)
        block_ref[rows] = block
        moments.add(block.astype(F32))

    convolve(window, weight, copies, total, finish)
    own_rows(place_ref, block_ref, near_out, far_out)
    moments.write(stats_out)


def column_to_row(column):
    square = jnp.broadcast_to(column, (128, 128))
    return jnp.sum(jnp.where(iota((128, 128), 0) == iota((128, 128), 1), square, 0.0), axis=0, keepdims=True)


def third_kernel(
    place_ref, stats_ref, rows_ref, near_ref, far_ref, norms_ref, weight_ref, embed_ref, bias_ref,
    own_ref, other_ref, patches_ref, parcel_ref, window, weight, folds,
):
    n = FRAMES * HALF
    for p in range(3):
        for row in range(4):
            for plane in range(4):
                block = (p * 4 + row) * 4 + plane
                for dh in range(2):
                    for dw in range(2):
                        at = (2 * dh + dw) * LAT
                        q, r = row - dh, plane - dw
                        if 0 <= q < 3 and 0 <= r < 3:
                            weight[block, at : at + LAT] = weight_ref[9 * p + 3 * q + r]
                        else:
                            weight[block, at : at + LAT] = jnp.zeros((LAT, C), BF16)
    fill_window(place_ref, stats_ref, rows_ref, near_ref, far_ref, norms_ref, 2, window)
    patches = None
    for p in range(3):
        for row in range(4):
            for plane in range(4):
                cells = window[row, p : p + FRAMES, plane].reshape(n, C)
                term = nt_dot(cells, weight[(p * 4 + row) * 4 + plane])
                patches = term if patches is None else patches + term
    patches_ref[...] = patches
    rounded = patches.astype(BF16)
    twice = jnp.concatenate([rounded, rounded], axis=1)
    spread = jnp.zeros((n, 128), F32)
    for at in range(0, D, C):
        embedded = dot(twice, embed_ref[:, at : at + C]) + bias_ref[0:1, at : at + C]
        embedded = embedded * embedded
        spread = spread + (embedded[:, 0:128] + embedded[:, 128:256])
    spread = jnp.sum(spread, axis=1, keepdims=True) * (1.0 / D)
    rstd = lax.rsqrt(spread + EPS)
    scaled = (rounded.astype(F32) * rstd).reshape(FRAMES, 2, 8, 64)
    rstd = jnp.broadcast_to(rstd, (n, 128)).reshape(FRAMES, 2, 8, 128)
    both = jnp.concatenate([scaled[:, side].reshape(128, 64) for side in range(2)], axis=1)
    parcel_ref[0:128] = both.astype(BF16)
    line = iota((16, 128), 0)
    lines = jnp.where(line == 4, 1.0, 0.0)
    for side in range(2):
        each = column_to_row(rstd[:, side].reshape(128, 128)[:, 0:1])
        high = each.astype(BF16).astype(F32)
        lines = jnp.where(line == 2 * side, high, lines)
        lines = jnp.where(line == 2 * side + 1, each - high, lines)
    parcel_ref[128:144] = lines.astype(BF16)
    own, other = own_ref[...].astype(F32), other_ref[...].astype(F32)
    lane = iota((4 * QROWS, 128), 1)
    parcel_ref[144:288] = jnp.where(lane < 64, own, pltpu.roll(other, 64, 1)).astype(BF16)
    folds[0 : 4 * QROWS] = own
    folds[4 * QROWS : 8 * QROWS] = other
    folds[8 * QROWS :] = jnp.zeros((8, 128), F32)
    lane = iota((40, 128), 1)
    ends = jnp.zeros((40, 128), F32)
    for i in range(8):
        ends = jnp.where((lane >> 3) == i, pltpu.roll(folds[i * QROWS : i * QROWS + 40], (8 * i + 64) % 128, 1), ends)
    parcel_ref[288:336] = jnp.concatenate([ends, jnp.zeros((8, 128), F32)], axis=0).astype(BF16)


def latent_kernel(patches_ref, latent_ref):
    n = FRAMES * HALF
    patches = patches_ref[...]
    turned = jnp.transpose(jnp.concatenate([patches, jnp.zeros_like(patches)], axis=1))
    out = None
    for dw in range(2):
        rows = jnp.concatenate([turned[(2 * dh + dw) * LAT : (2 * dh + dw + 1) * LAT] for dh in range(2)], axis=0)
        high = rows.astype(BF16).astype(F32)
        mid = (rows - high).astype(BF16).astype(F32)
        parts = jnp.concatenate([high, mid, rows - high - mid], axis=0).astype(BF16)
        column = iota((n, 2 * n), 1)
        spread = one_hot(column == iota((n, 2 * n), 0) * 2 + dw)
        term = dot(parts, spread)
        term = term[0:32] + term[32:64] + term[64:96]
        out = term if out is None else out + term
    for frame in range(FRAMES):
        for dh in range(2):
            latent_ref[frame, dh] = out[dh * LAT : (dh + 1) * LAT, frame * 32 : (frame + 1) * 32]


def fold_kernel(
    w0_ref, w1_ref, w2_ref, w3_ref, embed_ref, bias_ref, own_mods_ref, mods_ref,
    own_ref, other_ref, embed_out, bias_out, stacked, wide,
):
    embed = embed_ref[...].astype(F32)
    embed = embed - jnp.mean(embed, axis=1, keepdims=True)
    high = embed.astype(BF16)
    embed_out[0:64] = high
    embed_out[64:128] = (embed - high.astype(F32)).astype(BF16)
    center = bias_ref[...] - jnp.mean(bias_ref[...], axis=1, keepdims=True)
    bias_out[...] = jnp.broadcast_to(center, (8, D))
    for i in range(4):
        block = (w0_ref, w1_ref, w2_ref, w3_ref)[i][...].astype(F32)
        block = jnp.concatenate([block, jnp.zeros((QPAD - QROWS, D), F32)], axis=0)
        stacked[i * QPAD : (i + 1) * QPAD] = block.astype(BF16)
    row = iota((64, D), 0)
    sides = []
    for mod_ref in (own_mods_ref, mods_ref):
        scale, shift = 1.0 + mod_ref[0:1], mod_ref[1:2]
        bias = center * scale
        bias_high = bias.astype(BF16).astype(F32)
        shift_high = shift.astype(BF16).astype(F32)
        ends = jnp.where(row == 0, bias_high, jnp.where(row == 1, bias - bias_high, 0.0))
        ends = jnp.where(row == 2, shift_high, jnp.where(row == 3, shift - shift_high, ends))
        sides += [embed * scale, ends]
    every = jnp.concatenate(sides, axis=0).astype(BF16)
    out = nt_dot(stacked[...], every)
    lane = iota((4 * QPAD, 128), 1)
    for side, target in enumerate((own_ref, other_ref)):
        part = out[:, side * 128 : (side + 1) * 128]
        bias = part[:, 64:65] + part[:, 65:66]
        shift = part[:, 66:67] + part[:, 67:68]
        bias_high = bias.astype(BF16).astype(F32)
        shift_high = shift.astype(BF16).astype(F32)
        part = jnp.where((lane == 64) | (lane == 68), bias_high, part)
        part = jnp.where(lane == 65, bias - bias_high, part)
        part = jnp.where(lane == 66, shift_high, part)
        part = jnp.where(lane == 67, shift - shift_high, part)
        for i in range(4):
            wide[i * QROWS : (i + 1) * QROWS] = part[i * QPAD : i * QPAD + QROWS]
        target[...] = wide[...].astype(BF16)


WIDE = HEADS * HDIM


def sort_folds(place_ref, clip_ref, *refs):
    asks_ref, keys_ref, values_ref, loose, wide = refs[8:]
    seq, clip = place_ref[0], clip_ref[0]
    spot = iota((40, 128), 1)
    for j in range(SEQ):
        loose[j] = refs[4 * (j & 1) + ((j >> 1) & 3)][j >> 3, 144:336].astype(F32)
        for k in range(CLIPS):
            at = ((clip ^ (2 * (k & 3) + (k >> 2))) * SEQ + (seq ^ j)) * QROWS
            block = loose[j, (k & 3) * QROWS : (k & 3) * QROWS + 40]
            block = pltpu.roll(block, 64, 1) if k >> 2 else block
            ends = pltpu.roll(loose[j, 144:184], (64 - 8 * k) % 128, 1)
            block = jnp.where(spot < 64, block, jnp.where(spot < 69, ends, 0.0))
            wide[pl.ds(at, QROWS)] = block[:QROWS]
    lane = iota((WIDE, 128), 1)
    rows = wide[0:WIDE]
    asks_ref[:, 0:128] = rows.astype(BF16)
    asks_ref[:, 128:256] = pltpu.roll(rows, 64, 1).astype(BF16)
    for part, target in ((1, keys_ref), (2, values_ref)):
        rows = wide[part * WIDE : (part + 1) * WIDE]
        bias = rows[:, 64:65] + rows[:, 65:66]
        shift = rows[:, 66:67] + rows[:, 67:68]
        left = jnp.where(lane < 64, rows, 0.0)
        target[:, 0:128] = left.astype(BF16)
        target[:, 256:384] = pltpu.roll(left, 64, 1).astype(BF16)
        for side in range(2):
            extra = jnp.where((lane == 2 * side) | (lane == 2 * side + 1), bias, 0.0)
            extra = jnp.where(lane == 4, shift, extra)
            target[:, 256 * side + 128 : 256 * side + 256] = extra.astype(BF16)


def attend_kernel(place_ref, clip_ref, *refs):
    out_ref, asks_ref, keys_ref, values_ref, loose, wide, queries, mixed, scores, weights = refs[8:]
    sort_folds(place_ref, clip_ref, *refs[:8], asks_ref, keys_ref, values_ref, loose, wide)
    seq = place_ref[0]
    blocks = [refs[4 * (j & 1) + ((j >> 1) & 3)].at[j >> 3] for j in range(SEQ)]
    lane = iota((128, 128), 1)
    pick = one_hot(iota((8, 128), 1) == iota((8, 128), 0) + seq * 8)
    twin = pl.ds(pl.multiple_of((seq >> 1) * 16, 16), 16)
    tokens, scales = [], []
    for block in blocks:
        pair = block[twin].astype(F32)
        tokens.append(jnp.where((seq & 1) == 1, pair[8:16], pair[0:8]))
        scales.append(nt_dot(pick, block[128:144]))
    tokens = jnp.concatenate(tokens, axis=0)
    scales = jnp.concatenate(scales, axis=0)
    asked = []
    for side in range(2):
        high, low = scales[:, 2 * side : 2 * side + 1], scales[:, 2 * side + 1 : 2 * side + 2]
        spot = lane - 64 * (1 - side)
        own = jnp.where((lane >> 6) == side, tokens, 0.0)
        own = jnp.where((spot == 0) | (spot == 1), high, own)
        own = jnp.where((spot == 2) | (spot == 3), 1.0, own)
        own = jnp.where(spot == 4, low, own).astype(BF16)
        asked.append((nt_dot(own, asks_ref[:, 128 * side : 128 * side + 128]) * (1.0 / math.sqrt(HDIM))).astype(BF16))
    for head in range(HEADS):
        cols = slice(head * HDIM, (head + 1) * HDIM)
        keyed = [
            dot(asked[side][:, cols], keys_ref[cols, 256 * side : 256 * side + 256]).reshape(SEQ, 8, 256)
            for side in range(2)
        ]
        queries[:, head] = jnp.concatenate(keyed, axis=1).astype(BF16)
    n = HEADS * HALF
    same = jnp.where(iota((8, n), 0) == (iota((8, n), 1) & 7), 1.0, 0.0)
    for j, block in enumerate(blocks):
        query = queries[j].reshape(n, 256)
        ends = lax.dot_general(block[128:144], query[:, 128:144], (((0,), (1,)), ((), ())), preferred_element_type=F32)
        scores[j] = nt_dot(block[0:128], query[:, 0:128]) + ends
    for j in range(SEQ):
        each = scores[j].reshape(FRAMES, 8, n)
        raised = jnp.exp(each - jnp.max(each, axis=0, keepdims=True))
        shares = raised * (same / jnp.sum(raised, axis=0))
        weights[j] = jnp.transpose(shares.astype(BF16).reshape(128, n))
    for j, block in enumerate(blocks):
        mix = dot(weights[j], block[0:128]).reshape(HEADS, 2, 8, 128)
        ends = nt_dot(weights[j], block[128:144]).reshape(HEADS, 2, 8, 16)
        for side in range(2):
            mixed[side, :, j * 8 : (j + 1) * 8, 0:128] = mix[:, side]
            mixed[side, :, j * 8 : (j + 1) * 8, 128:144] = ends[:, side]
    for head in range(HEADS):
        cols = slice(head * HDIM, (head + 1) * HDIM)
        out = []
        for side in range(2):
            part = nt_dot(mixed[side, head, :, 0:128].astype(BF16), values_ref[cols, 256 * side : 256 * side + 128])
            at = 256 * side + 128
            part = part + nt_dot(mixed[side, head, :, 128:144].astype(BF16), values_ref[cols, at : at + 16])
            out.append(part.reshape(SEQ, 8, HDIM))
        out = jnp.concatenate(out, axis=1).astype(BF16)
        for j in range(SEQ):
            out_ref[pl.ds(pl.multiple_of((seq ^ j) * HALF, HALF), HALF), cols] = out[j]


def shape(*dims, dtype=BF16):
    return jax.ShapeDtypeStruct(dims, dtype)


def call(body, outs, ins, scratch=(), flops=0, moved=0, limit=32, first_out=VMEM):
    outs = list(outs) if isinstance(outs, list) else outs
    if first_out is HBM:
        outs[0] = pltpu.HBM(outs[0].shape, outs[0].dtype)
    kernel = pl.pallas_call(
        body,
        out_shape=outs,
        in_specs=ins,
        out_specs=[first_out] + [VMEM] * (len(outs) - 1) if isinstance(outs, list) else VMEM,
        scratch_shapes=list(scratch),
        compiler_params=pltpu.CompilerParams(vmem_limit_bytes=limit << 20),
        cost_estimate=pl.CostEstimate(flops=flops, bytes_accessed=moved, transcendentals=0),
        name=body.__name__,
    )

    def run(*args):
        return kernel(
            *(pltpu.with_memory_space_constraint(x, pltpu.HBM) if spec is HBM else x for x, spec in zip(args, ins))
        )

    return run


def swap(values, axis, bits, count):
    return lax.ppermute(values, axis, [(i, i ^ bits) for i in range(count)])


CHIP_PAIRS = [(i, i ^ 1) for i in range(SEQ)]
NEXT_PAIRS = [(i, (i + 1 if i & 1 else i - 1) % SEQ) for i in range(SEQ)]


def neighbours(near, far):
    far = lax.ppermute(far, "seq", NEXT_PAIRS)
    return lax.ppermute(near, "seq", CHIP_PAIRS), far


def exchange(stats):
    return lax.all_to_all(stats, "seq", 0, 0, tiled=True)


def gather_seq(block, beside):
    over = swap(block, "seq", 8, SEQ)
    over, beside = lax.optimization_barrier((over, beside))
    pair = jnp.stack([block, over])
    near = [pair] + [swap(pair, "seq", bits, SEQ) for bits in (2, 4, 6)]
    return near + [swap(x, "seq", 1, SEQ) for x in near], beside


WINDOW = pltpu.VMEM((4, FRAMES + 2, 4, HALF, C), BF16)
WEIGHT = pltpu.VMEM((27, C, C), BF16)
CONV_FLOPS = 2 * CELLS * 27 * C * C


def shards(
    features,
    first_conv,
    second_conv,
    out_conv,
    norm_gains,
    norm_shifts,
    embed_weight,
    embed_bias,
    mod_shift,
    mod_scale,
    qkv_weight,
):
    place = lax.axis_index("seq").astype(jnp.int32).reshape(1)
    clip = lax.axis_index("clip").astype(jnp.int32).reshape(1)
    row = shape(ROW, C)
    stats = shape(SEQ, 1, 128, dtype=F32)
    taps = 27

    cells = shape(CELLS, C)
    long_row = shape(ROW + 16, C)
    rows_f, near, far, stats0, norms, own_mods = call(
        split_kernel,
        [cells, row, row, stats, shape(8, C, dtype=F32), shape(2, D, dtype=F32)],
        [SMEM] + [HBM] * 5,
        [
            pltpu.VMEM((FRAMES, 2, 32, C), BF16),
            pltpu.VMEM((3, C), F32),
            pltpu.VMEM((3, C), F32),
            pltpu.VMEM((1, D), F32),
            pltpu.VMEM((1, D), F32),
            pltpu.VMEM((2, CELLS, 128), F32),
            DMA((5,)),
        ],
        0,
        1 << 20,
    )(place, features.reshape(FRAMES, 2, 32, C), norm_gains, norm_shifts, mod_scale, mod_shift)
    near, far = neighbours(near, far)
    mods = swap(own_mods, "clip", 1, CLIPS)
    stats0 = exchange(stats0)
    stats0, mods = lax.optimization_barrier((stats0, mods))
    stats0, mine = lax.optimization_barrier((stats0, qkv_weight))
    rows = [qkv_weight] + [swap(mine, "clip", bits, CLIPS) for bits in (2, 4, 6)]
    hidden, center, near_h, far_h, stats1 = call(
        first_kernel,
        [cells, shape(8, C, dtype=F32), long_row, long_row, stats],
        [SMEM] + [VMEM] * 5 + [HBM],
        [WINDOW, WEIGHT, pltpu.VMEM((CELLS, C), F32), pltpu.VMEM((CELLS, C), BF16), DMA((4,))],
        CONV_FLOPS,
        5 << 20,
        first_out=HBM,
    )(place, stats0, rows_f, near, far, norms, first_conv.reshape(taps, C, C))
    near, far = neighbours(near_h, far_h)

    stats1 = exchange(stats1)
    stats1, *rows = lax.optimization_barrier((stats1, *rows))

    folded = shape(4 * QROWS, 128)
    block, near_b, far_b, stats2, own, other, embed, bias = call(
        second_kernel,
        [cells, row, row, stats, folded, folded, shape(128, D), shape(8, D, dtype=F32)],
        [SMEM, VMEM, HBM] + [VMEM] * 5 + [HBM] + [VMEM] * 8,
        [WINDOW, WEIGHT, pltpu.VMEM((CELLS, C), F32), pltpu.VMEM((CELLS, C), BF16), DMA((4,)),
            pltpu.VMEM((4 * QPAD, D), BF16), pltpu.VMEM((4 * QROWS, 128), F32),
        ],
        CONV_FLOPS,
        6 << 20,
    )(place, stats1, hidden, center, near, far, norms, rows_f, second_conv.reshape(taps, C, C), *rows, embed_weight, embed_bias.reshape(1, D), own_mods, mods)
    near, far = neighbours(near_b, far_b)
    stats2, *rows = lax.optimization_barrier((stats2, *rows))
    other = swap(other, "clip", 1, CLIPS)
    stats2 = exchange(stats2)
    patches, parcel = call(
        third_kernel,
        [shape(FRAMES * HALF, 4 * LAT, dtype=F32), shape(336, 128)],
        [SMEM] + [VMEM] * 10,
        [WINDOW, pltpu.VMEM((48, 4 * LAT, C), BF16), pltpu.VMEM((8 * QROWS + 8, 128), F32)],
        CONV_FLOPS // 2,
        4 << 20,
    )(
        place, stats2, block, near, far, norms,
        out_conv.transpose(0, 1, 2, 4, 3).reshape(taps, LAT, C), embed, bias, own, other,
    )
    latent = call(latent_kernel, shape(FRAMES, 2, LAT, 2 * HALF, dtype=F32), [VMEM])(patches)
    parcels, latent = gather_seq(parcel, latent)
    frame_heads = call(
        attend_kernel,
        shape(SEQ * HALF, WIDE),
        [SMEM] * 2 + [VMEM] * 8,
        [
            pltpu.VMEM((WIDE, 256), BF16),
            pltpu.VMEM((WIDE, 512), BF16),
            pltpu.VMEM((WIDE, 512), BF16),
            pltpu.VMEM((SEQ, 192, 128), F32),
            pltpu.VMEM((3 * WIDE, 128), F32),
            pltpu.VMEM((SEQ, HEADS, HALF, 256), BF16),
            pltpu.VMEM((2, HEADS, 128, 256), F32),
            pltpu.VMEM((SEQ, 128, HEADS * HALF), F32),
            pltpu.VMEM((SEQ, HEADS * HALF, 128), BF16),
        ],
    )(place, clip, *parcels)
    latent = latent.transpose(0, 1, 3, 2).reshape(1, FRAMES, 2, 2 * HALF, LAT)
    return (latent, frame_heads.reshape(1, 1, SEQ * HALF, WIDE))


def solution(mesh):
    placed = (
        P("clip", None, "seq", None, None),
        P(),
        P(),
        P(),
        P(),
        P(),
        P(),
        P(),
        P("clip", None),
        P("clip", None),
        P(("clip", "seq"), None),
    )
    return jax.shard_map(
        shards,
        mesh=mesh,
        in_specs=placed,
        out_specs=(P("clip", None, "seq", None, None), P("clip", "seq", None, None)),
        check_vma=False,
    )
```
